32 devices in a mesh: ax: 8 (over z, x), sec: 4 (over y, core).
Axes of the slice: x: 2, y: 2, z: 4, core: 2. Of those that a mesh axis runs over, the one named last changes fastest.
Arguments:
- load: float32 [1024, 6, 1024], P('ax', None, 'sec'), may hold values from -6 to 6
- disp: float32 [1024, 6, 1024], P('ax', None, 'sec'), may hold values from -1.5 to 1.5
- stiff: float32 [1024, 6, 1024], P('ax', None, 'sec'), may hold values from 0.5 to 2
- hole: int32 [1024, 1024], P('ax', 'sec'), may hold values 0 or 1
- section_class: int32 [1024], P('ax'), may hold values from 0 to 3
- class_table: float32 [4, 6], replicated, may hold values from 0.5 to 2
- precond: float32 [6, 6, 1024], replicated, may hold values from -0.5 to 0.5, as said below
Outputs:
- disp_new: float32 [1024, 6, 1024], P('ax', None, 'sec')
- residual_new: float32 [1024, 6, 1024], P('ax', None, 'sec')
- stats: float32 [3], replicated
The draws below stay inside these ranges and needn't reach their ends.
Inputs may be any that keep to these rules, and one draw needn't show every extreme that they name: `precond`: for each harmonic the matrix over the first two dimensions is symmetric and positive definite.
All inputs are finite; a program needn't handle non-finite values. No bound on the sum of `hole` on one device may be relied on, other than what follows from the above.
Results may differ from the reference program's by a relative error of at most 0.0075.
Values sent between devices are 32-bit elements; how exact they have to be, the bound alone decides.
No kernel may reach another device: no remote copies, remote signals or barrier semaphores. Data moves between devices by JAX's collectives and lax.ppermute only.
A program may use at most 64 MiB of HBM per device.

```python
import math
import jax
import jax.numpy as jnp
from jax import lax

CH = 3
RAD = 2
NC = 1024
CLASSES = 4
CA = 128
NA = 1024
N_AX = 8


def draw_precond(key, part):
    key_diag = jax.random.fold_in(key, 11)
    key_mix = jax.random.fold_in(key, 23)
    harmonic = jnp.arange(NC).astype(jnp.float32)
    symbol = 5.5 + 4.0 * jnp.sin(math.pi * harmonic / NC) ** 2
    rough = jnp.exp(jax.random.uniform(key_diag, (CH * RAD, NC), jnp.float32, math.log(0.5), math.log(2.0)))
    diagonal = rough / symbol[None, :]
    mixing = jax.random.uniform(key_mix, (CH * RAD, CH * RAD, NC), jnp.float32, -1.0, 1.0)
    mixing = 0.5 * (mixing + jnp.transpose(mixing, (1, 0, 2)))
    bound_pair = jnp.minimum(diagonal[:, None, :], diagonal[None, :, :])
    identity = jnp.eye(CH * RAD, dtype=jnp.float32)[:, :, None]
    return (1.0 - identity) * 0.18 * bound_pair * mixing + identity * diagonal[:, None, :]


def with_ends(values, stream_key, smallest, top_value):
    shape = values.shape
    spot = [jax.random.randint(jax.random.fold_in(stream_key, axis), (), 0, shape[axis]) for axis in range(len(shape))]
    values = values.at[tuple(spot)].set(smallest)
    longest = shape.index(max(shape))
    spot[longest] = (spot[longest] + 1) % shape[longest]
    return values.at[tuple(spot)].set(top_value)


def shard_levels(rng, shape, split, smallest, high):
    def one(dim, shards_of):
        heights = jax.random.uniform(jax.random.fold_in(jax.random.fold_in(rng, 6), dim), (shards_of,), jnp.float32, smallest / len(split), high / len(split))
        return jnp.repeat(jnp.exp(heights), shape[dim] // shards_of).reshape((-1,) + (1,) * (len(shape) - dim - 1))

    level = one(*split[0])
    for cut in split[1:]:
        level = level * one(*cut)
    return level


def gaussian(stream_key, shape, scale, limit, cuts=(), kind=jnp.bfloat16):
    entries = jax.random.normal(stream_key, shape, jnp.float32) * scale
    if len(cuts) > 0:
        entries = shard_levels(stream_key, shape, cuts, -0.22, 0.18) * entries
    return jnp.clip(entries, min=-limit, max=limit).astype(kind)


def setup_inputs(seed: int = 0) -> dict:
    key_list = jax.random.split(jax.random.key(seed), 8)
    load = gaussian(key_list[0], (NA, CH * RAD, NC), 1.0, 6.0, ((0, 8), (2, 4)), jnp.float32)
    disp = gaussian(key_list[1], (NA, CH * RAD, NC), 0.25, 1.5, ((0, 8), (2, 4)), jnp.float32)
    stiff = jnp.clip(jnp.exp(math.log(2.0) - 1.3862944 * jax.random.uniform(key_list[2], (NA, CH * RAD, NC), jnp.float32) ** shard_levels(key_list[2], (NA, CH * RAD, NC), ((0, 8), (2, 4)), -0.2, 0.2)), 0.5, 2.0)
    hole = with_ends((jax.random.randint(key_list[3], (NA, NC), 0, 16) < 1).astype(jnp.int32), jax.random.fold_in(key_list[3], 1), 0, 1)
    section_class = with_ends(jax.random.randint(key_list[4], (NA,), 0, CLASSES), jax.random.fold_in(key_list[4], 1), 0, CLASSES - 1).astype(jnp.int32)
    class_table = jnp.clip(jnp.exp(jax.random.uniform(key_list[5], (CLASSES, CH * RAD), jnp.float32, math.log(0.5), math.log(2.0))), 0.5, 2.0)
    precond = draw_precond(jax.random.fold_in(key_list[7], 71), 0)
    return {"load": load, "disp": disp, "stiff": stiff, "hole": hole, "section_class": section_class, "class_table": class_table, "precond": precond}


def swap_radial(field):
    extent = field.shape
    folded = field.reshape(extent[0], extent[1] // 2, 2, extent[2])
    return jnp.flip(folded, axis=2).reshape(extent)


def operate(field, stiffness):
    padded = jnp.pad(field, ((1, 1), (0, 0), (0, 0)))
    beside = padded[2:] + padded[:-2]
    beside = beside + jnp.roll(field, 1, axis=2) + jnp.roll(field, -1, axis=2)
    return (stiffness + 4.5) * field - beside - 0.5 * swap_radial(field)


def reference(load, disp, stiff, hole, section_class, class_table, precond):
    position = jnp.arange(NA).astype(jnp.float32)
    taper = 1.0 + 2.0 * position / (NA - 1)
    stiffness = stiff * (class_table[section_class] * taper[:, None])[:, :, None]
    solid = (1 - hole).astype(jnp.float32)[:, None, :]
    residual = solid * (load - operate(disp, stiffness))

    def transform(block):
        spectrum = jnp.fft.fft(block, axis=2)
        cos_part = jnp.einsum("qpk,apk->aqk", precond, spectrum.real, precision=lax.Precision.HIGHEST)
        sin_part = jnp.einsum("qpk,apk->aqk", precond, -spectrum.imag, precision=lax.Precision.HIGHEST)
        return jnp.fft.ifft(lax.complex(cos_part, -sin_part), axis=2).real

    blocks = residual.reshape(N_AX, CA, CH * RAD, NC)
    smoothed = lax.map(transform, blocks).reshape(NA, CH * RAD, NC)
    prec = solid * smoothed
    image = solid * operate(prec, stiffness)
    cell_total = NA * CH * RAD * NC
    inner_rz = jnp.sum(residual * prec) / cell_total
    inner_zq = jnp.sum(prec * image) / cell_total
    alpha = inner_rz / inner_zq
    disp_new = disp + alpha * prec
    residual_new = residual - alpha * image
    square_new = jnp.sum(residual_new * residual_new) / cell_total
    return disp_new, residual_new, jnp.stack([inner_rz, inner_zq, square_new])
```

```python
import functools

import jax
import jax.numpy as jnp
import ml_dtypes
import numpy as np
from jax import lax
from jax.experimental import pallas as pl
from jax.experimental.pallas import tpu as pltpu
from jax.sharding import PartitionSpec as P

F32 = jnp.float32
BF16 = jnp.bfloat16
SECTORS = 4
TILE = 8
LANES = 128


def two_parts(table):
    high = table.astype(ml_dtypes.bfloat16)
    low = (table - high.astype(np.float64)).astype(ml_dtypes.bfloat16)
    return high, low


def three_terms(table):
    high, low = two_parts(table)
    return np.concatenate([high, high, low], axis=0)


@functools.lru_cache(maxsize=None)
def harmonic_tables(width):
    around = SECTORS * width
    half = width // 2
    zero = [("c", 4 * q) for q in range(half + 1)] + [("s", 4 * q) for q in range(1, half)]
    two = [(f, 4 * q + 2) for f in "cs" for q in range(half)]
    one = [(f, 4 * q + 1) for f in "cs" for q in range(width)]
    columns = zero + two + one
    harmonic = np.array([k for _, k in columns], dtype=np.int64)
    is_sin = np.array([f == "s" for f, _ in columns])

    def wave(place, k, shift):
        return np.cos(2.0 * np.pi / around * ((place[:, None] * k[None, :]) % around) - shift)

    place = np.arange(width)
    shift = np.where(is_sin, np.pi / 2, 0.0)[None, :]
    direct = wave(place, harmonic, shift)
    ones = slice(2 * width, 4 * width)
    quarter = wave(place, harmonic[ones], shift[:, ones] - np.pi / 2)
    forward_zero = three_terms(direct[:, :width])
    forward_two = three_terms(direct[:, width : 2 * width])
    forward_one = three_terms(np.concatenate([direct[:, ones], quarter], axis=0))
    targets = np.concatenate([place, np.full(LANES, width)])
    targets[-1] = around - 1
    inverse = wave(targets, harmonic, shift).T
    inverse[:, width + 1 : -1] = 0.0
    fold = np.zeros((around, around))
    fold[harmonic, np.arange(around)] += 1.0 / around
    mirror = (around - harmonic) % around
    apart = mirror != harmonic
    fold[mirror[apart], np.arange(around)[apart]] += 1.0 / around
    return (
        forward_zero,
        forward_two,
        forward_one,
        three_terms(inverse),
        fold.astype(ml_dtypes.bfloat16),
    )


def split(x):
    high = x.astype(BF16)
    return high, (x - high.astype(F32)).astype(BF16)


def lanes_of(shape):
    return lax.broadcasted_iota(jnp.int32, shape, len(shape) - 1)


def rows_of(shape):
    return lax.broadcasted_iota(jnp.int32, shape, len(shape) - 2)


def shifted(x, before, after):
    lane = lanes_of(x.shape)
    size = x.shape[-1]
    left = jnp.where(lane == 0, before, pltpu.roll(x, 1, x.ndim - 1))
    right = jnp.where(lane == size - 1, after, pltpu.roll(x, size - 1, x.ndim - 1))
    return left, right


def stacked(x, before, after):
    row = rows_of(x.shape)
    size = x.shape[-2]
    up = jnp.where(row == 0, before, pltpu.roll(x, 1, x.ndim - 2))
    down = jnp.where(row == size - 1, after, pltpu.roll(x, size - 1, x.ndim - 2))
    return up, down


def fold_kernel(precond_ref, fold_ref, out_ref):
    value = precond_ref[...]
    high = value.astype(BF16)
    rest = value - high.astype(F32)
    middle = rest.astype(BF16)
    low = (rest - middle.astype(F32)).astype(BF16)
    terms = [jnp.dot(t, fold_ref[...], preferred_element_type=F32) for t in (high, middle, low)]
    out_ref[...] = terms[0] + (terms[1] + terms[2])


def local_kernel(
    cuts, comps, position_ref, table_ref, class_ref, load_ref, disp_ref, stiff_ref, hole_ref,
    first_ref, second_ref, ends_ref, factor_ref, up_ref, down_ref,
):
    slab, width = hole_ref.shape
    a, b, c = cuts
    classes = class_ref[...]
    position = position_ref[0] + lanes_of(classes.shape)
    taper = 1.0 + 2.0 * position.astype(F32) / (position_ref[1] - 1).astype(F32)
    rows = []
    for q in range(comps):
        value = jnp.zeros(classes.shape, F32)
        for kind in range(table_ref.shape[0]):
            value = jnp.where(classes == kind, table_ref[kind, q], value)
        rows.append(value * taper)
    rows.append(jnp.zeros((LANES - comps, slab), F32))
    factor_ref[...] = jnp.concatenate(rows, axis=0).T
    solid = (1 - hole_ref[...]).astype(F32)
    edge_left, edge_right = [], []
    for q in range(comps):
        field = disp_ref[q]
        left, right = shifted(field, 0.0, 0.0)
        up, down = stacked(field, 0.0, 0.0)
        stiffness = stiff_ref[q] * factor_ref[:, q : q + 1]
        image = (stiffness + 4.5) * field - (up + down + left + right) - 0.5 * disp_ref[q ^ 1]
        part = solid * (load_ref[q] - image)
        first_ref[pl.ds(q * (b - a), b - a), :] = part[a:b]
        second_ref[pl.ds(q * (c - b), c - b), :] = part[b:c]
        ends_ref[pl.ds(q * (a + slab - c), a), :] = part[:a]
        ends_ref[pl.ds(q * (a + slab - c) + a, slab - c), :] = part[c:]
        for ref, row in ((up_ref, slab - 1), (down_ref, 0)):
            ref[q : q + 1, :] = part[row : row + 1]
            ref[TILE + q : TILE + q + 1, :] = field[row : row + 1]
        edge_left.append(field[:, 0:1])
        edge_right.append(field[:, width - 1 : width])
    for ref, row in ((up_ref, slab - 1), (down_ref, 0)):
        ref[comps : TILE, :] = jnp.broadcast_to(solid[row : row + 1], (TILE - comps, width))
        ref[TILE + comps :, :] = jnp.zeros((TILE - comps, width), F32)
    edge_left += [solid[:, 0:1]] * (TILE - comps)
    edge_right += [solid[:, width - 1 : width]] * (TILE - comps)
    edges = jnp.concatenate(edge_left + edge_right + [jnp.zeros((slab, LANES - 2 * TILE), F32)], axis=1).T
    first_ref[pl.ds(comps * (b - a), TILE), :] = jnp.concatenate(
        [edges[:TILE], edges[TILE : 2 * TILE]], axis=1
    )


def ends_kernel(comps, ends_ref, up_ref, down_ref, before_ref, after_ref, out_ref):
    rows = ends_ref.shape[0] // comps
    width = ends_ref.shape[1]
    row = rows_of((rows, width))
    spare = rows_of((TILE, width))
    solid_before = before_ref[comps : comps + 1]
    solid_after = after_ref[comps : comps + 1]
    for q in range(comps):
        disp_before = before_ref[TILE + q : TILE + q + 1]
        disp_after = after_ref[TILE + q : TILE + q + 1]
        part = ends_ref[pl.ds(q * rows, rows), :]
        part = part + jnp.where(row == 0, down_ref[comps : comps + 1] * disp_before, 0.0)
        part = part + jnp.where(row == rows - 1, up_ref[comps : comps + 1] * disp_after, 0.0)
        out_ref[pl.ds(q * (rows + TILE), rows), :] = part
        res_before = before_ref[q : q + 1] + solid_before * down_ref[TILE + q : TILE + q + 1]
        res_after = after_ref[q : q + 1] + solid_after * up_ref[TILE + q : TILE + q + 1]
        beyond = jnp.zeros((TILE, width), F32)
        for i, value in enumerate((res_before, res_after, disp_before, disp_after, solid_before, solid_after)):
            beyond = jnp.where(spare == i, value, beyond)
        out_ref[pl.ds(q * (rows + TILE) + rows, TILE), :] = beyond


def in_order(odd, own, core, across, both):
    return own, jnp.where(odd, both, core), across, jnp.where(odd, core, both)


def butterfly(x0, x1, x2, x3):
    even, other = x0 + x2, x1 + x3
    return even + other, even - other, x0 - x2, x1 - x3


def edge_table(odd, blocks):
    tiles = in_order(odd, *blocks)
    left = [t[:, :LANES] for t in tiles]
    right = [t[:, LANES:] for t in tiles]
    solid = TILE - 1
    at_left = [left[s][solid:] * right[s - 1] for s in range(SECTORS)]
    at_right = [right[s][solid:] * left[(s + 1) % SECTORS] for s in range(SECTORS)]
    stack = []
    for one, other in zip(butterfly(*at_left), butterfly(*at_right)):
        stack += [one, other]
    stack += [at_left[0], at_right[0], right[3], left[1]]
    stack.append(jnp.zeros((LANES - len(stack) * TILE, LANES), F32))
    return jnp.concatenate(stack, axis=0).T


def transform_kernel(
    comps, rows_at, spare, make_edge, odd_ref, own_ref, core_ref, across_ref, both_ref, *refs,
):
    refs = list(refs)
    edge_in = None if make_edge else refs.pop(0)
    zero_ref, two_ref, one_ref, inverse_ref, weight_ref, hole_ref = refs[:6]
    refs = refs[6:]
    edge_ref = refs.pop(0) if make_edge else edge_in
    prec_ref, residual_ref, left_ref, spectrum_ref, scaled_ref = refs
    width = own_ref.shape[1]
    odd = odd_ref[0] == 1
    sign = jnp.where(odd, -1.0, 1.0)
    main = sum(size for _, size in rows_at)
    rows = main + spare
    total = comps * rows
    sources = (own_ref, core_ref, across_ref, both_ref)
    if make_edge:
        edge_ref[...] = edge_table(odd, [r[total : total + TILE] for r in sources])
    solid = jnp.concatenate([(1 - hole_ref[pl.ds(at, size)]).astype(F32) for at, size in rows_at], axis=0)
    edge = jnp.concatenate([edge_ref[pl.ds(at, size)] for at, size in rows_at], axis=0)
    lane = lanes_of((main, LANES))
    first = lane == 0
    last = lane == LANES - 1

    def with_edges(x, array, q):
        column = array * 2 * TILE + q
        head = x[:, :LANES] + jnp.where(first, edge[:, column : column + 1], 0.0)
        tail = x[:, -LANES:] + jnp.where(last, edge[:, column + TILE : column + TILE + 1], 0.0)
        middle = [x[:, LANES:-LANES]] if width > 2 * LANES else []
        return jnp.concatenate([head] + middle + [tail], axis=1)

    masks = []
    for q in range(comps):
        at = q * rows
        own, core, across, both = [r[pl.ds(at, main), :] for r in sources]
        arrays = butterfly(own, core, across, both)
        arrays = arrays[:3] + (sign * arrays[3],)
        arrays = [with_edges(x, i, q) for i, x in enumerate(arrays)]
        residual_ref[q] = with_edges(own, 4, q)
        if spare:
            tiles = in_order(odd, *[r[pl.ds(at + main, spare), :] for r in sources])
            disp = [pltpu.roll(t, spare - 2, 0) for t in tiles]
            holes = [pltpu.roll(t, spare - 4, 0) for t in tiles]
            place = lanes_of((spare, width))
            fixed = []
            for s in range(SECTORS):
                beside = jnp.where(place == 0, pltpu.roll(disp[s - 1], 1, 1), 0.0)
                beside = beside + jnp.where(
                    place == width - 1, pltpu.roll(disp[(s + 1) % SECTORS], width - 1, 1), 0.0
                )
                value = tiles[s] + holes[s] * beside
                fixed.append(jnp.where(rows_of((spare, width)) < 2, value, 0.0))
            masks.append(holes[0])
            more = butterfly(*fixed)
            arrays = [jnp.concatenate(pair, axis=0) for pair in zip(arrays, more)]
        for i, x in enumerate(arrays):
            high, low = split(x)
            left_ref[pl.ds(at, rows), 2 * i * width : (2 * i + 1) * width] = high
            left_ref[pl.ds(at, rows), (2 * i + 1) * width : (2 * i + 2) * width] = low

    def column(i):
        return left_ref[:, i * width : (i + 1) * width]

    def product(parts, table):
        return jnp.dot(jnp.concatenate(parts, axis=1), table[...], preferred_element_type=F32)

    spectrum_ref[:, :width] = product([column(0), column(1), column(0)], zero_ref)
    spectrum_ref[:, width : 2 * width] = product([column(2), column(3), column(2)], two_ref)
    spectrum_ref[:, 2 * width :] = product(
        [column(4), column(6), column(5), column(7), column(4), column(6)], one_ref
    )

    around = SECTORS * width

    def scale(step, carry):
        at = pl.multiple_of(step * LANES, LANES)
        parts = [spectrum_ref[pl.ds(p * rows, rows), pl.ds(at, LANES)] for p in range(comps)]
        for q in range(comps):
            value = parts[0] * weight_ref[q * comps : q * comps + 1, pl.ds(at, LANES)]
            for p in range(1, comps):
                value = value + parts[p] * weight_ref[q * comps + p : q * comps + p + 1, pl.ds(at, LANES)]
            high, low = split(value)
            scaled_ref[pl.ds(q * rows, rows), pl.ds(at, LANES)] = high
            scaled_ref[pl.ds(q * rows, rows), pl.ds(pl.multiple_of(around + at, LANES), LANES)] = low
        return carry

    lax.fori_loop(0, around // LANES, scale, 0)
    high = scaled_ref[:, :around]
    result = product([high, scaled_ref[:, around:], high], inverse_ref)
    for q in range(comps):
        at = q * rows
        part = result[at : at + main]
        prec_ref[q, :main] = jnp.concatenate([part[:, :width] * solid, part[:, width:]], axis=1)
        if spare:
            more = result[at + main : at + rows, :width] * masks[q]
            prec_ref[q, main:] = jnp.concatenate([more, jnp.zeros((spare, LANES), F32)], axis=1)


def whole(refs, q, cuts, slab, columns):
    a, b, c = cuts
    first, second, ends = refs
    return jnp.concatenate(
        [ends[q, :a, columns], first[q, :, columns], second[q, :, columns], ends[q, a : a + slab - c, columns]],
        axis=0,
    )


def image_kernel(
    cuts, comps, stiff_ref, hole_ref, factor_ref, edge_ref,
    p0_ref, p1_ref, p2_ref, r0_ref, r1_ref, r2_ref, image_ref, sums_ref,
):
    slab, width = hole_ref.shape
    a, _, c = cuts
    spare = a + slab - c
    precs = (p0_ref, p1_ref, p2_ref)
    solid = (1 - hole_ref[...]).astype(F32)
    own = slice(0, width)
    solid_before = edge_ref[:, 11 * TILE - 1 : 11 * TILE]
    solid_after = edge_ref[:, 12 * TILE - 1 : 12 * TILE]
    fields = [whole(precs, q, cuts, slab, own) for q in range(comps)]
    sums = [jnp.zeros((TILE, width), F32) for _ in range(5)]
    for q in range(comps):
        field = fields[q]
        tile = whole(precs, q, cuts, slab, slice(width, width + LANES))
        left, right = shifted(field, tile[:, LANES - 1 :] * solid_before, tile[:, :1] * solid_after)
        up, down = stacked(field, p2_ref[q, spare : spare + 1, own], p2_ref[q, spare + 1 : spare + 2, own])
        stiffness = stiff_ref[q] * factor_ref[:, q : q + 1]
        image = (stiffness + 4.5) * field - (up + down + left + right) - 0.5 * fields[q ^ 1]
        image = solid * image
        image_ref[q] = image
        residual = whole((r0_ref, r1_ref, r2_ref), q, cuts, slab, own)
        pairs = ((residual, field), (field, image), (residual, residual), (residual, image), (image, image))
        for i, (x, y) in enumerate(pairs):
            sums[i] = sums[i] + jnp.sum((x * y).reshape(slab // TILE, TILE, width), axis=0)
    lane = lanes_of(sums_ref.shape)
    row = jnp.zeros(sums_ref.shape, F32)
    for i, value in enumerate(sums):
        row = jnp.where(lane == i, jnp.sum(value), row)
    sums_ref[...] = row


def update_kernel(
    cuts, comps, cell_total, disp_ref, image_ref, gathered_ref,
    p0_ref, p1_ref, p2_ref, r0_ref, r1_ref, r2_ref, disp_out, residual_out, stats_out,
):
    slab, width = disp_ref.shape[1:]
    lane = lanes_of(gathered_ref.shape)
    values = gathered_ref[...] * (1.0 / cell_total)
    rz, zq, rr, ri, ii = [jnp.sum(jnp.where(lane == i, values, 0.0)) for i in range(5)]
    spot = lanes_of((1, LANES))
    top = jnp.where(spot >= 0, rz, 0.0)
    alpha_row = top / jnp.where(spot >= 0, zq, 0.0)
    square = rr + alpha_row * (alpha_row * ii - 2.0 * ri)
    stats_out[...] = jnp.where(spot == 0, rz, jnp.where(spot == 1, zq, square))
    alpha = alpha_row[:, :1]
    own = slice(0, width)
    for q in range(comps):
        disp_out[q] = disp_ref[q] + alpha * whole((p0_ref, p1_ref, p2_ref), q, cuts, slab, own)
        residual_out[q] = whole((r0_ref, r1_ref, r2_ref), q, cuts, slab, own) - alpha * image_ref[q]


VMEM = pl.BlockSpec(memory_space=pltpu.VMEM)
SMEM = pl.BlockSpec(memory_space=pltpu.SMEM)


def call(kernel, name, out_shapes, in_specs, flops, moved, scratch=()):
    return pl.pallas_call(
        kernel,
        out_shape=[jax.ShapeDtypeStruct(s, F32) for s in out_shapes],
        in_specs=in_specs,
        out_specs=[VMEM] * len(out_shapes),
        scratch_shapes=list(scratch),
        compiler_params=pltpu.CompilerParams(vmem_limit_bytes=32 * 1024 * 1024),
        cost_estimate=pl.CostEstimate(flops=flops, bytes_accessed=moved, transcendentals=0),
        name=name,
    )


def shards(load, disp, stiff, hole, section_class, class_table, precond):
    slab, comps, width = disp.shape
    ax, sec = lax.axis_size("ax"), lax.axis_size("sec")
    around = width * sec
    cell_total = slab * ax * comps * around
    cuts = (slab // 8, slab // 2, slab - slab // 8)
    a, b, c = cuts
    ends = a + slab - c
    load, disp, stiff = [x.transpose(1, 0, 2) for x in (load, disp, stiff)]
    zero, two, one, inverse, fold = harmonic_tables(width)
    block = 4 * comps * slab * width
    odd = (lax.axis_index("sec") % 2).astype(jnp.int32).reshape(1)
    position = jnp.stack([lax.axis_index("ax") * slab, jnp.int32(ax * slab)]).astype(jnp.int32)

    first, second, edge_rows, factor, up, down = call(
        functools.partial(local_kernel, cuts, comps), "local",
        [(comps * (b - a) + TILE, width), (comps * (c - b), width), (comps * ends, width),
         (slab, LANES), (2 * TILE, width), (2 * TILE, width)],
        [SMEM, SMEM] + [VMEM] * 5, 20 * comps * slab * width, 4 * block,
    )(position, class_table, section_class.reshape(1, slab), load, disp, stiff, hole)

    def across(x):
        return lax.ppermute(x, "sec", [(i, (i + sec // 2) % sec) for i in range(sec)])

    def beside(x):
        return lax.ppermute(x, "sec", [(i, i ^ 1) for i in range(sec)])

    def gather(x):
        far = across(x)
        return x, beside(x), far, beside(far)

    first = gather(first)
    before = lax.ppermute(up, "ax", [(i, i + 1) for i in range(ax - 1)])
    after = lax.ppermute(down, "ax", [(i + 1, i) for i in range(ax - 1)])
    second = gather(second)
    (last,) = call(
        functools.partial(ends_kernel, comps), "ends",
        [(comps * (ends + TILE), width)], [VMEM] * 5, comps * ends * width, 8 * comps * ends * width,
    )(edge_rows, up, down, before, after)
    last = gather(last)
    (weight,) = call(
        fold_kernel, "fold", [(comps * comps, around)], [VMEM] * 2,
        6 * comps * comps * around * around, 2 * around * around,
    )(precond.reshape(comps * comps, around), fold)

    def transform(blocks, rows_at, spare, edge):
        main = sum(size for _, size in rows_at)
        rows = main + spare
        total = comps * rows
        out_shapes = [(comps, rows, width + LANES), (comps, main, width)]
        if edge is None:
            out_shapes = [(slab, LANES)] + out_shapes
        operands = list(blocks) + ([] if edge is None else [edge]) + [zero, two, one, inverse, weight, hole]
        return call(
            functools.partial(transform_kernel, comps, rows_at, spare, edge is None), "transform",
            out_shapes, [SMEM] + [VMEM] * len(operands),
            2 * total * 3 * around * (width + 2 * width), 4 * total * width * 8,
            [pltpu.VMEM((total, 8 * width), BF16), pltpu.VMEM((total, around), F32),
             pltpu.VMEM((total, 2 * around), BF16)],
        )(odd, *operands)

    edge, prec0, res0 = transform(first, ((a, b - a),), 0, None)
    prec1, res1 = transform(second, ((b, c - b),), 0, edge)
    prec2, res2 = transform(last, ((0, a), (c, slab - c)), TILE, edge)

    image, sums = call(
        functools.partial(image_kernel, cuts, comps), "image",
        [(comps, slab, width), (ax * sec, LANES)], [VMEM] * 10, 30 * comps * slab * width, 5 * block,
    )(stiff, hole, factor, edge, prec0, prec1, prec2, res0, res1, res2)
    gathered = lax.all_to_all(sums, ("ax", "sec"), 0, 0, tiled=True)
    disp_new, residual_new, stats = call(
        functools.partial(update_kernel, cuts, comps, cell_total), "update",
        [(comps, slab, width), (comps, slab, width), (1, LANES)], [VMEM] * 9,
        4 * comps * slab * width, 6 * block,
    )(disp, image, gathered, prec0, prec1, prec2, res0, res1, res2)
    return disp_new.transpose(1, 0, 2), residual_new.transpose(1, 0, 2), stats[0, :3]


def solution(mesh):
    in_specs = (
        P("ax", None, "sec"),
        P("ax", None, "sec"),
        P("ax", None, "sec"),
        P("ax", "sec"),
        P("ax"),
        P(),
        P(),
    )
    out_specs = (P("ax", None, "sec"), P("ax", None, "sec"), P())
    return jax.shard_map(shards, mesh=mesh, in_specs=in_specs, out_specs=out_specs, check_vma=False)
```

```python
import functools

import jax
import jax.numpy as jnp
import ml_dtypes
import numpy as np
from jax import lax
from jax.experimental import pallas as pl
from jax.experimental.pallas import tpu as pltpu
from jax.sharding import PartitionSpec as P

F32 = jnp.float32
BF16 = jnp.bfloat16
SECTORS = 4
TILE = 8
LANES = 128


def three_terms(table):
    high = table.astype(ml_dtypes.bfloat16)
    low = (table - high.astype(np.float64)).astype(ml_dtypes.bfloat16)
    return np.concatenate([high, high, low], axis=0)


@functools.lru_cache(maxsize=None)
def harmonic_tables(width):
    around = SECTORS * width
    half = width // 2
    zero = [("c", 4 * q) for q in range(half + 1)] + [("s", 4 * q) for q in range(1, half)]
    two = [(f, 4 * q + 2) for f in "cs" for q in range(half)]
    one = [(f, 8 * q + 1) for f in "cs" for q in range(half)]
    five = [(f, 8 * q + 5) for f in "cs" for q in range(half)]
    columns = zero + two + one + five
    harmonic = np.array([k for _, k in columns], dtype=np.int64)
    is_sin = np.array([f == "s" for f, _ in columns])

    def wave(place, shift):
        angle = 2.0 * np.pi / around * ((place[:, None] * harmonic[None, :]) % around)
        return np.cos(angle - shift)

    place = np.arange(width)
    shift = np.where(is_sin, np.pi / 2, 0.0)[None, :]
    direct = wave(place, shift)
    turned = np.concatenate([direct[:half], wave(place[:half], shift - np.pi / 2)], axis=0)
    forward = [direct[:, :width], direct[:, width : 2 * width]]
    forward += [turned[:, 2 * width : 3 * width], turned[:, 3 * width :]]
    beyond = np.zeros((TILE, around), np.float32)
    beyond[:2] = wave(np.array([around - 1, width]), shift)
    fold = np.zeros((around, around))
    fold[harmonic, np.arange(around)] += 1.0 / around
    mirror = (around - harmonic) % around
    apart = mirror != harmonic
    fold[mirror[apart], np.arange(around)[apart]] += 1.0 / around
    return (
        np.concatenate([three_terms(t) for t in forward], axis=0),
        three_terms(direct.T),
        beyond,
        fold.astype(ml_dtypes.bfloat16),
    )


def split(x):
    high = x.astype(BF16)
    return high, (x - high.astype(F32)).astype(BF16)


def lanes_of(shape):
    return lax.broadcasted_iota(jnp.int32, shape, len(shape) - 1)


def rows_of(shape):
    return lax.broadcasted_iota(jnp.int32, shape, len(shape) - 2)


def beside_sum(x, before, after):
    lane = lanes_of(x.shape)
    size = x.shape[-1]
    left = jnp.where(lane == 0, before, pltpu.roll(x, 1, x.ndim - 1))
    right = jnp.where(lane == size - 1, after, pltpu.roll(x, size - 1, x.ndim - 1))
    return left + right


def stacked_sum(x, before=0.0, after=0.0):
    row = rows_of(x.shape)
    size = x.shape[0]
    up = jnp.where(row == 0, before, pltpu.roll(x, 1, 0))
    down = jnp.where(row == size - 1, after, pltpu.roll(x, size - 1, 0))
    return up + down


def fold_kernel(precond_ref, fold_ref, out_ref):
    value = jnp.concatenate([precond_ref[q] for q in range(precond_ref.shape[0])], axis=0)
    high = value.astype(BF16)
    rest = value - high.astype(F32)
    middle = rest.astype(BF16)
    low = (rest - middle.astype(F32)).astype(BF16)
    terms = [jnp.dot(t, fold_ref[...], preferred_element_type=F32) for t in (high, middle, low)]
    out_ref[...] = terms[0] + (terms[1] + terms[2])


def factor_columns(table_ref, class_ref, ax_size, comps):
    classes = class_ref[...]
    slab = classes.shape[1]
    position = lax.axis_index("ax") * slab + lanes_of(classes.shape)
    taper = 1.0 + 2.0 * position.astype(F32) / F32(ax_size * slab - 1)
    rows = []
    for q in range(comps):
        value = jnp.zeros(classes.shape, F32)
        for kind in range(table_ref.shape[0]):
            value = jnp.where(classes == kind, table_ref[kind, q], value)
        rows.append(value * taper)
    rows.append(jnp.zeros((LANES - comps, slab), F32))
    return jnp.concatenate(rows, axis=0).T


def copies(pairs, sems):
    started = [pltpu.make_async_copy(src, dst, sems.at[i]) for i, (src, dst) in enumerate(pairs)]
    for copy in started:
        copy.start()
    return started


def local_part(q, low, high, slab, solid, factor, load, stiff, disp_ref):
    start, stop = max(low - TILE, 0), min(high + TILE, slab)
    inner = slice(low - start, high - start)
    block = disp_ref[q, start:stop]
    field = block[inner]
    beside = stacked_sum(block)[inner] + beside_sum(field, 0.0, 0.0)
    stiffness = stiff * factor[low:high, q : q + 1]
    image = (stiffness + 4.5) * field - beside - 0.5 * disp_ref[q ^ 1, low:high]
    return solid[low:high] * (load - image)


def first_kernel(
    cuts, comps, ax_size, table_ref, class_ref, load_ref, disp_ref, stiff_ref, hole_ref,
    first_ref, load_in, disp_in, stiff_in, hole_in, sems,
):
    slab, width = hole_ref.shape
    a, b, _ = cuts
    moving = copies(
        [(hole_ref, hole_in)]
        + [(disp_ref.at[q], disp_in.at[q]) for q in range(comps)]
        + [(load_ref.at[q, pl.ds(a, b - a)], load_in.at[q]) for q in range(comps)]
        + [(stiff_ref.at[q, pl.ds(a, b - a)], stiff_in.at[q]) for q in range(comps)],
        sems,
    )
    factor = factor_columns(table_ref, class_ref, ax_size, comps)
    for copy in moving[: 1 + comps]:
        copy.wait()
    solid = (1 - hole_in[...]).astype(F32)
    spare = TILE - comps
    edge_left = [disp_in[q, :, 0:1] for q in range(comps)] + [solid[:, 0:1]] * spare
    edge_right = [disp_in[q, :, width - 1 : width] for q in range(comps)]
    edge_right += [solid[:, width - 1 : width]] * spare
    rest = [jnp.zeros((slab, LANES - 2 * TILE), F32)]
    edges = jnp.concatenate(edge_left + edge_right + rest, axis=1).T
    first_ref[pl.ds(comps * (b - a), TILE), :] = jnp.concatenate(
        [edges[:TILE], edges[TILE : 2 * TILE]], axis=1
    )
    for q in range(comps):
        moving[1 + comps + q].wait()
        moving[1 + 2 * comps + q].wait()
        first_ref[pl.ds(q * (b - a), b - a), :] = local_part(
            q, a, b, slab, solid, factor, load_in[q], stiff_in[q], disp_in
        )


def second_kernel(
    cuts, comps, ax_size, table_ref, class_ref, load_ref, disp_ref, stiff_ref, hole_ref,
    second_ref, ends_ref, factor_ref, up_ref, down_ref, load_in, disp_in, stiff_in, hole_in, sems,
):
    slab, width = hole_ref.shape
    a, b, c = cuts
    pairs = [(hole_ref, hole_in)] + [(disp_ref.at[q], disp_in.at[q]) for q in range(comps)]
    for q in range(comps):
        for src, dst in ((load_ref, load_in), (stiff_ref, stiff_in)):
            pairs.append((src.at[q, pl.ds(0, a)], dst.at[q, pl.ds(0, a)]))
            pairs.append((src.at[q, pl.ds(b, slab - b)], dst.at[q, pl.ds(a, slab - b)]))
    moving = copies(pairs, sems)
    factor_ref[...] = factor_columns(table_ref, class_ref, ax_size, comps)
    for copy in moving[: 1 + comps]:
        copy.wait()
    factor = factor_ref[...]
    solid = (1 - hole_in[...]).astype(F32)
    ends = a + slab - c
    for q in range(comps):
        for copy in moving[1 + comps + 4 * q : 5 + comps + 4 * q]:
            copy.wait()
        part = local_part(
            q, b, slab, slab, solid, factor, load_in[q, a:], stiff_in[q, a:], disp_in
        )
        top = local_part(q, 0, a, slab, solid, factor, load_in[q, :a], stiff_in[q, :a], disp_in)
        second_ref[pl.ds(q * (c - b), c - b), :] = part[: c - b]
        ends_ref[pl.ds(q * ends, a), :] = top
        ends_ref[pl.ds(q * ends + a, slab - c), :] = part[c - b :]
        up_ref[q : q + 1, :] = part[slab - b - 1 :]
        down_ref[q : q + 1, :] = top[:1]
        up_ref[TILE + q : TILE + q + 1, :] = disp_in[q, slab - 1 :]
        down_ref[TILE + q : TILE + q + 1, :] = disp_in[q, :1]
    spare = TILE - comps
    for ref, row in ((up_ref, slab - 1), (down_ref, 0)):
        ref[comps:TILE, :] = jnp.broadcast_to(solid[row : row + 1], (spare, width))
        ref[TILE + comps :, :] = jnp.zeros((spare, width), F32)


def ends_kernel(comps, ends_ref, up_ref, down_ref, before_ref, after_ref, out_ref):
    rows = ends_ref.shape[0] // comps
    width = ends_ref.shape[1]
    row = rows_of((rows, width))
    spare = rows_of((TILE, width))
    solid_before = before_ref[comps : comps + 1]
    solid_after = after_ref[comps : comps + 1]
    for q in range(comps):
        disp_before = before_ref[TILE + q : TILE + q + 1]
        disp_after = after_ref[TILE + q : TILE + q + 1]
        part = ends_ref[pl.ds(q * rows, rows), :]
        part = part + jnp.where(row == 0, down_ref[comps : comps + 1] * disp_before, 0.0)
        part = part + jnp.where(row == rows - 1, up_ref[comps : comps + 1] * disp_after, 0.0)
        out_ref[pl.ds(q * (rows + TILE), rows), :] = part
        res_before = before_ref[q : q + 1] + solid_before * down_ref[TILE + q : TILE + q + 1]
        res_after = after_ref[q : q + 1] + solid_after * up_ref[TILE + q : TILE + q + 1]
        beyond = jnp.zeros((TILE, width), F32)
        for i, value in enumerate((res_before, res_after, disp_before, disp_after, solid_before, solid_after)):
            beyond = jnp.where(spare == i, value, beyond)
        out_ref[pl.ds(q * (rows + TILE) + rows, TILE), :] = beyond


def in_order(odd, own, core, across, both):
    return own, jnp.where(odd, both, core), across, jnp.where(odd, core, both)


def butterfly(x0, x1, x2, x3):
    even, other = x0 + x2, x1 + x3
    return even + other, even - other, x0 - x2, x1 - x3


def edge_table(odd, blocks):
    tiles = in_order(odd, *blocks)
    left = [t[:, :LANES] for t in tiles]
    right = [t[:, LANES:] for t in tiles]
    solid = TILE - 1
    at_left = [left[s][solid:] * right[s - 1] for s in range(SECTORS)]
    at_right = [right[s][solid:] * left[(s + 1) % SECTORS] for s in range(SECTORS)]
    stack = []
    for one, other in zip(butterfly(*at_left), butterfly(*at_right)):
        stack += [one, other]
    stack += [at_left[0], at_right[0], right[3], left[1]]
    stack.append(jnp.zeros((LANES - len(stack) * TILE, LANES), F32))
    return jnp.concatenate(stack, axis=0).T


def transform_kernel(comps, rows_at, spare, make_edge, own_ref, core_ref, across_ref, both_ref, *refs):
    refs = list(refs)
    edge_in = None if make_edge else refs.pop(0)
    forward_ref, inverse_ref, beyond_ref, weight_ref, hole_ref = refs[:5]
    refs = refs[5:]
    edge_ref = refs.pop(0) if make_edge else edge_in
    prec_ref, residual_ref, left_ref, spectrum_ref, scaled_ref, halo_ref = refs
    width = own_ref.shape[1]
    half = width // 2
    odd = lax.axis_index("sec") % 2 == 1
    sign = jnp.where(odd, -1.0, 1.0)
    main = sum(size for _, size in rows_at)
    rows = main + spare
    total = comps * rows
    group = 1 if rows % 16 == 0 else 2
    sources = (own_ref, core_ref, across_ref, both_ref)
    if make_edge:
        edge_ref[...] = edge_table(odd, [r[total : total + TILE] for r in sources])
    solid = jnp.concatenate([(1 - hole_ref[pl.ds(at, size)]).astype(F32) for at, size in rows_at], axis=0)
    edge = jnp.concatenate([edge_ref[pl.ds(at, size)] for at, size in rows_at], axis=0)
    lane = lanes_of((main, LANES))
    first = lane == 0
    last = lane == LANES - 1

    def with_edges(x, array, q):
        column = array * 2 * TILE + q
        head = x[:, :LANES] + jnp.where(first, edge[:, column : column + 1], 0.0)
        tail = x[:, -LANES:] + jnp.where(last, edge[:, column + TILE : column + TILE + 1], 0.0)
        middle = [x[:, LANES:-LANES]] if width > 2 * LANES else []
        return jnp.concatenate([head] + middle + [tail], axis=1)

    def arrays_of(q):
        at = q * rows
        own, core, across, both = [r[pl.ds(at, main), :] for r in sources]
        arrays = butterfly(own, core, across, both)
        arrays = arrays[:3] + (sign * arrays[3],)
        arrays = [with_edges(x, i, q) for i, x in enumerate(arrays)]
        residual_ref[q] = with_edges(own, 4, q)
        mask = None
        if spare:
            tiles = in_order(odd, *[r[pl.ds(at + main, spare), :] for r in sources])
            disp = [pltpu.roll(t, spare - 2, 0) for t in tiles]
            holes = [pltpu.roll(t, spare - 4, 0) for t in tiles]
            place = lanes_of((spare, width))
            fixed = []
            for s in range(SECTORS):
                beside = jnp.where(place == 0, pltpu.roll(disp[s - 1], 1, 1), 0.0)
                beside = beside + jnp.where(
                    place == width - 1, pltpu.roll(disp[(s + 1) % SECTORS], width - 1, 1), 0.0
                )
                value = tiles[s] + holes[s] * beside
                fixed.append(jnp.where(rows_of((spare, width)) < 2, value, 0.0))
            mask = holes[0]
            arrays = [jnp.concatenate(pair, axis=0) for pair in zip(arrays, butterfly(*fixed))]
        y0, y2, real, imag = arrays
        turned_real = (real[:, half:] - imag[:, half:]) * F32(np.sqrt(0.5))
        turned_imag = (real[:, half:] + imag[:, half:]) * F32(np.sqrt(0.5))
        plus = jnp.concatenate([real[:, :half] + turned_real, imag[:, :half] + turned_imag], axis=1)
        minus = jnp.concatenate([real[:, :half] - turned_real, imag[:, :half] - turned_imag], axis=1)
        return (y0, y2, plus, minus), mask

    masks = []
    for start in range(0, comps, group):
        found = [arrays_of(q) for q in range(start, start + group)]
        masks += [mask for _, mask in found]
        at = pl.ds(start * rows, group * rows)
        for i in range(4):
            high, low = split(jnp.concatenate([arrays[i] for arrays, _ in found], axis=0))
            left_ref[at, 2 * i * width : (2 * i + 1) * width] = high
            left_ref[at, (2 * i + 1) * width : (2 * i + 2) * width] = low

    for i in range(4):
        high = left_ref[:, 2 * i * width : (2 * i + 1) * width]
        low = left_ref[:, (2 * i + 1) * width : (2 * i + 2) * width]
        spectrum_ref[:, i * width : (i + 1) * width] = jnp.dot(
            jnp.concatenate([high, low, high], axis=1),
            forward_ref[pl.ds(3 * i * width, 3 * width), :],
            preferred_element_type=F32,
        )

    around = SECTORS * width
    block = rows if group > 1 else 16

    def scale(step, carry):
        def at(q, count):
            return pl.ds(pl.multiple_of(q * rows + step * block, TILE), count)

        halo = [[jnp.zeros((block, LANES), F32) for _ in range(2)] for _ in range(comps)]
        for lanes in range(0, around, LANES):
            here = slice(lanes, lanes + LANES)
            parts = [spectrum_ref[at(p, block), here] for p in range(comps)]
            for start in range(0, comps, group):
                values = []
                for q in range(start, start + group):
                    value = parts[0] * weight_ref[q * comps : q * comps + 1, here]
                    for p in range(1, comps):
                        value = value + parts[p] * weight_ref[q * comps + p : q * comps + p + 1, here]
                    for i in range(2):
                        halo[q][i] = halo[q][i] + value * beyond_ref[i : i + 1, here]
                    values.append(value)
                high, low = split(jnp.concatenate(values, axis=0))
                scaled_ref[at(start, group * block), here] = high
                scaled_ref[at(start, group * block), around + lanes : around + lanes + LANES] = low
        for q in range(comps):
            before, after = [jnp.sum(x, axis=1, keepdims=True) for x in halo[q]]
            halo_ref[at(q, block), :] = jnp.where(lanes_of((block, LANES)) == 0, before, after)
        return carry

    lax.fori_loop(0, rows // block, scale, 0)
    high = scaled_ref[:, :around]
    result = jnp.dot(
        jnp.concatenate([high, scaled_ref[:, around:], high], axis=1),
        inverse_ref[...],
        preferred_element_type=F32,
    )
    for q in range(comps):
        at = q * rows
        prec_ref[q, :main, :width] = result[at : at + main] * solid
        prec_ref[q, :, width:] = halo_ref[pl.ds(at, rows), :]
        if spare:
            prec_ref[q, main:, :width] = result[at + main : at + rows] * masks[q]


def image_rows(q, fields, tiles, edge, stiff, solid, factor, before, after, inner):
    field = fields[q][inner]
    solid_before = edge[:, 11 * TILE - 1 : 11 * TILE]
    solid_after = edge[:, 12 * TILE - 1 : 12 * TILE]
    beside = beside_sum(field, tiles[q][:, :1] * solid_before, tiles[q][:, 1:2] * solid_after)
    beside = beside + stacked_sum(fields[q], before, after)[inner]
    stiffness = stiff * factor[:, q : q + 1]
    return field, solid * ((stiffness + 4.5) * field - beside - 0.5 * fields[q ^ 1][inner])


def add_sums(sums, residual, field, image):
    rows, width = field.shape
    pairs = ((residual, field), (field, image), (residual, residual), (residual, image), (image, image))
    return [
        total + jnp.sum((x * y).reshape(rows // TILE, TILE, width), axis=0)
        for total, (x, y) in zip(sums, pairs)
    ]


def middle_kernel(
    cuts, comps, stiff_ref, hole_ref, factor_ref, edge_ref, p0_ref, p1_ref, r0_ref, r1_ref, image_ref, sums_ref,
):
    slab, width = hole_ref.shape
    a, b, c = cuts
    low, high = a + TILE, c - TILE
    fields = [jnp.concatenate([p0_ref[q, :, :width], p1_ref[q, :, :width]], axis=0) for q in range(comps)]
    solid = (1 - hole_ref[low:high]).astype(F32)
    factor, edge = factor_ref[low:high], edge_ref[low:high]
    sums = [jnp.zeros((TILE, width), F32) for _ in range(5)]
    for q in range(comps):
        tile = jnp.concatenate([p0_ref[q, TILE:, width:], p1_ref[q, :-TILE, width:]], axis=0)
        field, image = image_rows(
            q, fields, {q: tile}, edge, stiff_ref[q, low:high], solid, factor, 0.0, 0.0, slice(TILE, -TILE)
        )
        image_ref[q] = image
        residual = jnp.concatenate([r0_ref[q, TILE:], r1_ref[q, :-TILE]], axis=0)
        sums = add_sums(sums, residual, field, image)
    for i, total in enumerate(sums):
        sums_ref[pl.ds(i * TILE, TILE), :] = total


def outer_kernel(
    cuts, comps, stiff_ref, hole_ref, factor_ref, edge_ref, p0_ref, p1_ref, p2_ref,
    r0_ref, r1_ref, r2_ref, partial_ref, image_ref, sums_ref,
):
    slab, width = hole_ref.shape
    a, b, c = cuts
    own, side = slice(0, width), slice(width, width + LANES)
    reach = a + TILE
    spare = a + slab - c
    sums = [partial_ref[pl.ds(i * TILE, TILE), :] for i in range(5)]
    tops = [jnp.concatenate([p2_ref[q, :a, own], p0_ref[q, : 2 * TILE, own]], axis=0) for q in range(comps)]
    bottoms = [jnp.concatenate([p1_ref[q, -2 * TILE :, own], p2_ref[q, a:spare, own]], axis=0) for q in range(comps)]
    solid = (1 - hole_ref[...]).astype(F32)
    factor, edge = factor_ref[...], edge_ref[...]
    for q in range(comps):
        tile = jnp.concatenate([p2_ref[q, :a, side], p0_ref[q, :TILE, side]], axis=0)
        rows = slice(0, reach)
        field, image = image_rows(
            q, tops, {q: tile}, edge[rows], stiff_ref[q, rows], solid[rows], factor[rows],
            p2_ref[q, spare : spare + 1, own], 0.0, slice(0, reach),
        )
        image_ref[q, :reach] = image
        residual = jnp.concatenate([r2_ref[q, :a], r0_ref[q, :TILE]], axis=0)
        sums = add_sums(sums, residual, field, image)
        tile = jnp.concatenate([p1_ref[q, -TILE:, side], p2_ref[q, a:spare, side]], axis=0)
        rows = slice(c - TILE, slab)
        field, image = image_rows(
            q, bottoms, {q: tile}, edge[rows], stiff_ref[q, rows], solid[rows], factor[rows],
            0.0, p2_ref[q, spare + 1 : spare + 2, own], slice(TILE, None),
        )
        image_ref[q, reach:] = image
        residual = jnp.concatenate([r1_ref[q, -TILE:], r2_ref[q, a:]], axis=0)
        sums = add_sums(sums, residual, field, image)
    row = jnp.zeros((1, LANES), F32)
    spot = lanes_of((1, LANES))
    for i, value in enumerate(sums):
        value = jnp.sum(jnp.sum(value, axis=0, keepdims=True), axis=1, keepdims=True)
        row = jnp.where(spot == i, value, row)
    sums_ref[...] = jnp.broadcast_to(row, sums_ref.shape)


def update_kernel(
    cuts, comps, cell_total, disp_ref, middle_ref, outer_ref, gathered_ref,
    p0_ref, p1_ref, p2_ref, r0_ref, r1_ref, r2_ref, disp_out, residual_out, stats_out,
):
    slab, width = disp_ref.shape[1:]
    a, b, c = cuts
    values = jnp.sum(gathered_ref[...], axis=0, keepdims=True) * F32(1.0 / cell_total)
    rz, zq, rr, ri, ii = [values[:, i : i + 1] for i in range(5)]
    alpha = rz / zq
    square = rr + alpha * (alpha * ii - 2.0 * ri)
    stats_out[...] = jnp.concatenate([rz, zq, square], axis=1)
    own = slice(0, width)
    reach = a + TILE
    for q in range(comps):
        disp_out[q, :a] = disp_ref[q, :a] + alpha * p2_ref[q, :a, own]
        disp_out[q, a:b] = disp_ref[q, a:b] + alpha * p0_ref[q, :, own]
        disp_out[q, b:c] = disp_ref[q, b:c] + alpha * p1_ref[q, :, own]
        disp_out[q, c:] = disp_ref[q, c:] + alpha * p2_ref[q, a : a + slab - c, own]
        image = jnp.concatenate([outer_ref[q, :reach], middle_ref[q], outer_ref[q, reach:]], axis=0)
        residual_out[q, :a] = r2_ref[q, :a] - alpha * image[:a]
        residual_out[q, a:b] = r0_ref[q] - alpha * image[a:b]
        residual_out[q, b:c] = r1_ref[q] - alpha * image[b:c]
        residual_out[q, c:] = r2_ref[q, a:] - alpha * image[c:]


VMEM = pl.BlockSpec(memory_space=pltpu.VMEM)
SMEM = pl.BlockSpec(memory_space=pltpu.SMEM)
HBM = pl.BlockSpec(memory_space=pltpu.HBM)
FULL = 62


def call(kernel, name, out_shapes, in_specs, flops, moved, scratch=(), grant=32):
    return pl.pallas_call(
        kernel,
        out_shape=[jax.ShapeDtypeStruct(s, F32) for s in out_shapes],
        in_specs=in_specs,
        out_specs=[VMEM] * len(out_shapes),
        scratch_shapes=list(scratch),
        compiler_params=pltpu.CompilerParams(vmem_limit_bytes=grant * 1024 * 1024),
        cost_estimate=pl.CostEstimate(flops=flops, bytes_accessed=moved, transcendentals=0),
        name=name,
    )


def transform_call(blocks, edge, tables, hole, rows_at, spare, comps, width, slab):
    forward, inverse, beyond, weight = tables
    around = SECTORS * width
    main = sum(size for _, size in rows_at)
    rows = main + spare
    total = comps * rows
    out_shapes = [(comps, rows, width + LANES), (comps, main, width)]
    if edge is None:
        out_shapes = [(slab, LANES)] + out_shapes
    operands = list(blocks) + ([] if edge is None else [edge]) + [forward, inverse, beyond, weight, hole]
    return call(
        functools.partial(transform_kernel, comps, rows_at, spare, edge is None), "transform",
        out_shapes, [VMEM] * len(operands),
        2 * total * 3 * around * 2 * width, 4 * total * width * 8,
        [pltpu.VMEM((total, 8 * width), BF16), pltpu.VMEM((total, around), F32),
         pltpu.VMEM((total, 2 * around), BF16), pltpu.VMEM((total, LANES), F32)],
    )(*operands)


def after_all(x, *others):
    return lax.optimization_barrier((x, *others))[0]


def shards(load, disp, stiff, hole, section_class, class_table, precond):
    slab, comps, width = disp.shape
    ax, sec = lax.axis_size("ax"), lax.axis_size("sec")
    around = width * sec
    cell_total = slab * ax * comps * around
    cuts = (slab // 16, slab // 16 * 9, slab - slab // 16)
    a, b, c = cuts
    ends = a + slab - c
    load, disp, stiff = [x.transpose(1, 0, 2) for x in (load, disp, stiff)]
    forward, inverse, beyond, fold = harmonic_tables(width)
    block = 4 * comps * slab * width
    classes = section_class.reshape(1, slab)

    def inputs(rows, count):
        return [pltpu.VMEM((comps, rows, width), F32), pltpu.VMEM((comps, slab, width), F32),
                pltpu.VMEM((comps, rows, width), F32), pltpu.VMEM((slab, width), jnp.int32),
                pltpu.SemaphoreType.DMA((count,))]

    specs = [SMEM, VMEM] + [HBM] * 4
    arguments = (class_table, classes, load, disp, stiff, hole)
    (first,) = call(
        functools.partial(first_kernel, cuts, comps, ax), "first",
        [(comps * (b - a) + TILE, width)], specs, 10 * comps * slab * width, 2 * block,
        inputs(b - a, 1 + 3 * comps), FULL,
    )(*arguments)
    second, edge_rows, factor, up, down = call(
        functools.partial(second_kernel, cuts, comps, ax), "second",
        [(comps * (c - b), width), (comps * ends, width), (slab, LANES), (2 * TILE, width), (2 * TILE, width)],
        specs, 10 * comps * slab * width, 2 * block,
        inputs(a + slab - b, 1 + 5 * comps), FULL,
    )(*arguments)

    def across(x):
        return lax.ppermute(x, "sec", [(i, (i + sec // 2) % sec) for i in range(sec)])

    def beside(x):
        return lax.ppermute(x, "sec", [(i, i ^ 1) for i in range(sec)])

    far0 = across(first)
    far1 = across(second)
    before = lax.ppermute(up, "ax", [(i, i + 1) for i in range(ax - 1)])
    after = lax.ppermute(down, "ax", [(i + 1, i) for i in range(ax - 1)])
    (weight,) = call(
        fold_kernel, "fold", [(comps * comps, around)], [VMEM] * 2,
        6 * comps * comps * around * around, 2 * around * around,
    )(precond, fold)
    (last,) = call(
        functools.partial(ends_kernel, comps), "ends",
        [(comps * (ends + TILE), width)], [VMEM] * 5, comps * ends * width, 8 * comps * ends * width,
    )(edge_rows, up, down, before, after)
    far2 = across(last)
    tables = (forward, inverse, beyond, weight)

    far0 = after_all(far0, second, last)
    edge, prec0, res0 = transform_call(
        (first, beside(first), far0, beside(far0)), None, tables, hole, ((a, b - a),), 0, comps, width, slab
    )
    far1 = after_all(far1, prec0)
    prec1, res1 = transform_call(
        (second, beside(second), far1, beside(far1)), edge, tables, hole, ((b, c - b),), 0, comps, width, slab
    )
    far2 = after_all(far2, prec1)
    image, partial = call(
        functools.partial(middle_kernel, cuts, comps), "middle",
        [(comps, c - a - 2 * TILE, width), (5 * TILE, width)], [VMEM] * 8, 30 * comps * slab * width, 4 * block,
    )(stiff, hole, factor, edge, prec0, prec1, res0, res1)
    prec2, res2 = transform_call(
        (last, beside(last), far2, beside(far2)), edge, tables, hole, ((0, a), (c, slab - c)), TILE, comps, width, slab
    )
    image_ends, sums = call(
        functools.partial(outer_kernel, cuts, comps), "outer",
        [(comps, ends + 2 * TILE, width), (ax * sec, LANES)], [VMEM] * 11, 8 * comps * slab * width, block,
    )(stiff, hole, factor, edge, prec0, prec1, prec2, res0, res1, res2, partial)
    gathered = lax.all_to_all(sums, ("ax", "sec"), 0, 0, tiled=True)
    disp_new, residual_new, stats = call(
        functools.partial(update_kernel, cuts, comps, cell_total), "update",
        [(comps, slab, width), (comps, slab, width), (1, 3)], [VMEM] * 10,
        4 * comps * slab * width, 6 * block,
    )(disp, image, image_ends, gathered, prec0, prec1, prec2, res0, res1, res2)
    return disp_new.transpose(1, 0, 2), residual_new.transpose(1, 0, 2), stats.reshape(3)


def solution(mesh):
    in_specs = (
        P("ax", None, "sec"),
        P("ax", None, "sec"),
        P("ax", None, "sec"),
        P("ax", "sec"),
        P("ax"),
        P(),
        P(),
    )
    out_specs = (P("ax", None, "sec"), P("ax", None, "sec"), P())
    return jax.shard_map(shards, mesh=mesh, in_specs=in_specs, out_specs=out_specs, check_vma=False)
```

```python
import functools

import jax
import jax.numpy as jnp
import ml_dtypes
import numpy as np
from jax import lax
from jax.experimental import pallas as pl
from jax.experimental.pallas import tpu as pltpu
from jax.sharding import PartitionSpec as P

F32 = jnp.float32
BF16 = jnp.bfloat16
SECTORS = 4
TILE = 8
LANES = 128


def three_terms(table):
    high = table.astype(ml_dtypes.bfloat16)
    low = (table - high.astype(np.float64)).astype(ml_dtypes.bfloat16)
    return np.concatenate([high, high, low], axis=0)


@functools.lru_cache(maxsize=None)
def harmonic_tables(width):
    around = SECTORS * width
    half = width // 2
    zero = [("c", 4 * q) for q in range(half + 1)] + [("s", 4 * q) for q in range(1, half)]
    two = [(f, 4 * q + 2) for f in "cs" for q in range(half)]
    one = [(f, 8 * q + 1) for f in "cs" for q in range(half)]
    five = [(f, 8 * q + 5) for f in "cs" for q in range(half)]
    columns = zero + two + one + five
    harmonic = np.array([k for _, k in columns], dtype=np.int64)
    is_sin = np.array([f == "s" for f, _ in columns])

    def wave(place, shift):
        angle = 2.0 * np.pi / around * ((place[:, None] * harmonic[None, :]) % around)
        return np.cos(angle - shift)

    place = np.arange(width)
    shift = np.where(is_sin, np.pi / 2, 0.0)[None, :]
    direct = wave(place, shift)
    turned = np.concatenate([direct[:half], wave(place[:half], shift - np.pi / 2)], axis=0)
    forward = [direct[:, :width], direct[:, width : 2 * width]]
    forward += [turned[:, 2 * width : 3 * width], turned[:, 3 * width :]]
    beyond = wave(np.array([around - 1, width]), shift).astype(np.float32)
    beyond = np.repeat(beyond[:, None, :], TILE, axis=1)
    fold = np.zeros((around, 4 * half))
    kinds = [4 * np.arange(half), 4 * np.arange(half) + 2, 8 * np.arange(half) + 1, 8 * np.arange(half) + 5]
    for column, k in enumerate(np.concatenate(kinds)):
        for place in {k, (around - k) % around}:
            fold[place, column] = 1.0 / around
    return (
        np.concatenate([three_terms(t) for t in forward], axis=0),
        three_terms(direct.T),
        beyond,
        fold.astype(ml_dtypes.bfloat16),
    )


def split(x):
    high = x.astype(BF16)
    return high, (x - high.astype(F32)).astype(BF16)


def lanes_of(shape):
    return lax.broadcasted_iota(jnp.int32, shape, len(shape) - 1)


def rows_of(shape):
    return lax.broadcasted_iota(jnp.int32, shape, len(shape) - 2)


def beside_sum(x, before, after):
    lane = lanes_of(x.shape)
    size = x.shape[-1]
    left = jnp.where(lane == 0, before, pltpu.roll(x, 1, x.ndim - 1))
    right = jnp.where(lane == size - 1, after, pltpu.roll(x, size - 1, x.ndim - 1))
    return left + right


def stacked_sum(x, before=0.0, after=0.0):
    row = rows_of(x.shape)
    size = x.shape[0]
    up = jnp.where(row == 0, before, pltpu.roll(x, 1, 0))
    down = jnp.where(row == size - 1, after, pltpu.roll(x, size - 1, 0))
    return up + down


def fold_kernel(precond_ref, fold_ref, out_ref):
    comps = precond_ref.shape[0]
    value = jnp.concatenate([precond_ref[q] for q in range(comps)], axis=0)
    pairs, around = value.shape
    high = value.astype(BF16)
    rest = value - high.astype(F32)
    middle = rest.astype(BF16)
    low = (rest - middle.astype(F32)).astype(BF16)
    terms = [jnp.dot(t, fold_ref[...], preferred_element_type=F32) for t in (high, middle, low)]
    folded = terms[0] + (terms[1] + terms[2])
    half = folded.shape[1] // 4
    zero = folded[:, :half]
    top = value[:, around // 2 : around // 2 + 1] * F32(1.0 / around)
    other = jnp.where(lanes_of(zero.shape) == 0, top, zero)
    folded = jnp.concatenate([zero, other, folded[:, half:]], axis=1)
    for i in range(pairs):
        out_ref[i] = jnp.broadcast_to(folded[i : i + 1], out_ref.shape[1:])


def factor_columns(table_ref, class_ref, ax_size, comps):
    classes = class_ref[...]
    slab = classes.shape[1]
    position = lax.axis_index("ax") * slab + lanes_of(classes.shape)
    taper = 1.0 + 2.0 * position.astype(F32) / F32(ax_size * slab - 1)
    rows = []
    for q in range(comps):
        value = jnp.zeros(classes.shape, F32)
        for kind in range(table_ref.shape[0]):
            value = jnp.where(classes == kind, table_ref[kind, q], value)
        rows.append(value * taper)
    rows.append(jnp.zeros((LANES - comps, slab), F32))
    return jnp.concatenate(rows, axis=0).T


def local_part(q, block, inner, solid, factor, load, stiff, other):
    field = block[inner]
    beside = stacked_sum(block)[inner] + beside_sum(field, 0.0, 0.0)
    stiffness = stiff * factor[:, q : q + 1]
    image = (stiffness + 4.5) * field - beside - 0.5 * other[inner]
    return solid * (load - image)


def edge_rows(fields, solid):
    rows, width = solid.shape
    sources = fields + [solid] * (TILE - len(fields))
    columns = [x[:, :1] for x in sources] + [x[:, width - 1 :] for x in sources]
    table = jnp.concatenate(columns + [jnp.zeros((rows, LANES - 2 * TILE), F32)], axis=1)
    if rows < LANES:
        table = jnp.concatenate([table, jnp.zeros((LANES - rows, LANES), F32)], axis=0)
    table = table.T
    return table[:TILE], table[TILE : 2 * TILE]


def first_kernel(
    cuts, comps, ax_size, table_ref, class_ref, load_ref, disp_ref, stiff_ref, hole_ref,
    first_ref, ends_ref, factor_ref, up_ref, down_ref,
    table_in, class_in, load_in, disp_in, stiff_in, hole_in, first_out, ends_out, factor_out, up_out, down_out,
    in_sems, out_sems,
):
    slab, width = hole_ref.shape
    a, b, c = cuts
    top, bottom = b + TILE, slab - c + TILE

    def copy(src, dst, sems, i):
        moving = pltpu.make_async_copy(src, dst, sems.at[i])
        moving.start()
        return moving

    def two(src, dst, i):
        return [
            copy(src.at[pl.ds(0, top)], dst.at[pl.ds(0, top)], in_sems, i),
            copy(src.at[pl.ds(slab - bottom, bottom)], dst.at[pl.ds(top, bottom)], in_sems, i + 1),
        ]

    small = [copy(class_ref, class_in, in_sems, 0), copy(table_ref, table_in, in_sems, 1)]
    hole_moving = two(hole_ref, hole_in, 2)
    moving = []
    for q in range(comps):
        moving.append([])
        for k, (src, dst) in enumerate(((disp_ref, disp_in), (load_ref, load_in), (stiff_ref, stiff_in))):
            moving[q] += two(src.at[q], dst.at[q], 4 + 6 * q + 2 * k)
    for one in small:
        one.wait()
    factor_out[...] = factor_columns(table_in, class_in, ax_size, comps)
    leaving = [copy(factor_out, factor_ref, out_sems, 0)]
    for one in hole_moving:
        one.wait()
    solid = (1 - hole_in[...]).astype(F32)
    factor = factor_out[...]
    ends = a + slab - c
    stride = b - a
    for q in range(comps):
        if q % 2 == 0:
            for one in moving[q] + moving[q + 1]:
                one.wait()
        high = disp_in[q, :top]
        low = disp_in[q, top:]
        upper = local_part(
            q, high, slice(0, b), solid[:b], factor[:b], load_in[q, :b], stiff_in[q, :b], disp_in[q ^ 1, :top]
        )
        lower = local_part(
            q, low, slice(TILE, bottom), solid[top + TILE :], factor[c:],
            load_in[q, top + TILE :], stiff_in[q, top + TILE :], disp_in[q ^ 1, top:],
        )
        first_out[pl.ds(q * stride, stride), :] = upper[a:]
        leaving.append(
            copy(first_out.at[pl.ds(q * stride, stride)], first_ref.at[pl.ds(q * stride, stride)], out_sems, 1 + q)
        )
        ends_out[pl.ds(q * ends, a), :] = upper[:a]
        ends_out[pl.ds(q * ends + a, slab - c), :] = lower
        up_out[q : q + 1, :] = lower[slab - c - 1 :]
        down_out[q : q + 1, :] = upper[:1]
        up_out[TILE + q : TILE + q + 1, :] = low[bottom - 1 :]
        down_out[TILE + q : TILE + q + 1, :] = high[:1]
    spare = TILE - comps
    for ref, row in ((up_out, top + bottom - 1), (down_out, 0)):
        ref[comps:TILE, :] = jnp.broadcast_to(solid[row : row + 1], (spare, width))
        ref[TILE + comps :, :] = jnp.zeros((spare, width), F32)
    leaving.append(copy(up_out, up_ref, out_sems, 1 + comps))
    leaving.append(copy(down_out, down_ref, out_sems, 2 + comps))

    def chosen(x):
        return jnp.concatenate([x[a:b], x[:a], x[top + TILE :]], axis=0)

    left, right = edge_rows([chosen(disp_in[q]) for q in range(comps)], chosen(solid))
    first_out[pl.ds(comps * stride, TILE), :] = jnp.concatenate([left, right], axis=1)
    left, right = [pltpu.roll(x, LANES - stride, 1) for x in (left, right)]
    ends_out[pl.ds(comps * ends, TILE), :] = jnp.concatenate([left, right], axis=1)
    tail = pl.ds(comps * stride, TILE)
    leaving.append(copy(first_out.at[tail], first_ref.at[tail], out_sems, 3 + comps))
    leaving.append(copy(ends_out, ends_ref, out_sems, 4 + comps))
    for one in leaving:
        one.wait()


def second_kernel(cuts, comps, load_ref, disp_ref, stiff_ref, hole_ref, factor_ref, second_ref):
    _, b, c = cuts
    solid = (1 - hole_ref[b:c]).astype(F32)
    factor = factor_ref[b:c]
    rows = c - b
    around = slice(b - TILE, c + TILE)
    for q in range(comps):
        second_ref[pl.ds(q * rows, rows), :] = local_part(
            q, disp_ref[q, around], slice(TILE, TILE + rows), solid, factor,
            load_ref[q, b:c], stiff_ref[q, b:c], disp_ref[q ^ 1, around],
        )
    left, right = edge_rows([disp_ref[q, b:c] for q in range(comps)], solid)
    second_ref[pl.ds(comps * rows, TILE), :] = jnp.concatenate([left, right], axis=1)


def ends_kernel(comps, ends_ref, up_ref, down_ref, before_ref, after_ref, out_ref):
    rows = (ends_ref.shape[0] - TILE) // comps
    width = ends_ref.shape[1]
    row = rows_of((rows, width))
    spare = rows_of((TILE, width))
    solid_before = before_ref[comps : comps + 1]
    solid_after = after_ref[comps : comps + 1]
    for q in range(comps):
        disp_before = before_ref[TILE + q : TILE + q + 1]
        disp_after = after_ref[TILE + q : TILE + q + 1]
        part = ends_ref[pl.ds(q * rows, rows), :]
        part = part + jnp.where(row == 0, down_ref[comps : comps + 1] * disp_before, 0.0)
        part = part + jnp.where(row == rows - 1, up_ref[comps : comps + 1] * disp_after, 0.0)
        out_ref[pl.ds(q * (rows + TILE), rows), :] = part
        res_before = before_ref[q : q + 1] + solid_before * down_ref[TILE + q : TILE + q + 1]
        res_after = after_ref[q : q + 1] + solid_after * up_ref[TILE + q : TILE + q + 1]
        beyond = jnp.zeros((TILE, width), F32)
        for i, value in enumerate((res_before, res_after, disp_before, disp_after, solid_before, solid_after)):
            beyond = jnp.where(spare == i, value, beyond)
        out_ref[pl.ds(q * (rows + TILE) + rows, TILE), :] = beyond
    out_ref[pl.ds(comps * (rows + TILE), TILE), :] = ends_ref[pl.ds(comps * rows, TILE), :]


def in_order(odd, own, core, across, both):
    return own, jnp.where(odd, both, core), across, jnp.where(odd, core, both)


def butterfly(x0, x1, x2, x3):
    even, other = x0 + x2, x1 + x3
    return even + other, even - other, x0 - x2, x1 - x3


def edge_table(odd, blocks):
    tiles = in_order(odd, *blocks)
    left = [t[:, :LANES] for t in tiles]
    right = [t[:, LANES:] for t in tiles]
    solid = TILE - 1
    at_left = [left[s][solid:] * right[s - 1] for s in range(SECTORS)]
    at_right = [right[s][solid:] * left[(s + 1) % SECTORS] for s in range(SECTORS)]
    stack = []
    for one, other in zip(butterfly(*at_left), butterfly(*at_right)):
        stack += [one, other]
    stack += [at_left[0], at_right[0], right[3], left[1]]
    stack.append(jnp.zeros((LANES - len(stack) * TILE, LANES), F32))
    return jnp.concatenate(stack, axis=0).T


def transform_kernel(
    comps, rows_at, spare, own_ref, core_ref, across_ref, both_ref,
    forward_ref, inverse_ref, beyond_ref, weight_ref, hole_ref,
    prec_ref, residual_ref, left_ref, spectrum_ref, scaled_ref, halo_ref,
):
    width = own_ref.shape[1]
    half = width // 2
    odd = lax.axis_index("sec") % 2 == 1
    sign = jnp.where(odd, -1.0, 1.0)
    main = sum(size for _, size in rows_at)
    rows = main + spare
    total = comps * rows
    group = 1 if rows % 16 == 0 else 2
    sources = (own_ref, core_ref, across_ref, both_ref)
    solid = jnp.concatenate([(1 - hole_ref[pl.ds(at, size)]).astype(F32) for at, size in rows_at], axis=0)
    edge = edge_table(odd, [r[total : total + TILE] for r in sources])[:main]
    lane = lanes_of((main, LANES))
    first = lane == 0
    last = lane == LANES - 1

    def with_edges(x, array, q):
        column = array * 2 * TILE + q
        head = x[:, :LANES] + jnp.where(first, edge[:, column : column + 1], 0.0)
        tail = x[:, -LANES:] + jnp.where(last, edge[:, column + TILE : column + TILE + 1], 0.0)
        middle = [x[:, LANES:-LANES]] if width > 2 * LANES else []
        return jnp.concatenate([head] + middle + [tail], axis=1)

    def arrays_of(q):
        at = q * rows
        own, core, across, both = [r[pl.ds(at, main), :] for r in sources]
        arrays = butterfly(own, core, across, both)
        arrays = arrays[:3] + (sign * arrays[3],)
        arrays = [with_edges(x, i, q) for i, x in enumerate(arrays)]
        residual_ref[q] = with_edges(own, 4, q)
        mask = None
        if spare:
            tiles = in_order(odd, *[r[pl.ds(at + main, spare), :] for r in sources])
            disp = [pltpu.roll(t, spare - 2, 0) for t in tiles]
            holes = [pltpu.roll(t, spare - 4, 0) for t in tiles]
            place = lanes_of((spare, width))
            fixed = []
            for s in range(SECTORS):
                beside = jnp.where(place == 0, pltpu.roll(disp[s - 1], 1, 1), 0.0)
                beside = beside + jnp.where(
                    place == width - 1, pltpu.roll(disp[(s + 1) % SECTORS], width - 1, 1), 0.0
                )
                value = tiles[s] + holes[s] * beside
                fixed.append(jnp.where(rows_of((spare, width)) < 2, value, 0.0))
            mask = holes[0]
            arrays = [jnp.concatenate(pair, axis=0) for pair in zip(arrays, butterfly(*fixed))]
        y0, y2, real, imag = arrays
        turned_real = (real[:, half:] - imag[:, half:]) * F32(np.sqrt(0.5))
        turned_imag = (real[:, half:] + imag[:, half:]) * F32(np.sqrt(0.5))
        plus = jnp.concatenate([real[:, :half] + turned_real, imag[:, :half] + turned_imag], axis=1)
        minus = jnp.concatenate([real[:, :half] - turned_real, imag[:, :half] - turned_imag], axis=1)
        return (y0, y2, plus, minus), mask

    beyond_solid = jnp.where(first, edge[:, 11 * TILE - 1 : 11 * TILE], edge[:, 12 * TILE - 1 : 12 * TILE])
    masks = []
    for start in range(0, comps, group):
        found = [arrays_of(q) for q in range(start, start + group)]
        masks += [mask for _, mask in found]
        at = pl.ds(start * rows, group * rows)
        for i in range(4):
            high, low = split(jnp.concatenate([arrays[i] for arrays, _ in found], axis=0))
            left_ref[at, 2 * i * width : (2 * i + 1) * width] = high
            left_ref[at, (2 * i + 1) * width : (2 * i + 2) * width] = low

    for i in range(4):
        high = left_ref[:, 2 * i * width : (2 * i + 1) * width]
        low = left_ref[:, (2 * i + 1) * width : (2 * i + 2) * width]
        part = jnp.dot(
            jnp.concatenate([high, low, high], axis=1),
            forward_ref[pl.ds(3 * i * width, 3 * width), :],
            preferred_element_type=F32,
        )
        spectrum_ref[:, :, i * width : (i + 1) * width] = part.reshape(total // TILE, TILE, width)

    around = SECTORS * width

    def scale(row, count):
        tiles = count // TILE

        def spectrum(p, lanes):
            return spectrum_ref[pl.ds((p * rows + row) // TILE, tiles), :, lanes]

        for start in range(0, comps, group):
            halo = [[None, None] for _ in range(group)]
            for k in range(4):
                for h in range(2):
                    lanes = slice(k * width + h * half, k * width + (h + 1) * half)
                    kind = h if k == 0 else k + 1
                    values = []
                    for i in range(group):
                        value = None
                        for p in range(comps):
                            weight = weight_ref[(start + i) * comps + p, :, kind * half : (kind + 1) * half]
                            term = spectrum(p, lanes) * weight
                            value = term if value is None else value + term
                        for side in range(2):
                            term = value * beyond_ref[side, :, lanes]
                            halo[i][side] = term if halo[i][side] is None else halo[i][side] + term
                        values.append(value.reshape(count, half))
                    high, low = split(values[0] if group == 1 else jnp.concatenate(values, axis=0))
                    at = pl.ds(start * rows + row, group * count)
                    scaled_ref[at, lanes] = high
                    scaled_ref[at, around + lanes.start : around + lanes.stop] = low
            for i in range(group):
                before, after = [jnp.sum(x, axis=2, keepdims=True) for x in halo[i]]
                tile = jnp.where(lanes_of((tiles, TILE, LANES)) == 0, before, after)
                halo_ref[pl.ds((start + i) * rows + row, count), :] = tile.reshape(count, LANES)

    step = rows if group > 1 else 32
    for row in range(0, rows, step):
        scale(row, min(step, rows - row))
    high = scaled_ref[:, :around]
    result = jnp.dot(
        jnp.concatenate([high, scaled_ref[:, around:], high], axis=1),
        inverse_ref[...],
        preferred_element_type=F32,
    )
    for q in range(comps):
        at = q * rows
        prec_ref[q, :main, :width] = result[at : at + main] * solid
        side = halo_ref[pl.ds(at, rows), :]
        prec_ref[q, :main, width:] = side[:main] * beyond_solid
        if spare:
            prec_ref[q, main:, :width] = result[at + main : at + rows] * masks[q]
            prec_ref[q, main:, width:] = side[main:]


def image_rows(q, fields, tile, stiff, solid, factor, before, after, inner):
    field = fields[q][inner]
    beside = beside_sum(field, tile[:, :1], tile[:, 1:2])
    beside = beside + stacked_sum(fields[q], before, after)[inner]
    stiffness = stiff * factor[:, q : q + 1]
    return field, solid * ((stiffness + 4.5) * field - beside - 0.5 * fields[q ^ 1][inner])


def add_sums(sums, residual, field, image):
    rows, width = field.shape
    pairs = ((residual, field), (field, image), (residual, residual), (residual, image), (image, image))
    return [
        total + jnp.sum((x * y).reshape(rows // TILE, TILE, width), axis=0)
        for total, (x, y) in zip(sums, pairs)
    ]


def early_kernel(
    cuts, comps, stiff_ref, hole_ref, factor_ref, p0_ref, p1_ref, r0_ref, r1_ref, image_ref, sums_ref,
):
    slab, width = hole_ref.shape
    a, b, c = cuts
    high = b - TILE
    spare = a + slab - c
    own, side = slice(0, width), slice(width, width + LANES)
    fields = [jnp.concatenate([p1_ref[q, :a, own], p0_ref[q, :, own]], axis=0) for q in range(comps)]
    solid = (1 - hole_ref[:high]).astype(F32)
    factor = factor_ref[:high]
    sums = [jnp.zeros((TILE, width), F32) for _ in range(5)]
    for q in range(comps):
        tile = jnp.concatenate([p1_ref[q, :a, side], p0_ref[q, :-TILE, side]], axis=0)
        field, image = image_rows(
            q, fields, tile, stiff_ref[q, :high], solid, factor, p1_ref[q, spare : spare + 1, own], 0.0, slice(0, high)
        )
        image_ref[q] = image
        residual = jnp.concatenate([r1_ref[q, :a], r0_ref[q, :-TILE]], axis=0)
        sums = add_sums(sums, residual, field, image)
    for i, total in enumerate(sums):
        sums_ref[pl.ds(i * TILE, TILE), :] = total


def late_kernel(
    cuts, comps, stiff_ref, hole_ref, factor_ref, p0_ref, p1_ref, p2_ref,
    r0_ref, r1_ref, r2_ref, partial_ref, image_ref, sums_ref,
):
    slab, width = hole_ref.shape
    a, b, c = cuts
    low = b - TILE
    spare = a + slab - c
    own, side = slice(0, width), slice(width, width + LANES)
    sums = [partial_ref[pl.ds(i * TILE, TILE), :] for i in range(5)]
    fields = [
        jnp.concatenate([p0_ref[q, -2 * TILE :, own], p2_ref[q, :, own], p1_ref[q, a:spare, own]], axis=0)
        for q in range(comps)
    ]
    solid = (1 - hole_ref[low:]).astype(F32)
    factor = factor_ref[low:]
    for q in range(comps):
        tile = jnp.concatenate([p0_ref[q, -TILE:, side], p2_ref[q, :, side], p1_ref[q, a:spare, side]], axis=0)
        field, image = image_rows(
            q, fields, tile, stiff_ref[q, low:], solid, factor,
            0.0, p1_ref[q, spare + 1 : spare + 2, own], slice(TILE, None),
        )
        image_ref[q] = image
        residual = jnp.concatenate([r0_ref[q, -TILE:], r2_ref[q], r1_ref[q, a:]], axis=0)
        sums = add_sums(sums, residual, field, image)
    row = jnp.zeros((1, LANES), F32)
    spot = lanes_of((1, LANES))
    for i, value in enumerate(sums):
        value = jnp.sum(jnp.sum(value, axis=0, keepdims=True), axis=1, keepdims=True)
        row = jnp.where(spot == i, value, row)
    sums_ref[...] = jnp.broadcast_to(row, sums_ref.shape)


def update_kernel(
    cuts, comps, cell_total, disp_ref, early_ref, late_ref, gathered_ref,
    p0_ref, p1_ref, p2_ref, r0_ref, r1_ref, r2_ref, disp_out, residual_out, stats_out,
):
    slab, width = disp_ref.shape[1:]
    a, b, c = cuts
    values = jnp.sum(gathered_ref[...], axis=0, keepdims=True) * F32(1.0 / cell_total)
    rz, zq, rr, ri, ii = [values[:, i : i + 1] for i in range(5)]
    alpha = rz / zq
    square = rr + alpha * (alpha * ii - 2.0 * ri)
    stats_out[...] = jnp.concatenate([rz, zq, square], axis=1)
    low = b - TILE
    pieces = (
        (slice(0, a), p1_ref, r1_ref, slice(0, a)),
        (slice(a, b), p0_ref, r0_ref, slice(0, b - a)),
        (slice(b, c), p2_ref, r2_ref, slice(0, c - b)),
        (slice(c, slab), p1_ref, r1_ref, slice(a, a + slab - c)),
    )
    for q in range(comps):
        image = jnp.concatenate([early_ref[q], late_ref[q]], axis=0)
        for here, prec, residual, there in pieces:
            disp_out[q, here] = disp_ref[q, here] + alpha * prec[q, there, :width]
            residual_out[q, here] = residual[q, there] - alpha * image[here]


VMEM = pl.BlockSpec(memory_space=pltpu.VMEM)
SMEM = pl.BlockSpec(memory_space=pltpu.SMEM)
HBM = pl.BlockSpec(memory_space=pltpu.HBM)
FULL = 62


def call(kernel, name, out_shapes, in_specs, flops, moved, scratch=(), grant=32, out_spec=None):
    return pl.pallas_call(
        kernel,
        out_shape=[jax.ShapeDtypeStruct(s, F32) for s in out_shapes],
        in_specs=in_specs,
        out_specs=[out_spec or VMEM] * len(out_shapes),
        scratch_shapes=list(scratch),
        compiler_params=pltpu.CompilerParams(vmem_limit_bytes=grant * 1024 * 1024),
        cost_estimate=pl.CostEstimate(flops=flops, bytes_accessed=moved, transcendentals=0),
        name=name,
    )


def transform_call(blocks, tables, hole, rows_at, spare, comps, width):
    around = SECTORS * width
    main = sum(size for _, size in rows_at)
    rows = main + spare
    total = comps * rows
    operands = list(blocks) + list(tables) + [hole]
    return call(
        functools.partial(transform_kernel, comps, rows_at, spare), "transform",
        [(comps, rows, width + LANES), (comps, main, width)], [VMEM] * len(operands),
        2 * total * 3 * around * 2 * width, 4 * total * width * 8,
        [pltpu.VMEM((total, 8 * width), BF16), pltpu.VMEM((total // TILE, TILE, around), F32),
         pltpu.VMEM((total, 2 * around), BF16), pltpu.VMEM((total, LANES), F32)],
    )(*operands)


def after_all(x, *others):
    return lax.optimization_barrier((x, *others))[0]


def shards(load, disp, stiff, hole, section_class, class_table, precond):
    slab, comps, width = disp.shape
    ax, sec = lax.axis_size("ax"), lax.axis_size("sec")
    around = width * sec
    cell_total = slab * ax * comps * around
    cuts = (slab // 16, slab // 16 * 11, slab - slab // 16)
    a, b, c = cuts
    ends = a + slab - c
    load, disp, stiff = [x.transpose(1, 0, 2) for x in (load, disp, stiff)]
    forward, inverse, beyond, fold = harmonic_tables(width)
    block = 4 * comps * slab * width
    classes = section_class.reshape(1, slab)

    reach = b + slab - c + 2 * TILE
    shapes = [(comps * (b - a) + TILE, width), (comps * ends + TILE, width), (slab, LANES),
              (2 * TILE, width), (2 * TILE, width)]
    first, edge, factor, up, down = call(
        functools.partial(first_kernel, cuts, comps, ax), "first",
        shapes, [HBM] * 6, 10 * comps * slab * width, 2 * block,
        [pltpu.SMEM(class_table.shape, F32), pltpu.VMEM((1, slab), jnp.int32)]
        + [pltpu.VMEM((comps, reach, width), F32)] * 3 + [pltpu.VMEM((reach, width), jnp.int32)]
        + [pltpu.VMEM(shape, F32) for shape in shapes]
        + [pltpu.SemaphoreType.DMA((4 + 6 * comps,)), pltpu.SemaphoreType.DMA((5 + comps,))],
        FULL, HBM,
    )(class_table, classes, load, disp, stiff, hole)
    (second,) = call(
        functools.partial(second_kernel, cuts, comps), "second",
        [(comps * (c - b) + TILE, width)], [VMEM] * 5, 10 * comps * (c - b) * width, 2 * block,
    )(load, disp, stiff, hole, factor)

    def across(x):
        return lax.ppermute(x, "sec", [(i, i ^ 2) for i in range(sec)])

    def both(x):
        return lax.ppermute(x, "sec", [(i, i ^ 3) for i in range(sec)])

    def beside(x):
        return lax.ppermute(x, "sec", [(i, i ^ 1) for i in range(sec)])

    far0 = across(first)
    before = lax.ppermute(up, "ax", [(i, i + 1) for i in range(ax - 1)])
    after = lax.ppermute(down, "ax", [(i + 1, i) for i in range(ax - 1)])
    (weight,) = call(
        fold_kernel, "fold", [(comps * comps, TILE, 5 * width // 2)], [VMEM] * 2,
        6 * comps * comps * around * around, 2 * around * around,
    )(precond, fold)
    (last,) = call(
        functools.partial(ends_kernel, comps), "ends",
        [(comps * (ends + TILE) + TILE, width)], [VMEM] * 5, comps * ends * width, 8 * comps * ends * width,
    )(edge, up, down, before, after)
    far1 = both(last)
    far2 = across(second)
    tables = (forward, inverse, beyond, weight)

    far0 = after_all(far0, second, last, weight)
    prec0, res0 = transform_call(
        (first, beside(first), far0, beside(far0)), tables, hole, ((a, b - a),), 0, comps, width
    )
    far1 = after_all(far1, prec0)
    prec1, res1 = transform_call(
        (last, beside(last), beside(far1), far1), tables, hole, ((0, a), (c, slab - c)), TILE, comps, width
    )
    far2 = after_all(far2, prec1)
    image, partial = call(
        functools.partial(early_kernel, cuts, comps), "early",
        [(comps, b - TILE, width), (5 * TILE, width)], [VMEM] * 7, 30 * comps * slab * width, 4 * block,
    )(stiff, hole, factor, prec0, prec1, res0, res1)
    prec2, res2 = transform_call(
        (second, beside(second), far2, beside(far2)), tables, hole, ((b, c - b),), 0, comps, width
    )
    image_late, sums = call(
        functools.partial(late_kernel, cuts, comps), "late",
        [(comps, slab - b + TILE, width), (ax * sec, LANES)], [VMEM] * 10, 8 * comps * slab * width, block,
    )(stiff, hole, factor, prec0, prec1, prec2, res0, res1, res2, partial)
    gathered = lax.all_to_all(sums, ("ax", "sec"), 0, 0, tiled=True)
    disp_new, residual_new, stats = call(
        functools.partial(update_kernel, cuts, comps, cell_total), "update",
        [(comps, slab, width), (comps, slab, width), (1, 3)], [VMEM] * 10,
        4 * comps * slab * width, 6 * block,
    )(disp, image, image_late, gathered, prec0, prec1, prec2, res0, res1, res2)
    return disp_new.transpose(1, 0, 2), residual_new.transpose(1, 0, 2), stats.reshape(3)


def solution(mesh):
    in_specs = (
        P("ax", None, "sec"),
        P("ax", None, "sec"),
        P("ax", None, "sec"),
        P("ax", "sec"),
        P("ax"),
        P(),
        P(),
    )
    out_specs = (P("ax", None, "sec"), P("ax", None, "sec"), P())
    return jax.shard_map(shards, mesh=mesh, in_specs=in_specs, out_specs=out_specs, check_vma=False)
```

```python
import functools

import jax
import jax.numpy as jnp
import ml_dtypes
import numpy as np
from jax import lax
from jax.experimental import pallas as pl
from jax.experimental.pallas import tpu as pltpu
from jax.sharding import PartitionSpec as P

F32 = jnp.float32
BF16 = jnp.bfloat16
SECTORS = 4
TILE = 8
LANES = 128


def two_parts(table):
    high = table.astype(ml_dtypes.bfloat16)
    low = (table - high.astype(np.float64)).astype(ml_dtypes.bfloat16)
    return np.stack([high, low])


@functools.lru_cache(maxsize=None)
def harmonic_tables(width):
    around = SECTORS * width
    half = width // 2
    zero = [("c", 4 * q) for q in range(half + 1)] + [("s", 4 * q) for q in range(1, half)]
    two = [(f, 4 * q + 2) for f in "cs" for q in range(half)]
    one = [(f, 8 * q + 1) for f in "cs" for q in range(half)]
    five = [(f, 8 * q + 5) for f in "cs" for q in range(half)]
    columns = zero + two + one + five
    harmonic = np.array([k for _, k in columns], dtype=np.int64)
    is_sin = np.array([f == "s" for f, _ in columns])

    def wave(place, shift):
        angle = 2.0 * np.pi / around * ((place[:, None] * harmonic[None, :]) % around)
        return np.cos(angle - shift)

    place = np.arange(width)
    shift = np.where(is_sin, np.pi / 2, 0.0)[None, :]
    direct = wave(place, shift)
    turned = np.concatenate([direct[:half], wave(place[:half], shift - np.pi / 2)], axis=0)
    forward = [direct[:, :width], direct[:, width : 2 * width]]
    forward += [turned[:, 2 * width : 3 * width], turned[:, 3 * width :]]
    ends = np.array([around - 1, 2 * width, around - width - 1, width])
    beyond = np.repeat(wave(ends, shift).astype(np.float32)[:, None, :], TILE, axis=1)
    odd = np.concatenate([direct.T, wave(place + width, shift).T], axis=1)[2 * width :]
    fold = np.zeros((around, 4 * half))
    kinds = [4 * np.arange(half), 4 * np.arange(half) + 2, 8 * np.arange(half) + 1, 8 * np.arange(half) + 5]
    for column, k in enumerate(np.concatenate(kinds)):
        for place in {k, (around - k) % around}:
            fold[place, column] = 1.0 / around
    return (
        np.stack([two_parts(t) for t in forward]),
        np.stack([two_parts(t) for t in (direct.T[:width], direct.T[width : 2 * width])]),
        two_parts(odd),
        beyond,
        fold.astype(ml_dtypes.bfloat16),
    )


def split(x):
    high = x.astype(BF16)
    return high, (x - high.astype(F32)).astype(BF16)


def product(high, low, table_ref):
    left = jnp.concatenate([high, low, high], axis=1)
    table = jnp.concatenate([table_ref[0], table_ref[0], table_ref[1]], axis=0)
    return jnp.dot(left, table, preferred_element_type=F32)


def lanes_of(shape):
    return lax.broadcasted_iota(jnp.int32, shape, len(shape) - 1)


def rows_of(shape):
    return lax.broadcasted_iota(jnp.int32, shape, len(shape) - 2)


def beside_sum(x, before, after):
    lane = lanes_of(x.shape)
    size = x.shape[-1]
    left = jnp.where(lane == 0, before, pltpu.roll(x, 1, x.ndim - 1))
    right = jnp.where(lane == size - 1, after, pltpu.roll(x, size - 1, x.ndim - 1))
    return left + right


def stacked_sum(x, before=0.0, after=0.0):
    row = rows_of(x.shape)
    size = x.shape[0]
    up = jnp.where(row == 0, before, pltpu.roll(x, 1, 0))
    down = jnp.where(row == size - 1, after, pltpu.roll(x, size - 1, 0))
    return up + down


def fold_kernel(precond_ref, fold_ref, *refs):
    out_ref, beyond_ref = refs[-2:]
    comps = precond_ref.shape[0]
    value = jnp.concatenate([precond_ref[q] for q in range(comps)], axis=0)
    pairs, around = value.shape
    high = value.astype(BF16)
    rest = value - high.astype(F32)
    middle = rest.astype(BF16)
    low = (rest - middle.astype(F32)).astype(BF16)
    terms = [jnp.dot(t, fold_ref[...], preferred_element_type=F32) for t in (high, middle, low)]
    folded = terms[0] + (terms[1] + terms[2])
    half = folded.shape[1] // 4
    zero = folded[:, :half]
    top = value[:, around // 2 : around // 2 + 1] * F32(1.0 / around)
    other = jnp.where(lanes_of(zero.shape) == 0, top, zero)
    folded = jnp.concatenate([zero, other, folded[:, half:]], axis=1)
    for i in range(pairs):
        out_ref[i] = jnp.broadcast_to(folded[i : i + 1], out_ref.shape[1:])
    rest = [jnp.zeros((TILE - comps, folded.shape[1]), F32)]
    for p in range(comps):
        beyond_ref[p] = jnp.concatenate([folded[i : i + 1] for i in range(p, pairs, comps)] + rest, axis=0)


def factor_columns(table_ref, class_ref, ax_size, comps):
    classes = class_ref[...]
    slab = classes.shape[1]
    position = lax.axis_index("ax") * slab + lanes_of(classes.shape)
    taper = 1.0 + 2.0 * position.astype(F32) / F32(ax_size * slab - 1)
    rows = []
    for q in range(comps):
        value = jnp.zeros(classes.shape, F32)
        for kind in range(table_ref.shape[0]):
            value = jnp.where(classes == kind, table_ref[kind, q], value)
        rows.append(value * taper)
    rows.append(jnp.zeros((LANES - comps, slab), F32))
    return jnp.concatenate(rows, axis=0).T


def local_part(q, block, inner, solid, factor, load, stiff, other):
    field = block[inner]
    beside = stacked_sum(block)[inner] + beside_sum(field, 0.0, 0.0)
    stiffness = stiff * factor[:, q : q + 1]
    image = (stiffness + 4.5) * field - beside - 0.5 * other[inner]
    return solid * (load - image)


def edge_rows(fields, solid):
    rows, width = solid.shape
    sources = fields + [solid] * (TILE - len(fields))
    columns = [x[:, :1] for x in sources] + [x[:, width - 1 :] for x in sources]
    table = jnp.concatenate(columns + [jnp.zeros((rows, LANES - 2 * TILE), F32)], axis=1)
    if rows < LANES:
        table = jnp.concatenate([table, jnp.zeros((LANES - rows, LANES), F32)], axis=0)
    table = table.T
    return table[:TILE], table[TILE : 2 * TILE]


def first_kernel(
    end, comps, ax_size, table_ref, class_ref, load_ref, disp_ref, stiff_ref, hole_ref,
    keep_ref, other_ref, ends_ref, factor_ref, up_ref, down_ref,
    table_in, class_in, load_in, disp_in, stiff_in, hole_in, inner_out, ends_out, factor_out, up_out, down_out,
    in_sems, out_sems,
):
    slab, width = hole_ref.shape
    half = slab // 2
    inner = half - end
    core = lax.axis_index("sec") % 2

    def copy(src, dst, sems, i):
        moving = pltpu.make_async_copy(src, dst, sems.at[i])
        moving.start()
        return moving

    small = [
        copy(class_ref, class_in, in_sems, 0), copy(table_ref, table_in, in_sems, 1), copy(hole_ref, hole_in, in_sems, 2)
    ]
    moving = []
    for q in range(comps):
        pairs = ((disp_ref, disp_in), (load_ref, load_in), (stiff_ref, stiff_in))
        moving.append([copy(src.at[q], dst.at[q], in_sems, 3 + 3 * q + k) for k, (src, dst) in enumerate(pairs)])
    for one in small:
        one.wait()
    factor_out[...] = factor_columns(table_in, class_in, ax_size, comps)
    leaving = [copy(factor_out, factor_ref, out_sems, 0)]
    solid = (1 - hole_in[...]).astype(F32)
    factor = factor_out[...]
    for q in range(comps):
        if q % 2 == 0:
            for one in moving[q] + moving[q + 1]:
                one.wait()
        field = disp_in[q]
        part = local_part(q, field, slice(0, slab), solid, factor, load_in[q], stiff_in[q], disp_in[q ^ 1])
        rows = pl.ds(q * inner, inner)
        inner_out[0, rows, :] = part[end:half]
        inner_out[1, rows, :] = part[half : slab - end]
        leaving.append(copy(inner_out.at[core, rows], keep_ref.at[rows], out_sems, 1 + 2 * q))
        leaving.append(copy(inner_out.at[1 - core, rows], other_ref.at[rows], out_sems, 2 + 2 * q))
        rows = pl.ds(q * end, end)
        ends_out[0, rows, :] = part[:end]
        ends_out[1, rows, :] = part[slab - end :]
        up_out[q : q + 1, :] = part[slab - 1 :]
        down_out[q : q + 1, :] = part[:1]
        up_out[TILE + q : TILE + q + 1, :] = field[slab - 1 :]
        down_out[TILE + q : TILE + q + 1, :] = field[:1]
    spare = TILE - comps
    for ref, row in ((up_out, slab - 1), (down_out, 0)):
        ref[comps:TILE, :] = jnp.broadcast_to(solid[row : row + 1], (spare, width))
        ref[TILE + comps :, :] = jnp.zeros((spare, width), F32)
    count = 1 + 2 * comps
    leaving.append(copy(up_out, up_ref, out_sems, count))
    leaving.append(copy(down_out, down_ref, out_sems, count + 1))

    def ordered(x):
        return jnp.concatenate([x[end:half], x[:end], x[half:]], axis=0)

    edges = edge_rows([ordered(disp_in[q]) for q in range(comps)], ordered(solid))
    last = pl.ds(comps * inner, TILE)
    for h in range(2):
        inner_out[h, last, :] = jnp.concatenate([pltpu.roll(x, (LANES - half * h) % LANES, 1) for x in edges], axis=1)
        ends_out[h, pl.ds(comps * end, 2 * TILE), :] = (down_out, up_out)[h][...]
    leaving.append(copy(inner_out.at[core, last], keep_ref.at[last], out_sems, count + 2))
    leaving.append(copy(inner_out.at[1 - core, last], other_ref.at[last], out_sems, count + 3))
    leaving.append(copy(ends_out, ends_ref, out_sems, count + 4))
    for one in leaving:
        one.wait()


def ends_kernel(comps, ends_ref, before_ref, after_ref, keep_ref, other_ref, out_ref):
    rows = (ends_ref.shape[1] - 2 * TILE) // comps
    width = ends_ref.shape[2]
    row = rows_of((rows, width))
    core = lax.axis_index("sec") % 2
    for h, far_ref, at in ((0, before_ref, 0), (1, after_ref, rows - 1)):
        own_ref = ends_ref.at[h, pl.ds(comps * rows, 2 * TILE)]
        solid_own = own_ref[comps : comps + 1]
        far = far_ref[...]
        for q in range(comps):
            part = ends_ref[h, pl.ds(q * rows, rows), :]
            part = part + jnp.where(row == at, solid_own * far[TILE + q : TILE + q + 1], 0.0)
            out_ref[h, pl.ds(q * rows, rows), :] = part
        solid_far = far[comps : comps + 1]
        residual = far[:TILE] + solid_far * own_ref[TILE:]
        out_ref[h, pl.ds(comps * rows, TILE), :] = jnp.where(rows_of(residual.shape) < comps, residual, solid_far)
        out_ref[h, pl.ds(comps * rows + TILE, TILE), :] = far[TILE:]
    keep_ref[...] = out_ref[core]
    other_ref[...] = out_ref[1 - core]


def in_order(odd, own, core, across, both):
    return own, jnp.where(odd, both, core), across, jnp.where(odd, core, both)


def butterfly(x0, x1, x2, x3):
    even, other = x0 + x2, x1 + x3
    return even + other, even - other, x0 - x2, x1 - x3


def edge_table(odd, blocks):
    tiles = in_order(odd, *blocks)
    left = [t[:, :LANES] for t in tiles]
    right = [t[:, LANES:] for t in tiles]
    solid = TILE - 1
    at_left = [left[s][solid:] * right[s - 1] for s in range(SECTORS)]
    at_right = [right[s][solid:] * left[(s + 1) % SECTORS] for s in range(SECTORS)]
    stack = []
    for one, other in zip(butterfly(*at_left), butterfly(*at_right)):
        stack += [one, other]
    stack += [at_left[0], at_right[0]]
    stack += [jnp.where(odd, at_left[3], at_left[1]), jnp.where(odd, at_right[3], at_right[1])]
    stack += [right[3], left[1], jnp.where(odd, right[2], right[0]), jnp.where(odd, left[0], left[2])]
    return jnp.concatenate(stack, axis=0).T


def transform_kernel(
    comps, main, at_end, edge_at, hole_at, own_ref, core_ref, across_ref, both_ref,
    forward_ref, even_ref, odd_ref, beyond_ref, weight_ref, beyond_weight_ref, hole_ref, edge_ref,
    prec_ref, residual_ref, back_ref, left_ref, spectrum_ref, scaled_ref, halo_ref,
):
    width = own_ref.shape[1]
    half = width // 2
    core = lax.axis_index("sec") % 2
    odd = core == 1
    sign = jnp.where(odd, -1.0, 1.0)
    rows = main
    total = comps * rows
    group = 1 if rows % 16 == 0 else 2
    sources = (own_ref, core_ref, across_ref, both_ref)
    start, stride = hole_at
    solid = (1 - hole_ref[pl.ds(pl.multiple_of(start + stride * core, TILE), main)]).astype(F32)
    if not at_end:
        edge_ref[...] = edge_table(odd, [r[total : total + TILE] for r in sources])
    edge = edge_ref[pl.ds(edge_at, main), :]
    lane = lanes_of((main, LANES))
    first = lane == 0
    last = lane == LANES - 1

    def edge_column(tile, q):
        column = tile * TILE + q
        return edge[:, column : column + 1]

    def with_edges(x, array, q):
        head = x[:, :LANES] + jnp.where(first, edge_column(2 * array, q), 0.0)
        tail = x[:, -LANES:] + jnp.where(last, edge_column(2 * array + 1, q), 0.0)
        middle = [x[:, LANES:-LANES]] if width > 2 * LANES else []
        return jnp.concatenate([head] + middle + [tail], axis=1)

    def arrays_of(q):
        at = q * rows
        own, core, across, both = [r[pl.ds(at, main), :] for r in sources]
        arrays = butterfly(own, core, across, both)
        arrays = arrays[:3] + (sign * arrays[3],)
        arrays = [with_edges(x, i, q) for i, x in enumerate(arrays)]
        residual_ref[q] = with_edges(own, 4, q)
        return turned(*arrays)

    def turned(y0, y2, real, imag):
        turned_real = (real[:, half:] - imag[:, half:]) * F32(np.sqrt(0.5))
        turned_imag = (real[:, half:] + imag[:, half:]) * F32(np.sqrt(0.5))
        plus = jnp.concatenate([real[:, :half] + turned_real, imag[:, :half] + turned_imag], axis=1)
        minus = jnp.concatenate([real[:, :half] - turned_real, imag[:, :half] - turned_imag], axis=1)
        return y0, y2, plus, minus

    def arrays_beyond():
        tiles = in_order(odd, *[r[pl.ds(total, TILE), :] for r in sources])
        disp = in_order(odd, *[r[pl.ds(total + TILE, TILE), :] for r in sources])
        place = lanes_of((TILE, width))
        fixed = []
        for s in range(SECTORS):
            beside = jnp.where(place == 0, pltpu.roll(disp[s - 1], 1, 1), 0.0)
            beside = beside + jnp.where(
                place == width - 1, pltpu.roll(disp[(s + 1) % SECTORS], width - 1, 1), 0.0
            )
            value = tiles[s] + tiles[s][comps : comps + 1] * beside
            fixed.append(jnp.where(rows_of((TILE, width)) < comps, value, 0.0))
        return turned(*butterfly(*fixed))

    def put(at, arrays):
        for i, x in enumerate(arrays):
            high, low = split(x)
            left_ref[at, 2 * i * width : (2 * i + 1) * width] = high
            left_ref[at, (2 * i + 1) * width : (2 * i + 2) * width] = low

    for begin in range(0, comps, group):
        found = [arrays_of(q) for q in range(begin, begin + group)]
        put(pl.ds(begin * rows, group * rows), [jnp.concatenate([x[i] for x in found], axis=0) for i in range(4)])
    if at_end:
        put(pl.ds(total, 2 * TILE), [jnp.concatenate([x, jnp.zeros_like(x)], axis=0) for x in arrays_beyond()])
    height = left_ref.shape[0]

    for i in range(4):
        high = left_ref[:, 2 * i * width : (2 * i + 1) * width]
        low = left_ref[:, (2 * i + 1) * width : (2 * i + 2) * width]
        part = product(high, low, forward_ref.at[i])
        spectrum_ref[:, :, i * width : (i + 1) * width] = part.reshape(height // TILE, TILE, width)

    around = SECTORS * width

    def scale(row, count):
        tiles = count // TILE

        def spectrum(p, lanes):
            return spectrum_ref[pl.ds((p * rows + row) // TILE, tiles), :, lanes]

        for begin in range(0, comps, group):
            halo = [[None, None] for _ in range(group)]
            for k in range(4):
                for h in range(2):
                    lanes = slice(k * width + h * half, k * width + (h + 1) * half)
                    kind = h if k == 0 else k + 1
                    values = []
                    for i in range(group):
                        value = None
                        for p in range(comps):
                            weight = weight_ref[(begin + i) * comps + p, :, kind * half : (kind + 1) * half]
                            term = spectrum(p, lanes) * weight
                            value = term if value is None else value + term
                        for side in range(2):
                            term = value * beyond_ref[2 * core + side, :, lanes]
                            halo[i][side] = term if halo[i][side] is None else halo[i][side] + term
                        values.append(value.reshape(count, half))
                    high, low = split(values[0] if group == 1 else jnp.concatenate(values, axis=0))
                    at = pl.ds(begin * rows + row, group * count)
                    scaled_ref[at, lanes] = high
                    scaled_ref[at, around + lanes.start : around + lanes.stop] = low
            for i in range(group):
                before, after = [jnp.sum(x, axis=2, keepdims=True) for x in halo[i]]
                tile = jnp.where(lanes_of((tiles, TILE, LANES)) == 0, before, after)
                halo_ref[pl.ds((begin + i) * rows + row, count), :] = tile.reshape(count, LANES)

    def scale_beyond():
        at = pl.ds(total, 2 * TILE)
        for k in range(4):
            for h in range(2):
                lanes = slice(k * width + h * half, k * width + (h + 1) * half)
                kind = h if k == 0 else k + 1
                parts = spectrum_ref[total // TILE, :, lanes]
                value = None
                for p in range(comps):
                    term = parts[p : p + 1] * beyond_weight_ref[p, :, kind * half : (kind + 1) * half]
                    value = term if value is None else value + term
                high, low = split(jnp.concatenate([value, jnp.zeros_like(value)], axis=0))
                scaled_ref[at, lanes] = high
                scaled_ref[at, around + lanes.start : around + lanes.stop] = low

    if at_end:
        scale_beyond()
    step = rows if group > 1 else 32
    for row in range(0, rows, step):
        scale(row, min(step, rows - row))

    def inverse(columns, table_ref):
        low = scaled_ref[:, around + columns.start : around + columns.stop]
        return product(scaled_ref[:, columns], low, table_ref)

    zero = inverse(slice(0, width), even_ref.at[0])
    two = inverse(slice(width, 2 * width), even_ref.at[1])
    odds = inverse(slice(2 * width, around), odd_ref)
    own_all = zero + two + odds[:, :width]
    other_all = zero - two + sign * odds[:, width:]
    for q in range(comps):
        at = q * rows
        own, other = own_all[at : at + rows], other_all[at : at + rows]
        side = halo_ref[pl.ds(at, rows), :]
        far_before, far_after = side[:, :1], side[:, 1:2]
        own_before = jnp.where(odd, other[:, width - 1 :], far_before)
        own_after = jnp.where(odd, far_after, other[:, :1])
        other_before = jnp.where(odd, far_before, own[:, width - 1 :])
        other_after = jnp.where(odd, own[:, :1], far_after)
        solids = [edge_column(tile, TILE - 1) for tile in (12, 13, 14, 15)]
        at = pl.ds(at, rows)
        prec_ref[at, :width] = own * solid
        prec_ref[at, width:] = jnp.where(first, own_before * solids[0], own_after * solids[1])
        tile = jnp.where(first, other_before * solids[2], other_after * solids[3])
        tile = jnp.where(lane == 2, edge_column(10, q), jnp.where(lane == 3, edge_column(11, q), tile))
        back_ref[at, :width] = other
        back_ref[at, width:] = tile
    if at_end:
        at = pl.ds(total, TILE)
        for ref, result, source in ((prec_ref, own_all, own_ref), (back_ref, other_all, core_ref)):
            ref[at, :width] = result[total : total + TILE] * source[pl.ds(total + comps, 1), :]
            ref[at, width:] = jnp.zeros((TILE, LANES), F32)


def image_rows(q, fields, tile, stiff, solid, factor, before, after, inner):
    field = fields[q][inner]
    beside = beside_sum(field, tile[:, :1], tile[:, 1:2])
    beside = beside + stacked_sum(fields[q], before, after)[inner]
    stiffness = stiff * factor[:, q : q + 1]
    return field, solid * ((stiffness + 4.5) * field - beside - 0.5 * fields[q ^ 1][inner])


def add_sums(sums, residual, field, image):
    rows, width = field.shape
    pairs = ((residual, field), (field, image), (residual, residual), (residual, image), (image, image))
    return [
        total + jnp.sum((x * y).reshape(rows // TILE, TILE, width), axis=0)
        for total, (x, y) in zip(sums, pairs)
    ]


def returned(back, sent, solid, q, rows):
    width = sent.shape[1]
    side = back[pl.ds(q * rows, rows), width:]
    residual = sent[pl.ds(q * rows, rows), :]
    lane = lanes_of(residual.shape)
    residual = residual + jnp.where(lane == 0, side[:, 2:3], 0.0) + jnp.where(lane == width - 1, side[:, 3:4], 0.0)
    return back[pl.ds(q * rows, rows), :width] * solid, side, residual


def early_kernel(
    end, comps, stiff_ref, hole_ref, factor_ref, own_ref, back_ref, residual_ref, sent_ref,
    prec_out, residual_out, image_ref, sums_ref,
):
    slab, width = hole_ref.shape
    inner = slab // 2 - end
    core = lax.axis_index("sec") % 2
    here = pl.ds(pl.multiple_of(inner * core, TILE), inner)
    there = pl.ds(pl.multiple_of(inner * (1 - core), TILE), inner)
    solid_there = (1 - hole_ref[pl.ds(pl.multiple_of(end + inner * (1 - core), TILE), inner)]).astype(F32)
    for q in range(comps):
        prec, side, residual = returned(back_ref, sent_ref, solid_there, q, inner)
        prec_out[q, here] = own_ref[pl.ds(q * inner, inner), :]
        prec_out[q, there, :width] = prec
        prec_out[q, there, width:] = side
        residual_out[q, here] = residual_ref[q]
        residual_out[q, there] = residual
    low, high = end + TILE, slab - end - TILE
    core_rows = slice(TILE, 2 * inner - TILE)
    solid = (1 - hole_ref[low:high]).astype(F32)
    factor = factor_ref[low:high]
    sums = [jnp.zeros((TILE, width), F32) for _ in range(5)]
    for q in range(comps):
        fields = {k: prec_out[k, :, :width] for k in (q, q ^ 1)}
        field, image = image_rows(
            q, fields, prec_out[q, core_rows, width:], stiff_ref[q, low:high], solid, factor, 0.0, 0.0, core_rows
        )
        image_ref[q] = image
        sums = add_sums(sums, residual_out[q, core_rows], field, image)
    for i, total in enumerate(sums):
        sums_ref[pl.ds(i * TILE, TILE), :] = total


def late_kernel(
    end, comps, stiff_ref, hole_ref, factor_ref, inner_ref, inner_residual_ref,
    own_ref, back_ref, residual_ref, sent_ref, partial_ref,
    prec_out, residual_out, image_ref, sums_ref,
):
    slab, width = hole_ref.shape
    reach = end + TILE
    core = lax.axis_index("sec") % 2
    odd = core == 1
    solid = (1 - hole_ref[...]).astype(F32)
    factor = factor_ref[...]
    sums = [partial_ref[pl.ds(i * TILE, TILE), :] for i in range(5)]
    fields, tiles, beyond, residuals = [[], []], [[], []], [[], []], [[], []]
    for q in range(comps):
        solid_there = jnp.where(odd, solid[:end], solid[slab - end :])
        there, side, residual = returned(back_ref, sent_ref, solid_there, q, end)
        rows, far = pl.ds(q * end, end), pl.ds(comps * end + q, 1)
        here, own_side = own_ref[rows, :width], own_ref[rows, width:]
        far_here, far_there = own_ref[far, :width], back_ref[far, :width]
        for h, swap in ((0, odd), (1, core == 0)):
            prec = jnp.where(swap, there, here)
            tile = jnp.where(swap, side, own_side)
            rest = jnp.where(swap, residual, residual_ref[q])
            beyond[h].append(jnp.where(swap, far_there, far_here))
            rows = pl.ds(end * h, end)
            prec_out[q, rows] = prec
            residual_out[q, rows] = rest
            near = slice(0, 2 * TILE) if h == 0 else slice(-2 * TILE, None)
            close = slice(0, TILE) if h == 0 else slice(-TILE, None)
            parts = [prec, inner_ref[q, near, :width]]
            sides = [tile, inner_ref[q, close, width:]]
            rests = [rest, inner_residual_ref[q, close]]
            order = slice(None) if h == 0 else slice(None, None, -1)
            fields[h].append(jnp.concatenate(parts[order], axis=0))
            tiles[h].append(jnp.concatenate(sides[order], axis=0))
            residuals[h].append(jnp.concatenate(rests[order], axis=0))
    for h in range(2):
        rows = slice(0, reach) if h == 0 else slice(slab - reach, slab)
        inner = slice(0, reach) if h == 0 else slice(TILE, None)
        for q in range(comps):
            before, after = (beyond[0][q], 0.0) if h == 0 else (0.0, beyond[1][q])
            field, image = image_rows(
                q, fields[h], tiles[h][q], stiff_ref[q, rows], solid[rows], factor[rows], before, after, inner
            )
            image_ref[q, pl.ds(reach * h, reach)] = image
            sums = add_sums(sums, residuals[h][q], field, image)
    row = jnp.zeros((1, LANES), F32)
    spot = lanes_of((1, LANES))
    for i, value in enumerate(sums):
        value = jnp.sum(jnp.sum(value, axis=0, keepdims=True), axis=1, keepdims=True)
        row = jnp.where(spot == i, value, row)
    sums_ref[...] = jnp.broadcast_to(row, sums_ref.shape)


def update_kernel(
    end, comps, cell_total, disp_ref, gathered_ref, inner_ref, inner_residual_ref, inner_image_ref,
    ends_ref, ends_residual_ref, ends_image_ref, disp_out, residual_out, stats_out,
):
    slab, width = disp_ref.shape[1:]
    values = jnp.sum(gathered_ref[...], axis=0, keepdims=True) * F32(1.0 / cell_total)
    rz, zq, rr, ri, ii = [values[:, i : i + 1] for i in range(5)]
    alpha = rz / zq
    square = rr + alpha * (alpha * ii - 2.0 * ri)
    stats_out[...] = jnp.concatenate([rz, zq, square], axis=1)
    reach = end + TILE
    inner = slice(end, slab - end)
    for q in range(comps):
        disp_out[q, :end] = disp_ref[q, :end] + alpha * ends_ref[q, :end]
        disp_out[q, inner] = disp_ref[q, inner] + alpha * inner_ref[q, :, :width]
        disp_out[q, slab - end :] = disp_ref[q, slab - end :] + alpha * ends_ref[q, end:]
        image = jnp.concatenate([ends_image_ref[q, :reach], inner_image_ref[q], ends_image_ref[q, reach:]], axis=0)
        residual_out[q, :end] = ends_residual_ref[q, :end] - alpha * image[:end]
        residual_out[q, inner] = inner_residual_ref[q] - alpha * image[inner]
        residual_out[q, slab - end :] = ends_residual_ref[q, end:] - alpha * image[slab - end :]


VMEM = pl.BlockSpec(memory_space=pltpu.VMEM)
SMEM = pl.BlockSpec(memory_space=pltpu.SMEM)
HBM = pl.BlockSpec(memory_space=pltpu.HBM)
FULL = 62


def call(kernel, name, out_shapes, in_specs, flops, moved, scratch=(), grant=32, out_spec=None):
    return pl.pallas_call(
        kernel,
        out_shape=[jax.ShapeDtypeStruct(s, F32) for s in out_shapes],
        in_specs=in_specs,
        out_specs=[out_spec or VMEM] * len(out_shapes),
        scratch_shapes=list(scratch),
        compiler_params=pltpu.CompilerParams(vmem_limit_bytes=grant * 1024 * 1024),
        cost_estimate=pl.CostEstimate(flops=flops, bytes_accessed=moved, transcendentals=0),
        name=name,
    )


def transform_call(blocks, tables, hole, edge, main, edge_at, hole_at, comps, width, slab, weight):
    around = SECTORS * width
    at_end = edge is not None
    total = comps * main
    out_rows = total + (TILE if at_end else 0)
    rows = total + (2 * TILE if at_end else 0)
    operands = list(blocks) + list(tables) + [hole] + ([edge] if at_end else [])
    shapes = [(out_rows, width + LANES), (comps, main, width), (out_rows, width + LANES)]
    return call(
        functools.partial(transform_kernel, comps, main, at_end, edge_at, hole_at), "transform",
        ([] if at_end else [(slab, LANES)]) + shapes, [VMEM] * len(operands),
        weight * 2 * total * 3 * around * 3 * width, weight * 4 * total * width * 8,
        [pltpu.VMEM((rows, 8 * width), BF16), pltpu.VMEM((rows // TILE, TILE, around), F32),
         pltpu.VMEM((rows, 2 * around), BF16), pltpu.VMEM((total, LANES), F32)],
    )(*operands)


def after_all(x, *others):
    return lax.optimization_barrier((x, *others))[0]


def shards(load, disp, stiff, hole, section_class, class_table, precond):
    slab, comps, width = disp.shape
    ax, sec = lax.axis_size("ax"), lax.axis_size("sec")
    around = width * sec
    cell_total = slab * ax * comps * around
    end = slab // 16 * 2
    inner = slab // 2 - end
    load, disp, stiff = [x.transpose(1, 0, 2) for x in (load, disp, stiff)]
    forward, even, odd, beyond, fold = harmonic_tables(width)
    block = 4 * comps * slab * width
    classes = section_class.reshape(1, slab)

    sent = (comps * inner + TILE, width)
    ends_shape = (2, comps * end + 2 * TILE, width)
    shapes = [sent, sent, ends_shape, (slab, LANES), (2 * TILE, width), (2 * TILE, width)]
    keep, other, edge, factor, up, down = call(
        functools.partial(first_kernel, end, comps, ax), "first",
        shapes, [HBM] * 6, 10 * comps * slab * width, 2 * block,
        [pltpu.SMEM(class_table.shape, F32), pltpu.VMEM((1, slab), jnp.int32)]
        + [pltpu.VMEM((comps, slab, width), F32)] * 3 + [pltpu.VMEM((slab, width), jnp.int32)]
        + [pltpu.VMEM((2,) + sent, F32)] + [pltpu.VMEM(shape, F32) for shape in shapes[2:]]
        + [pltpu.SemaphoreType.DMA((3 + 3 * comps,)), pltpu.SemaphoreType.DMA((6 + 2 * comps,))],
        FULL, HBM,
    )(class_table, classes, load, disp, stiff, hole)

    def to(x, mask):
        return lax.ppermute(x, "sec", [(i, i ^ mask) for i in range(sec)])

    def gather(keep, other):
        return keep, to(other, 1), to(keep, 2), to(other, 3)

    blocks = gather(keep, other)
    before = lax.ppermute(up, "ax", [(i, i + 1) for i in range(ax - 1)])
    after = lax.ppermute(down, "ax", [(i + 1, i) for i in range(ax - 1)])
    weight, beyond_weight = call(
        fold_kernel, "fold", [(comps * comps, TILE, 5 * width // 2), (comps, TILE, 5 * width // 2)], [VMEM] * 6,
        1, 1,
    )(precond, fold, forward, even, odd, beyond)
    rows = (comps * end + 2 * TILE, width)
    keep_ends, other_ends = call(
        functools.partial(ends_kernel, comps), "ends",
        [rows, rows], [VMEM] * 3, 2 * comps * end * width, 16 * comps * end * width, [pltpu.VMEM((2,) + rows, F32)],
    )(after_all(edge, weight), before, after)
    end_blocks = gather(keep_ends, other_ends)
    tables = (forward, even, odd, beyond, weight, beyond_weight)

    across = after_all(blocks[2], keep_ends, weight)
    edge, own, residual, back = transform_call(
        (keep, blocks[1], across, blocks[3]), tables, hole, None, inner, 0, (end, inner), comps, width, slab, 0
    )
    back = to(back, 1)
    across = after_all(end_blocks[2], own)
    own_ends, residual_ends, back_ends = transform_call(
        (keep_ends, end_blocks[1], across, end_blocks[3]), tables, hole, edge, end, inner, (0, slab - end),
        comps, width, slab, 100,
    )
    back_ends = to(back_ends, 1)
    prec, residual, image, partial = call(
        functools.partial(early_kernel, end, comps), "early",
        [(comps, 2 * inner, width + LANES), (comps, 2 * inner, width), (comps, 2 * (inner - TILE), width), (5 * TILE, width)],
        [VMEM] * 7, 30 * comps * slab * width, 4 * block,
    )(stiff, hole, after_all(factor, own_ends), own, back, residual, other)
    prec_ends, residual_ends, image_ends, sums = call(
        functools.partial(late_kernel, end, comps), "late",
        [(comps, 2 * end, width), (comps, 2 * end, width), (comps, 2 * (end + TILE), width), (ax * sec, LANES)],
        [VMEM] * 10, 8 * comps * slab * width, block,
    )(stiff, hole, factor, prec, residual, own_ends, back_ends, residual_ends, other_ends, partial)
    gathered = lax.all_to_all(sums, ("ax", "sec"), 0, 0, tiled=True)
    disp_new, residual_new, stats = call(
        functools.partial(update_kernel, end, comps, cell_total), "update",
        [(comps, slab, width), (comps, slab, width), (1, 3)], [VMEM] * 8,
        4 * comps * slab * width, 6 * block,
    )(disp, gathered, prec, residual, image, prec_ends, residual_ends, image_ends)
    return disp_new.transpose(1, 0, 2), residual_new.transpose(1, 0, 2), stats.reshape(3)


def solution(mesh):
    in_specs = (
        P("ax", None, "sec"),
        P("ax", None, "sec"),
        P("ax", None, "sec"),
        P("ax", "sec"),
        P("ax"),
        P(),
        P(),
    )
    out_specs = (P("ax", None, "sec"), P("ax", None, "sec"), P())
    return jax.shard_map(shards, mesh=mesh, in_specs=in_specs, out_specs=out_specs, check_vma=False)
```

```python
import functools

import jax
import jax.numpy as jnp
import ml_dtypes
import numpy as np
from jax import lax
from jax.experimental import pallas as pl
from jax.experimental.pallas import tpu as pltpu
from jax.sharding import PartitionSpec as P

F32 = jnp.float32
BF16 = jnp.bfloat16
SECTORS = 4
TILE = 8
LANES = 128


def two_parts(table):
    high = table.astype(ml_dtypes.bfloat16)
    low = (table - high.astype(np.float64)).astype(ml_dtypes.bfloat16)
    return np.stack([high, low])


@functools.lru_cache(maxsize=None)
def harmonic_tables(width):
    around = SECTORS * width
    half = width // 2
    zero = [("c", 4 * q) for q in range(half + 1)] + [("s", 4 * q) for q in range(1, half)]
    two = [(f, 4 * q + 2) for f in "cs" for q in range(half)]
    one = [(f, 8 * q + 1) for f in "cs" for q in range(half)]
    five = [(f, 8 * q + 5) for f in "cs" for q in range(half)]
    columns = zero + two + one + five
    harmonic = np.array([k for _, k in columns], dtype=np.int64)
    is_sin = np.array([f == "s" for f, _ in columns])

    def wave(place, shift):
        angle = 2.0 * np.pi / around * ((place[:, None] * harmonic[None, :]) % around)
        return np.cos(angle - shift)

    place = np.arange(width)
    shift = np.where(is_sin, np.pi / 2, 0.0)[None, :]
    direct = wave(place, shift)
    turned = np.concatenate([direct[:half], wave(place[:half], shift - np.pi / 2)], axis=0)
    forward = [direct[:, :width], direct[:, width : 2 * width]]
    forward += [turned[:, 2 * width : 3 * width], turned[:, 3 * width :]]
    ends = np.array([around - 1, 2 * width, around - width - 1, width])
    beyond = np.repeat(wave(ends, shift).astype(np.float32)[:, None, :], TILE, axis=1)
    odd = np.concatenate([direct.T, wave(place + width, shift).T], axis=1)[2 * width :]
    return (
        np.stack([two_parts(t) for t in forward]),
        np.stack([two_parts(t) for t in (direct.T[:width], direct.T[width : 2 * width])]),
        two_parts(odd),
        beyond,
    )


def split(x):
    high = x.astype(BF16)
    return high, (x - high.astype(F32)).astype(BF16)


def product(high, low, table_ref):
    left = jnp.concatenate([high, low, high], axis=1)
    table = jnp.concatenate([table_ref[0], table_ref[0], table_ref[1]], axis=0)
    return jnp.dot(left, table, preferred_element_type=F32)


def lanes_of(shape):
    return lax.broadcasted_iota(jnp.int32, shape, len(shape) - 1)


def rows_of(shape):
    return lax.broadcasted_iota(jnp.int32, shape, len(shape) - 2)


def beside_sum(x, before, after):
    lane = lanes_of(x.shape)
    size = x.shape[-1]
    left = jnp.where(lane == 0, before, pltpu.roll(x, 1, x.ndim - 1))
    right = jnp.where(lane == size - 1, after, pltpu.roll(x, size - 1, x.ndim - 1))
    return left + right


def stacked_sum(x, before=0.0, after=0.0):
    row = rows_of(x.shape)
    size = x.shape[0]
    up = jnp.where(row == 0, before, pltpu.roll(x, 1, 0))
    down = jnp.where(row == size - 1, after, pltpu.roll(x, size - 1, 0))
    return up + down


def fold_kernel(precond_ref, *refs):
    out_ref, beyond_ref = refs[-2:]
    comps = precond_ref.shape[0]
    value = jnp.concatenate([precond_ref[q] for q in range(comps)], axis=0)
    pairs, around = value.shape
    high = value.astype(BF16)
    rest = value - high.astype(F32)
    middle = rest.astype(BF16)
    low = (rest - middle.astype(F32)).astype(BF16)
    half = around // 8
    row, step = rows_of((around, half)), lanes_of((around, half))
    kinds = []
    for k in (4 * step, 4 * step + 2, 8 * step + 1, 8 * step + 5):
        kinds.append(jnp.where((row == k) | (row == around - k), F32(1.0 / around), 0.0).astype(BF16))
    fold = jnp.concatenate(kinds, axis=1)
    terms = [jnp.dot(t, fold, preferred_element_type=F32) for t in (high, middle, low)]
    folded = terms[0] + (terms[1] + terms[2])
    zero = folded[:, :half]
    top = value[:, around // 2 : around // 2 + 1] * F32(1.0 / around)
    other = jnp.where(lanes_of(zero.shape) == 0, top, zero)
    folded = jnp.concatenate([zero, other, folded[:, half:]], axis=1)
    for i in range(pairs):
        out_ref[i] = jnp.broadcast_to(folded[i : i + 1], out_ref.shape[1:])
    rest = [jnp.zeros((TILE - comps, folded.shape[1]), F32)]
    for p in range(comps):
        beyond_ref[p] = jnp.concatenate([folded[i : i + 1] for i in range(p, pairs, comps)] + rest, axis=0)


def factor_columns(table_ref, class_ref, ax_size, comps):
    classes = class_ref[...]
    slab = classes.shape[1]
    position = lax.axis_index("ax") * slab + lanes_of(classes.shape)
    taper = 1.0 + 2.0 * position.astype(F32) / F32(ax_size * slab - 1)
    rows = []
    for q in range(comps):
        value = jnp.zeros(classes.shape, F32)
        for kind in range(table_ref.shape[0]):
            value = jnp.where(classes == kind, table_ref[kind, q], value)
        rows.append(value * taper)
    rows.append(jnp.zeros((LANES - comps, slab), F32))
    return jnp.concatenate(rows, axis=0).T


def local_part(q, block, inner, solid, factor, load, stiff, other):
    field = block[inner]
    beside = stacked_sum(block)[inner] + beside_sum(field, 0.0, 0.0)
    stiffness = stiff * factor[:, q : q + 1]
    image = (stiffness + 4.5) * field - beside - 0.5 * other[inner]
    return solid * (load - image)


def edge_rows(fields, solid):
    rows, width = solid.shape
    sources = fields + [solid] * (TILE - len(fields))
    columns = [x[:, :1] for x in sources] + [x[:, width - 1 :] for x in sources]
    table = jnp.concatenate(columns + [jnp.zeros((rows, LANES - 2 * TILE), F32)], axis=1)
    if rows < LANES:
        table = jnp.concatenate([table, jnp.zeros((LANES - rows, LANES), F32)], axis=0)
    table = table.T
    return table[:TILE], table[TILE : 2 * TILE]


def copy(src, dst, sem):
    moving = pltpu.make_async_copy(src, dst, sem)
    moving.start()
    return moving


def first_kernel(
    end, comps, ax_size, table_ref, class_ref, load_ref, disp_ref, stiff_ref, hole_ref, keep_ref,
    table_in, class_in, load_in, disp_in, stiff_in, hole_in, keep_out, factor_in, in_sems, out_sems,
):
    slab, width = hole_ref.shape
    half = slab // 2
    inner, reach = half - end, half + TILE
    core = lax.axis_index("sec") % 2
    base = pl.multiple_of((half - TILE) * core, TILE)
    start = pl.multiple_of(end + inner * core, TILE)
    here = pl.ds(pl.multiple_of(end - (end - TILE) * core, TILE), inner)
    around = pl.ds(pl.multiple_of(end - TILE - (end - TILE) * core, TILE), inner + 2 * TILE)
    tail = pl.ds(pl.multiple_of((reach - end) * core, TILE), end)
    small = [
        copy(class_ref, class_in, in_sems.at[0]),
        copy(table_ref, table_in, in_sems.at[1]),
        copy(hole_ref.at[pl.ds(base, reach)], hole_in, in_sems.at[2]),
    ]
    pairs = comps // 2
    moving = []
    for g in range(pairs):
        both = pl.ds(2 * g, 2)
        arrays = (
            (disp_ref.at[both, pl.ds(base, reach)], disp_in), (load_ref.at[both, pl.ds(start, inner)], load_in),
            (stiff_ref.at[both, pl.ds(start, inner)], stiff_in),
        )
        moving.append([copy(src, dst.at[both], in_sems.at[3 + 3 * g + k]) for k, (src, dst) in enumerate(arrays)])
    for one in small:
        one.wait()
    factor_in[...] = factor_columns(table_in, class_in, ax_size, comps)
    factor = factor_in[pl.ds(start, inner), :]
    solid = (1 - hole_in[here, :]).astype(F32)
    solid_tail = (1 - hole_in[tail, :]).astype(F32)
    inside = slice(TILE, TILE + inner)
    leaving = []
    for g in range(pairs):
        moving[g][0].wait()
        if g == pairs - 1:
            fields = [jnp.concatenate([disp_in[q, here], disp_in[q, tail]], axis=0) for q in range(comps)]
            last = pl.ds(comps * inner, TILE)
            keep_out[last, :] = jnp.concatenate(
                edge_rows(fields, jnp.concatenate([solid, solid_tail], axis=0)), axis=1
            )
            leaving.append(copy(keep_out.at[last], keep_ref.at[last], out_sems.at[pairs]))
        moving[g][1].wait()
        moving[g][2].wait()
        for q in (2 * g, 2 * g + 1):
            keep_out[pl.ds(q * inner, inner), :] = local_part(
                q, disp_in[q, around], inside, solid, factor, load_in[q], stiff_in[q], disp_in[q ^ 1, around]
            )
        rows = pl.ds(2 * g * inner, 2 * inner)
        leaving.append(copy(keep_out.at[rows], keep_ref.at[rows], out_sems.at[g]))
    for one in leaving:
        one.wait()


def second_kernel(
    end, comps, ax_size, table_ref, class_ref, load_ref, disp_ref, stiff_ref, hole_ref,
    other_ref, ends_ref, factor_ref, near_ref, next_ref,
    table_in, class_in, load_in, disp_in, stiff_in, hole_in, inner_out, ends_out, factor_out, message_out,
    in_sems, out_sems,
):
    slab, width = hole_ref.shape
    half = slab // 2
    inner = half - end
    core = lax.axis_index("sec") % 2

    small = [
        copy(class_ref, class_in, in_sems.at[0]), copy(table_ref, table_in, in_sems.at[1]), copy(hole_ref, hole_in, in_sems.at[2])
    ]
    pairs = comps // 2
    moving = []
    for g in range(pairs):
        both = pl.ds(2 * g, 2)
        arrays = ((disp_ref, disp_in), (load_ref, load_in), (stiff_ref, stiff_in))
        moving.append([copy(src.at[both], dst.at[both], in_sems.at[3 + 3 * g + k]) for k, (src, dst) in enumerate(arrays)])
    for one in small:
        one.wait()
    factor_out[...] = factor_columns(table_in, class_in, ax_size, comps)
    leaving = [copy(factor_out, factor_ref, out_sems.at[0])]
    solid = (1 - hole_in[...]).astype(F32)
    spare = TILE - comps
    for h, row in ((0, 0), (1, slab - 1)):
        message_out[h, comps:TILE, :] = jnp.broadcast_to(solid[row : row + 1], (spare, width))
        message_out[h, TILE + comps :, :] = jnp.zeros((spare, width), F32)
    factor = factor_out[...]

    def ordered(x):
        return jnp.concatenate([x[end:half], x[:end], x[half:]], axis=0)

    for g in range(pairs):
        moving[g][0].wait()
        if g == pairs - 1:
            edges = edge_rows([ordered(disp_in[q]) for q in range(comps)], ordered(solid))
            last = pl.ds(comps * inner, TILE)
            for h in range(2):
                inner_out[h, last, :] = jnp.concatenate(
                    [pltpu.roll(x, (LANES - half * h) % LANES, 1) for x in edges], axis=1
                )
            leaving.append(copy(inner_out.at[1 - core, last], other_ref.at[last], out_sems.at[2]))
        moving[g][1].wait()
        moving[g][2].wait()
        for q in (2 * g, 2 * g + 1):
            field = disp_in[q]
            part = local_part(q, field, slice(0, slab), solid, factor, load_in[q], stiff_in[q], disp_in[q ^ 1])
            rows = pl.ds(q * inner, inner)
            inner_out[0, rows, :] = part[end:half]
            inner_out[1, rows, :] = part[half : slab - end]
            rows = pl.ds(q * end, end)
            ends_out[0, rows, :] = part[:end]
            ends_out[1, rows, :] = part[slab - end :]
            for h, row in ((0, slice(0, 1)), (1, slice(slab - 1, slab))):
                message_out[h, q : q + 1, :] = part[row]
                message_out[h, TILE + q : TILE + q + 1, :] = field[row]
        rows = pl.ds(2 * g * inner, 2 * inner)
        leaving.append(copy(inner_out.at[1 - core, rows], other_ref.at[rows], out_sems.at[4 + 2 * g]))
    count = 3 + 2 * pairs
    side = lax.axis_index("ax") % 2
    leaving.append(copy(message_out.at[1 - side], near_ref, out_sems.at[count]))
    leaving.append(copy(message_out.at[side], next_ref, out_sems.at[count + 1]))
    for h in range(2):
        ends_out[h, pl.ds(comps * end, 2 * TILE), :] = message_out[h]
    leaving.append(copy(ends_out, ends_ref, out_sems.at[count + 2]))
    for one in leaving:
        one.wait()


def ends_kernel(comps, ends_ref, near_ref, next_ref, keep_ref, other_ref, out_ref):
    rows = (ends_ref.shape[1] - 2 * TILE) // comps
    width = ends_ref.shape[2]
    row = rows_of((rows, width))
    spot, place = rows_of((TILE, width)), lanes_of((TILE, width))
    core = lax.axis_index("sec") % 2
    odd = lax.axis_index("ax") % 2 == 1
    near, other = near_ref[...], next_ref[...]
    for h, far, at in ((0, jnp.where(odd, near, other), 0), (1, jnp.where(odd, other, near), rows - 1)):
        own_ref = ends_ref.at[h, pl.ds(comps * rows, 2 * TILE)]
        solid_own = own_ref[comps : comps + 1]
        for q in range(comps):
            part = ends_ref[h, pl.ds(q * rows, rows), :]
            part = part + jnp.where(row == at, solid_own * far[TILE + q : TILE + q + 1], 0.0)
            out_ref[h, pl.ds(q * rows, rows), :] = part
        solid_far, disp_far = far[comps : comps + 1], far[TILE:]
        edges = jnp.where(place == spot, disp_far[:, :1], 0.0)
        edges = edges + jnp.where(place == spot + TILE, disp_far[:, width - 1 :], 0.0)
        edges = jnp.sum(edges, axis=0, keepdims=True)
        beyond = far[:TILE] + solid_far * own_ref[TILE:]
        beyond = jnp.where(spot < comps, beyond, jnp.where(spot == TILE - 1, edges, solid_far))
        out_ref[h, pl.ds(comps * rows, TILE), :] = beyond
    keep_ref[...] = out_ref[core]
    other_ref[...] = out_ref[1 - core]


def in_order(odd, own, core, across, both):
    return own, jnp.where(odd, both, core), across, jnp.where(odd, core, both)


def butterfly(x0, x1, x2, x3):
    even, other = x0 + x2, x1 + x3
    return even + other, even - other, x0 - x2, x1 - x3


def edge_table(odd, blocks):
    tiles = in_order(odd, *blocks)
    left = [t[:, :LANES] for t in tiles]
    right = [t[:, LANES:] for t in tiles]
    solid = TILE - 1
    at_left = [left[s][solid:] * right[s - 1] for s in range(SECTORS)]
    at_right = [right[s][solid:] * left[(s + 1) % SECTORS] for s in range(SECTORS)]
    stack = []
    for one, other in zip(butterfly(*at_left), butterfly(*at_right)):
        stack += [one, other]
    stack += [at_left[0], at_right[0]]
    stack += [jnp.where(odd, at_left[3], at_left[1]), jnp.where(odd, at_right[3], at_right[1])]
    stack += [right[3], left[1], jnp.where(odd, right[2], right[0]), jnp.where(odd, left[0], left[2])]
    return jnp.concatenate(stack, axis=0).T


def transform_kernel(
    comps, main, at_end, edge_at, hole_at, own_ref, core_ref, across_ref, both_ref,
    forward_ref, even_ref, odd_ref, beyond_ref, weight_ref, beyond_weight_ref, hole_ref, edge_ref,
    prec_ref, residual_ref, back_ref, left_ref, spectrum_ref, scaled_ref, halo_ref,
):
    width = own_ref.shape[1]
    half = width // 2
    core = lax.axis_index("sec") % 2
    odd = core == 1
    sign = jnp.where(odd, -1.0, 1.0)
    rows = main
    total = comps * rows
    group = 1 if rows % 16 == 0 else 2
    sources = (own_ref, core_ref, across_ref, both_ref)
    start, stride = hole_at
    solid = (1 - hole_ref[pl.ds(pl.multiple_of(start + stride * core, TILE), main)]).astype(F32)
    if not at_end:
        edge_ref[...] = edge_table(odd, [r[total : total + TILE] for r in sources])
    edge = edge_ref[pl.ds(edge_at, main), :]
    lane = lanes_of((main, LANES))
    first = lane == 0
    last = lane == LANES - 1

    def edge_column(tile, q):
        column = tile * TILE + q
        return edge[:, column : column + 1]

    def with_edges(x, array, q):
        head = x[:, :LANES] + jnp.where(first, edge_column(2 * array, q), 0.0)
        tail = x[:, -LANES:] + jnp.where(last, edge_column(2 * array + 1, q), 0.0)
        middle = [x[:, LANES:-LANES]] if width > 2 * LANES else []
        return jnp.concatenate([head] + middle + [tail], axis=1)

    def arrays_of(q):
        at = q * rows
        own, core, across, both = [r[pl.ds(at, main), :] for r in sources]
        arrays = butterfly(own, core, across, both)
        arrays = arrays[:3] + (sign * arrays[3],)
        arrays = [with_edges(x, i, q) for i, x in enumerate(arrays)]
        residual_ref[q] = with_edges(own, 4, q)
        return turned(*arrays)

    def turned(y0, y2, real, imag):
        turned_real = (real[:, half:] - imag[:, half:]) * F32(np.sqrt(0.5))
        turned_imag = (real[:, half:] + imag[:, half:]) * F32(np.sqrt(0.5))
        plus = jnp.concatenate([real[:, :half] + turned_real, imag[:, :half] + turned_imag], axis=1)
        minus = jnp.concatenate([real[:, :half] - turned_real, imag[:, :half] - turned_imag], axis=1)
        return y0, y2, plus, minus

    def arrays_beyond():
        tiles = in_order(odd, *[r[pl.ds(total, TILE), :] for r in sources])
        spot, place = rows_of((TILE, width)), lanes_of((TILE, width))

        def column(tile, at):
            return jnp.sum(jnp.where(place == spot + at, tile[TILE - 1 :], 0.0), axis=1, keepdims=True)

        fixed = []
        for s in range(SECTORS):
            beside = jnp.where(place == 0, column(tiles[s - 1], TILE), 0.0)
            beside = beside + jnp.where(place == width - 1, column(tiles[(s + 1) % SECTORS], 0), 0.0)
            value = tiles[s] + tiles[s][comps : comps + 1] * beside
            fixed.append(jnp.where(spot < comps, value, 0.0))
        return turned(*butterfly(*fixed))

    def put(at, arrays):
        for i, x in enumerate(arrays):
            high, low = split(x)
            left_ref[at, 2 * i * width : (2 * i + 1) * width] = high
            left_ref[at, (2 * i + 1) * width : (2 * i + 2) * width] = low

    for begin in range(0, comps, group):
        found = [arrays_of(q) for q in range(begin, begin + group)]
        put(pl.ds(begin * rows, group * rows), [jnp.concatenate([x[i] for x in found], axis=0) for i in range(4)])
    if at_end:
        put(pl.ds(total, 2 * TILE), [jnp.concatenate([x, jnp.zeros_like(x)], axis=0) for x in arrays_beyond()])
    height = left_ref.shape[0]

    for i in range(4):
        high = left_ref[:, 2 * i * width : (2 * i + 1) * width]
        low = left_ref[:, (2 * i + 1) * width : (2 * i + 2) * width]
        part = product(high, low, forward_ref.at[i])
        spectrum_ref[:, :, i * width : (i + 1) * width] = part.reshape(height // TILE, TILE, width)

    around = SECTORS * width

    def scale(row, count):
        tiles = count // TILE

        def spectrum(p, lanes):
            return spectrum_ref[pl.ds((p * rows + row) // TILE, tiles), :, lanes]

        for begin in range(0, comps, group):
            halo = [[None, None] for _ in range(group)]
            for k in range(4):
                for h in range(2):
                    lanes = slice(k * width + h * half, k * width + (h + 1) * half)
                    kind = h if k == 0 else k + 1
                    values = []
                    for i in range(group):
                        value = None
                        for p in range(comps):
                            weight = weight_ref[(begin + i) * comps + p, :, kind * half : (kind + 1) * half]
                            term = spectrum(p, lanes) * weight
                            value = term if value is None else value + term
                        for side in range(2):
                            term = value * beyond_ref[2 * core + side, :, lanes]
                            halo[i][side] = term if halo[i][side] is None else halo[i][side] + term
                        values.append(value.reshape(count, half))
                    high, low = split(values[0] if group == 1 else jnp.concatenate(values, axis=0))
                    at = pl.ds(begin * rows + row, group * count)
                    scaled_ref[at, lanes] = high
                    scaled_ref[at, around + lanes.start : around + lanes.stop] = low
            for i in range(group):
                before, after = [jnp.sum(x, axis=2, keepdims=True) for x in halo[i]]
                tile = jnp.where(lanes_of((tiles, TILE, LANES)) == 0, before, after)
                halo_ref[pl.ds((begin + i) * rows + row, count), :] = tile.reshape(count, LANES)

    def scale_beyond():
        at = pl.ds(total, 2 * TILE)
        for k in range(4):
            for h in range(2):
                lanes = slice(k * width + h * half, k * width + (h + 1) * half)
                kind = h if k == 0 else k + 1
                parts = spectrum_ref[total // TILE, :, lanes]
                value = None
                for p in range(comps):
                    term = parts[p : p + 1] * beyond_weight_ref[p, :, kind * half : (kind + 1) * half]
                    value = term if value is None else value + term
                high, low = split(jnp.concatenate([value, jnp.zeros_like(value)], axis=0))
                scaled_ref[at, lanes] = high
                scaled_ref[at, around + lanes.start : around + lanes.stop] = low

    if at_end:
        scale_beyond()
    step = rows if group > 1 else 32
    for row in range(0, rows, step):
        scale(row, min(step, rows - row))

    def inverse(columns, table_ref):
        low = scaled_ref[:, around + columns.start : around + columns.stop]
        return product(scaled_ref[:, columns], low, table_ref)

    zero = inverse(slice(0, width), even_ref.at[0])
    two = inverse(slice(width, 2 * width), even_ref.at[1])
    odds = inverse(slice(2 * width, around), odd_ref)
    own_all = zero + two + odds[:, :width]
    other_all = zero - two + sign * odds[:, width:]
    for q in range(comps):
        at = q * rows
        own, other = own_all[at : at + rows], other_all[at : at + rows]
        side = halo_ref[pl.ds(at, rows), :]
        far_before, far_after = side[:, :1], side[:, 1:2]
        own_before = jnp.where(odd, other[:, width - 1 :], far_before)
        own_after = jnp.where(odd, far_after, other[:, :1])
        other_before = jnp.where(odd, far_before, own[:, width - 1 :])
        other_after = jnp.where(odd, own[:, :1], far_after)
        solids = [edge_column(tile, TILE - 1) for tile in (12, 13, 14, 15)]
        at = pl.ds(at, rows)
        prec_ref[at, :width] = own * solid
        prec_ref[at, width:] = jnp.where(first, own_before * solids[0], own_after * solids[1])
        tile = jnp.where(first, other_before * solids[2], other_after * solids[3])
        tile = jnp.where(lane == 2, edge_column(10, q), jnp.where(lane == 3, edge_column(11, q), tile))
        back_ref[at, :width] = other
        back_ref[at, width:] = tile
    if at_end:
        at = pl.ds(total, TILE)
        for ref, result, source in ((prec_ref, own_all, own_ref), (back_ref, other_all, core_ref)):
            ref[at, :width] = result[total : total + TILE] * source[pl.ds(total + comps, 1), :]
            ref[at, width:] = jnp.zeros((TILE, LANES), F32)


def image_rows(q, fields, tile, stiff, solid, factor, before, after, inner):
    field = fields[q][inner]
    beside = beside_sum(field, tile[:, :1], tile[:, 1:2])
    beside = beside + stacked_sum(fields[q], before, after)[inner]
    stiffness = stiff * factor[:, q : q + 1]
    return field, solid * ((stiffness + 4.5) * field - beside - 0.5 * fields[q ^ 1][inner])


def add_sums(sums, residual, field, image):
    rows, width = field.shape
    pairs = ((residual, field), (field, image), (residual, residual), (residual, image), (image, image))
    return [
        total + jnp.sum((x * y).reshape(rows // TILE, TILE, width), axis=0)
        for total, (x, y) in zip(sums, pairs)
    ]


def returned(back, sent, solid, q, rows):
    width = sent.shape[1]
    side = back[pl.ds(q * rows, rows), width:]
    residual = sent[pl.ds(q * rows, rows), :]
    lane = lanes_of(residual.shape)
    residual = residual + jnp.where(lane == 0, side[:, 2:3], 0.0) + jnp.where(lane == width - 1, side[:, 3:4], 0.0)
    return back[pl.ds(q * rows, rows), :width] * solid, side, residual


def early_kernel(
    end, comps, stiff_ref, hole_ref, factor_ref, own_ref, back_ref, residual_ref, sent_ref,
    prec_out, residual_out, image_ref, sums_ref,
):
    slab, width = hole_ref.shape
    inner = slab // 2 - end
    core = lax.axis_index("sec") % 2
    here = pl.ds(pl.multiple_of(inner * core, TILE), inner)
    there = pl.ds(pl.multiple_of(inner * (1 - core), TILE), inner)
    solid_there = (1 - hole_ref[pl.ds(pl.multiple_of(end + inner * (1 - core), TILE), inner)]).astype(F32)
    for q in range(comps):
        prec, side, residual = returned(back_ref, sent_ref, solid_there, q, inner)
        prec_out[q, here] = own_ref[pl.ds(q * inner, inner), :]
        prec_out[q, there, :width] = prec
        prec_out[q, there, width:] = side
        residual_out[q, here] = residual_ref[q]
        residual_out[q, there] = residual
    low, high = end + TILE, slab - end - TILE
    core_rows = slice(TILE, 2 * inner - TILE)
    solid = (1 - hole_ref[low:high]).astype(F32)
    factor = factor_ref[low:high]
    sums = [jnp.zeros((TILE, width), F32) for _ in range(5)]
    for q in range(comps):
        fields = {k: prec_out[k, :, :width] for k in (q, q ^ 1)}
        field, image = image_rows(
            q, fields, prec_out[q, core_rows, width:], stiff_ref[q, low:high], solid, factor, 0.0, 0.0, core_rows
        )
        image_ref[q] = image
        sums = add_sums(sums, residual_out[q, core_rows], field, image)
    for i, total in enumerate(sums):
        sums_ref[pl.ds(i * TILE, TILE), :] = total


def late_kernel(
    end, comps, stiff_ref, hole_ref, factor_ref, inner_ref, inner_residual_ref,
    own_ref, back_ref, residual_ref, sent_ref, partial_ref,
    prec_out, residual_out, image_ref, sums_ref,
):
    slab, width = hole_ref.shape
    reach = end + TILE
    core = lax.axis_index("sec") % 2
    odd = core == 1
    solid = (1 - hole_ref[...]).astype(F32)
    factor = factor_ref[...]
    sums = [partial_ref[pl.ds(i * TILE, TILE), :] for i in range(5)]
    fields, tiles, beyond, residuals = [[], []], [[], []], [[], []], [[], []]
    for q in range(comps):
        solid_there = jnp.where(odd, solid[:end], solid[slab - end :])
        there, side, residual = returned(back_ref, sent_ref, solid_there, q, end)
        rows, far = pl.ds(q * end, end), pl.ds(comps * end + q, 1)
        here, own_side = own_ref[rows, :width], own_ref[rows, width:]
        far_here, far_there = own_ref[far, :width], back_ref[far, :width]
        for h, swap in ((0, odd), (1, core == 0)):
            prec = jnp.where(swap, there, here)
            tile = jnp.where(swap, side, own_side)
            rest = jnp.where(swap, residual, residual_ref[q])
            beyond[h].append(jnp.where(swap, far_there, far_here))
            rows = pl.ds(end * h, end)
            prec_out[q, rows] = prec
            residual_out[q, rows] = rest
            near = slice(0, 2 * TILE) if h == 0 else slice(-2 * TILE, None)
            close = slice(0, TILE) if h == 0 else slice(-TILE, None)
            parts = [prec, inner_ref[q, near, :width]]
            sides = [tile, inner_ref[q, close, width:]]
            rests = [rest, inner_residual_ref[q, close]]
            order = slice(None) if h == 0 else slice(None, None, -1)
            fields[h].append(jnp.concatenate(parts[order], axis=0))
            tiles[h].append(jnp.concatenate(sides[order], axis=0))
            residuals[h].append(jnp.concatenate(rests[order], axis=0))
    for h in range(2):
        rows = slice(0, reach) if h == 0 else slice(slab - reach, slab)
        inner = slice(0, reach) if h == 0 else slice(TILE, None)
        for q in range(comps):
            before, after = (beyond[0][q], 0.0) if h == 0 else (0.0, beyond[1][q])
            field, image = image_rows(
                q, fields[h], tiles[h][q], stiff_ref[q, rows], solid[rows], factor[rows], before, after, inner
            )
            image_ref[q, pl.ds(reach * h, reach)] = image
            sums = add_sums(sums, residuals[h][q], field, image)
    row = jnp.zeros((1, LANES), F32)
    spot = lanes_of((1, LANES))
    for i, value in enumerate(sums):
        value = jnp.sum(jnp.sum(value, axis=0, keepdims=True), axis=1, keepdims=True)
        row = jnp.where(spot == i, value, row)
    sums_ref[...] = jnp.broadcast_to(row, sums_ref.shape)


def update_kernel(
    end, comps, cell_total, disp_ref, gathered_ref, inner_ref, inner_residual_ref, inner_image_ref,
    ends_ref, ends_residual_ref, ends_image_ref, disp_out, residual_out, stats_out,
):
    slab, width = disp_ref.shape[1:]
    values = jnp.sum(gathered_ref[...], axis=0, keepdims=True) * F32(1.0 / cell_total)
    rz, zq, rr, ri, ii = [values[:, i : i + 1] for i in range(5)]
    alpha = rz / zq
    square = rr + alpha * (alpha * ii - 2.0 * ri)
    stats_out[...] = jnp.concatenate([rz, zq, square], axis=1)
    reach = end + TILE
    inner = slice(end, slab - end)
    for q in range(comps):
        disp_out[q, :end] = disp_ref[q, :end] + alpha * ends_ref[q, :end]
        disp_out[q, inner] = disp_ref[q, inner] + alpha * inner_ref[q, :, :width]
        disp_out[q, slab - end :] = disp_ref[q, slab - end :] + alpha * ends_ref[q, end:]
        image = jnp.concatenate([ends_image_ref[q, :reach], inner_image_ref[q], ends_image_ref[q, reach:]], axis=0)
        residual_out[q, :end] = ends_residual_ref[q, :end] - alpha * image[:end]
        residual_out[q, inner] = inner_residual_ref[q] - alpha * image[inner]
        residual_out[q, slab - end :] = ends_residual_ref[q, end:] - alpha * image[slab - end :]


VMEM = pl.BlockSpec(memory_space=pltpu.VMEM)
SMEM = pl.BlockSpec(memory_space=pltpu.SMEM)
HBM = pl.BlockSpec(memory_space=pltpu.HBM)
FULL = 62


def call(kernel, name, out_shapes, in_specs, flops, moved, scratch=(), grant=32, out_specs=None):
    return pl.pallas_call(
        kernel,
        out_shape=[jax.ShapeDtypeStruct(s, F32) for s in out_shapes],
        in_specs=in_specs,
        out_specs=out_specs or [VMEM] * len(out_shapes),
        scratch_shapes=list(scratch),
        compiler_params=pltpu.CompilerParams(vmem_limit_bytes=grant * 1024 * 1024),
        cost_estimate=pl.CostEstimate(flops=flops, bytes_accessed=moved, transcendentals=0),
        name=name,
    )


def transform_call(blocks, tables, hole, edge, main, edge_at, hole_at, comps, width, slab, weight):
    around = SECTORS * width
    at_end = edge is not None
    total = comps * main
    out_rows = total + (TILE if at_end else 0)
    rows = total + (2 * TILE if at_end else 0)
    operands = list(blocks) + list(tables) + [hole] + ([edge] if at_end else [])
    shapes = [(out_rows, width + LANES), (comps, main, width), (out_rows, width + LANES)]
    return call(
        functools.partial(transform_kernel, comps, main, at_end, edge_at, hole_at), "transform",
        ([] if at_end else [(slab, LANES)]) + shapes, [VMEM] * len(operands),
        weight * 2 * total * 3 * around * 3 * width, weight * 4 * total * width * 8,
        [pltpu.VMEM((rows, 8 * width), BF16), pltpu.VMEM((rows // TILE, TILE, around), F32),
         pltpu.VMEM((rows, 2 * around), BF16), pltpu.VMEM((total, LANES), F32)],
    )(*operands)


def after_all(x, *others):
    return lax.optimization_barrier((x, *others))[0]


def shards(load, disp, stiff, hole, section_class, class_table, precond):
    slab, comps, width = disp.shape
    ax, sec = lax.axis_size("ax"), lax.axis_size("sec")
    around = width * sec
    cell_total = slab * ax * comps * around
    end = slab // 16 * 2
    inner = slab // 2 - end
    load, disp, stiff = [x.transpose(1, 0, 2) for x in (load, disp, stiff)]
    forward, even, odd, beyond = harmonic_tables(width)
    block = 4 * comps * slab * width
    classes = section_class.reshape(1, slab)

    sent = (comps * inner + TILE, width)
    ends_shape = (2, comps * end + 2 * TILE, width)
    shapes = [sent, ends_shape, (slab, LANES), (2 * TILE, width), (2 * TILE, width)]
    small = [pltpu.SMEM(class_table.shape, F32), pltpu.VMEM((1, slab), jnp.int32)]
    arguments = (class_table, classes, load, disp, stiff, hole)
    reach = slab // 2 + TILE
    (keep,) = call(
        functools.partial(first_kernel, end, comps, ax), "first",
        [sent], [HBM] * 6, 10 * comps * inner * width, block,
        small + [pltpu.VMEM((comps, rows, width), F32) for rows in (inner, reach, inner)]
        + [pltpu.VMEM((reach, width), jnp.int32), pltpu.VMEM(sent, F32), pltpu.VMEM((slab, LANES), F32)]
        + [pltpu.SemaphoreType.DMA((3 + 3 * comps // 2,)), pltpu.SemaphoreType.DMA((1 + comps // 2,))],
        FULL, [HBM],
    )(*arguments)
    other, edge, factor, near, other_side = call(
        functools.partial(second_kernel, end, comps, ax), "second",
        shapes, [HBM] * 6, 10 * comps * slab * width, 2 * block,
        small + [pltpu.VMEM((comps, slab, width), F32)] * 3 + [pltpu.VMEM((slab, width), jnp.int32)]
        + [pltpu.VMEM((2,) + sent, F32)] + [pltpu.VMEM(shape, F32) for shape in shapes[1:3] + [(2, 2 * TILE, width)]]
        + [pltpu.SemaphoreType.DMA((3 + 3 * comps // 2,)), pltpu.SemaphoreType.DMA((6 + comps,))],
        FULL, [HBM] * len(shapes),
    )(*arguments)

    def to(x, mask):
        return lax.ppermute(x, "sec", [(i, i ^ mask) for i in range(sec)])

    def gather(keep, other):
        return keep, to(other, 1), to(keep, 2), to(other, 3)

    blocks = gather(keep, other)
    near = lax.ppermute(near, "ax", [(i, i ^ 1) for i in range(ax)])
    other_side = lax.ppermute(other_side, "ax", [(i, ((i + 1) ^ 1) - 1) for i in range(1, ax - 1)])
    weight, beyond_weight = call(
        fold_kernel, "fold", [(comps * comps, TILE, 5 * width // 2), (comps, TILE, 5 * width // 2)], [VMEM] * 5,
        1, 1,
    )(precond, forward, even, odd, beyond)
    rows = (comps * end + TILE, width)
    keep_ends, other_ends = call(
        functools.partial(ends_kernel, comps), "ends",
        [rows, rows], [VMEM] * 3, 2 * comps * end * width, 16 * comps * end * width, [pltpu.VMEM((2,) + rows, F32)],
    )(after_all(edge, weight), near, other_side)
    end_blocks = gather(keep_ends, other_ends)
    tables = (forward, even, odd, beyond, weight, beyond_weight)

    across = after_all(blocks[2], keep_ends, weight)
    edge, own, residual, back = transform_call(
        (keep, blocks[1], across, blocks[3]), tables, hole, None, inner, 0, (end, inner), comps, width, slab, 0
    )
    back = to(back, 1)
    across = after_all(end_blocks[2], own)
    own_ends, residual_ends, back_ends = transform_call(
        (keep_ends, end_blocks[1], across, end_blocks[3]), tables, hole, edge, end, inner, (0, slab - end),
        comps, width, slab, 100,
    )
    back_ends = to(back_ends, 1)
    prec, residual, image, partial = call(
        functools.partial(early_kernel, end, comps), "early",
        [(comps, 2 * inner, width + LANES), (comps, 2 * inner, width), (comps, 2 * (inner - TILE), width), (5 * TILE, width)],
        [VMEM] * 7, 30 * comps * slab * width, 4 * block,
    )(stiff, hole, after_all(factor, own_ends), own, back, residual, other)
    prec_ends, residual_ends, image_ends, sums = call(
        functools.partial(late_kernel, end, comps), "late",
        [(comps, 2 * end, width), (comps, 2 * end, width), (comps, 2 * (end + TILE), width), (ax * sec, LANES)],
        [VMEM] * 10, 8 * comps * slab * width, block,
    )(stiff, hole, factor, prec, residual, own_ends, back_ends, residual_ends, other_ends, partial)
    gathered = lax.all_to_all(sums, ("ax", "sec"), 0, 0, tiled=True)
    disp_new, residual_new, stats = call(
        functools.partial(update_kernel, end, comps, cell_total), "update",
        [(comps, slab, width), (comps, slab, width), (1, 3)], [VMEM] * 8,
        4 * comps * slab * width, 6 * block,
    )(disp, gathered, prec, residual, image, prec_ends, residual_ends, image_ends)
    return disp_new.transpose(1, 0, 2), residual_new.transpose(1, 0, 2), stats.reshape(3)


def solution(mesh):
    in_specs = (
        P("ax", None, "sec"),
        P("ax", None, "sec"),
        P("ax", None, "sec"),
        P("ax", "sec"),
        P("ax"),
        P(),
        P(),
    )
    out_specs = (P("ax", None, "sec"), P("ax", None, "sec"), P())
    return jax.shard_map(shards, mesh=mesh, in_specs=in_specs, out_specs=out_specs, check_vma=False)
```

```python
import functools

import jax
import jax.numpy as jnp
import ml_dtypes
import numpy as np
from jax import lax
from jax.experimental import pallas as pl
from jax.experimental.pallas import tpu as pltpu
from jax.sharding import PartitionSpec as P

F32 = jnp.float32
BF16 = jnp.bfloat16
SECTORS = 4
TILE = 8
LANES = 128


def two_parts(table):
    high = table.astype(ml_dtypes.bfloat16)
    low = (table - high.astype(np.float64)).astype(ml_dtypes.bfloat16)
    return np.stack([high, low])


@functools.lru_cache(maxsize=None)
def harmonic_tables(width):
    around = SECTORS * width
    half = width // 2
    zero = [("c", 4 * q) for q in range(half + 1)] + [("s", 4 * q) for q in range(1, half)]
    two = [(f, 4 * q + 2) for f in "cs" for q in range(half)]
    one = [(f, 8 * q + 1) for f in "cs" for q in range(half)]
    five = [(f, 8 * q + 5) for f in "cs" for q in range(half)]
    columns = zero + two + one + five
    harmonic = np.array([k for _, k in columns], dtype=np.int64)
    is_sin = np.array([f == "s" for f, _ in columns])

    def wave(place, shift):
        angle = 2.0 * np.pi / around * ((place[:, None] * harmonic[None, :]) % around)
        return np.cos(angle - shift)

    place = np.arange(width)
    shift = np.where(is_sin, np.pi / 2, 0.0)[None, :]
    direct = wave(place, shift)
    turned = np.concatenate([direct[:half], wave(place[:half], shift - np.pi / 2)], axis=0)
    forward = [direct[:, :width], direct[:, width : 2 * width]]
    forward += [turned[:, 2 * width : 3 * width], turned[:, 3 * width :]]
    ends = np.array([around - 1, 2 * width, around - width - 1, width])
    beyond = np.repeat(wave(ends, shift).astype(np.float32)[:, None, :], TILE, axis=1)
    odd = np.concatenate([direct.T, wave(place + width, shift).T], axis=1)[2 * width :]
    return (
        np.stack([two_parts(t) for t in forward]),
        np.stack([two_parts(t) for t in (direct.T[:width], direct.T[width : 2 * width])]),
        two_parts(odd),
        beyond,
    )


def split(x):
    high = x.astype(BF16)
    return high, (x - high.astype(F32)).astype(BF16)


def product(high, low, table_ref):
    left = jnp.concatenate([high, low, high], axis=1)
    table = jnp.concatenate([table_ref[0], table_ref[0], table_ref[1]], axis=0)
    return jnp.dot(left, table, preferred_element_type=F32)


def lanes_of(shape):
    return lax.broadcasted_iota(jnp.int32, shape, len(shape) - 1)


def rows_of(shape):
    return lax.broadcasted_iota(jnp.int32, shape, len(shape) - 2)


def beside_sum(x, before, after):
    lane = lanes_of(x.shape)
    size = x.shape[-1]
    left = jnp.where(lane == 0, before, pltpu.roll(x, 1, x.ndim - 1))
    right = jnp.where(lane == size - 1, after, pltpu.roll(x, size - 1, x.ndim - 1))
    return left + right


def stacked_sum(x, before=0.0, after=0.0):
    row = rows_of(x.shape)
    size = x.shape[0]
    up = jnp.where(row == 0, before, pltpu.roll(x, 1, 0))
    down = jnp.where(row == size - 1, after, pltpu.roll(x, size - 1, 0))
    return up + down


def fold_kernel(precond_ref, *refs):
    out_ref, beyond_ref = refs[-2:]
    comps = precond_ref.shape[0]
    value = jnp.concatenate([precond_ref[q] for q in range(comps)], axis=0)
    pairs, around = value.shape
    high = value.astype(BF16)
    rest = value - high.astype(F32)
    middle = rest.astype(BF16)
    low = (rest - middle.astype(F32)).astype(BF16)
    half = around // 8
    row, step = rows_of((around, half)), lanes_of((around, half))
    kinds = []
    for k in (4 * step, 4 * step + 2, 8 * step + 1, 8 * step + 5):
        kinds.append(jnp.where((row == k) | (row == around - k), F32(1.0 / around), 0.0).astype(BF16))
    fold = jnp.concatenate(kinds, axis=1)
    terms = [jnp.dot(t, fold, preferred_element_type=F32) for t in (high, middle, low)]
    folded = terms[0] + (terms[1] + terms[2])
    zero = folded[:, :half]
    top = value[:, around // 2 : around // 2 + 1] * F32(1.0 / around)
    other = jnp.where(lanes_of(zero.shape) == 0, top, zero)
    folded = jnp.concatenate([zero, other, folded[:, half:]], axis=1)
    for i in range(pairs):
        out_ref[i] = jnp.broadcast_to(folded[i : i + 1], out_ref.shape[1:])
    rest = [jnp.zeros((TILE - comps, folded.shape[1]), F32)]
    for p in range(comps):
        beyond_ref[p] = jnp.concatenate([folded[i : i + 1] for i in range(p, pairs, comps)] + rest, axis=0)


def factor_columns(table_ref, class_ref, ax_size, comps):
    classes = class_ref[...]
    slab = classes.shape[1]
    position = lax.axis_index("ax") * slab + lanes_of(classes.shape)
    taper = 1.0 + 2.0 * position.astype(F32) / F32(ax_size * slab - 1)
    rows = []
    for q in range(comps):
        value = jnp.zeros(classes.shape, F32)
        for kind in range(table_ref.shape[0]):
            value = jnp.where(classes == kind, table_ref[kind, q], value)
        rows.append(value * taper)
    rows.append(jnp.zeros((LANES - comps, slab), F32))
    return jnp.concatenate(rows, axis=0).T


def local_part(q, block, inner, solid, factor, load, stiff, other):
    field = block[inner]
    beside = stacked_sum(block)[inner] + beside_sum(field, 0.0, 0.0)
    stiffness = stiff * factor[:, q : q + 1]
    image = (stiffness + 4.5) * field - beside - 0.5 * other[inner]
    return solid * (load - image)


def edge_rows(fields, solid):
    rows, width = solid.shape
    sources = fields + [solid] * (TILE - len(fields))
    lane = lanes_of((rows, LANES))
    table = jnp.zeros((rows, LANES), F32)
    for i, x in enumerate(sources):
        table = jnp.where(lane == i, pltpu.roll(x[:, :LANES], i, 1) if i else x[:, :LANES], table)
        table = jnp.where(lane == TILE + i, pltpu.roll(x[:, width - LANES :], TILE + i + 1, 1), table)
    if rows < LANES:
        table = jnp.concatenate([table, jnp.zeros((LANES - rows, LANES), F32)], axis=0)
    table = table.T
    return table[:TILE], table[TILE : 2 * TILE]


def copy(src, dst, sem):
    moving = pltpu.make_async_copy(src, dst, sem)
    moving.start()
    return moving


def first_kernel(
    end, comps, ax_size, table_ref, class_ref, load_ref, disp_ref, stiff_ref, hole_ref, keep_ref,
    table_in, class_in, load_in, disp_in, stiff_in, hole_in, keep_out, factor_in, in_sems, out_sems,
):
    slab, width = hole_ref.shape
    half = slab // 2
    inner, reach = half - end, half + TILE
    core = lax.axis_index("sec") % 2
    base = pl.multiple_of((half - TILE) * core, TILE)
    start = pl.multiple_of(end + inner * core, TILE)
    here = pl.ds(pl.multiple_of(end - (end - TILE) * core, TILE), inner)
    around = pl.ds(pl.multiple_of(end - TILE - (end - TILE) * core, TILE), inner + 2 * TILE)
    tail = pl.ds(pl.multiple_of((reach - end) * core, TILE), end)
    small = [
        copy(class_ref, class_in, in_sems.at[0]),
        copy(table_ref, table_in, in_sems.at[1]),
        copy(hole_ref.at[pl.ds(base, reach)], hole_in, in_sems.at[2]),
    ]
    pairs = comps // 2
    moving = []
    for g in range(pairs):
        both = pl.ds(2 * g, 2)
        arrays = (
            (disp_ref.at[both, pl.ds(base, reach)], disp_in), (load_ref.at[both, pl.ds(start, inner)], load_in),
            (stiff_ref.at[both, pl.ds(start, inner)], stiff_in),
        )
        moving.append([copy(src, dst.at[both], in_sems.at[3 + 3 * g + k]) for k, (src, dst) in enumerate(arrays)])
    for one in small:
        one.wait()
    factor_in[...] = factor_columns(table_in, class_in, ax_size, comps)
    factor = factor_in[pl.ds(start, inner), :]
    solid = (1 - hole_in[here, :]).astype(F32)
    solid_tail = (1 - hole_in[tail, :]).astype(F32)
    inside = slice(TILE, TILE + inner)
    leaving = []
    for g in range(pairs):
        moving[g][0].wait()
        if g == pairs - 1:
            fields = [jnp.concatenate([disp_in[q, here], disp_in[q, tail]], axis=0) for q in range(comps)]
            last = pl.ds(comps * inner, TILE)
            keep_out[last, :] = jnp.concatenate(
                edge_rows(fields, jnp.concatenate([solid, solid_tail], axis=0)), axis=1
            )
            leaving.append(copy(keep_out.at[last], keep_ref.at[last], out_sems.at[comps]))
        moving[g][1].wait()
        moving[g][2].wait()
        for q in (2 * g, 2 * g + 1):
            rows = pl.ds(q * inner, inner)
            keep_out[rows, :] = local_part(
                q, disp_in[q, around], inside, solid, factor, load_in[q], stiff_in[q], disp_in[q ^ 1, around]
            )
            leaving.append(copy(keep_out.at[rows], keep_ref.at[rows], out_sems.at[q]))
    for one in leaving:
        one.wait()


def second_kernel(
    end, comps, ax_size, table_ref, class_ref, load_ref, disp_ref, stiff_ref, hole_ref,
    other_ref, ends_ref, factor_ref, near_ref, next_ref,
    table_in, class_in, load_in, disp_in, stiff_in, hole_in, inner_out, ends_out, factor_out, message_out,
    in_sems, out_sems,
):
    slab, width = hole_ref.shape
    half = slab // 2
    inner = half - end
    core = lax.axis_index("sec") % 2

    small = [
        copy(class_ref, class_in, in_sems.at[0]), copy(table_ref, table_in, in_sems.at[1]), copy(hole_ref, hole_in, in_sems.at[2])
    ]
    pairs = comps // 2
    moving = []
    for g in range(pairs):
        both = pl.ds(2 * g, 2)
        arrays = ((disp_ref, disp_in), (load_ref, load_in), (stiff_ref, stiff_in))
        moving.append([copy(src.at[both], dst.at[both], in_sems.at[3 + 3 * g + k]) for k, (src, dst) in enumerate(arrays)])
    for one in small:
        one.wait()
    factor_out[...] = factor_columns(table_in, class_in, ax_size, comps)
    leaving = [copy(factor_out, factor_ref, out_sems.at[0])]
    solid = (1 - hole_in[...]).astype(F32)
    spare = TILE - comps
    for h, row in ((0, 0), (1, slab - 1)):
        message_out[h, comps:TILE, :] = jnp.broadcast_to(solid[row : row + 1], (spare, width))
        message_out[h, TILE + comps :, :] = jnp.zeros((spare, width), F32)
    factor = factor_out[...]

    def ordered(x):
        return jnp.concatenate([x[end:half], x[:end], x[half:]], axis=0)

    for g in range(pairs):
        moving[g][0].wait()
        if g == pairs - 1:
            edges = edge_rows([ordered(disp_in[q]) for q in range(comps)], ordered(solid))
            last = pl.ds(comps * inner, TILE)
            for h in range(2):
                inner_out[h, last, :] = jnp.concatenate(
                    [pltpu.roll(x, (LANES - half * h) % LANES, 1) for x in edges], axis=1
                )
            leaving.append(copy(inner_out.at[1 - core, last], other_ref.at[last], out_sems.at[2]))
        moving[g][1].wait()
        moving[g][2].wait()
        for q in (2 * g, 2 * g + 1):
            field = disp_in[q]
            part = local_part(q, field, slice(0, slab), solid, factor, load_in[q], stiff_in[q], disp_in[q ^ 1])
            rows = pl.ds(q * inner, inner)
            inner_out[0, rows, :] = part[end:half]
            inner_out[1, rows, :] = part[half : slab - end]
            rows = pl.ds(q * end, end)
            ends_out[0, rows, :] = part[:end]
            ends_out[1, rows, :] = part[slab - end :]
            for h, row in ((0, slice(0, 1)), (1, slice(slab - 1, slab))):
                message_out[h, q : q + 1, :] = part[row]
                message_out[h, TILE + q : TILE + q + 1, :] = field[row]
        rows = pl.ds(2 * g * inner, 2 * inner)
        leaving.append(copy(inner_out.at[1 - core, rows], other_ref.at[rows], out_sems.at[4 + 2 * g]))
    count = 3 + 2 * pairs
    side = lax.axis_index("ax") % 2
    leaving.append(copy(message_out.at[1 - side], near_ref, out_sems.at[count]))
    leaving.append(copy(message_out.at[side], next_ref, out_sems.at[count + 1]))
    for h in range(2):
        ends_out[h, pl.ds(comps * end, 2 * TILE), :] = message_out[h]
    leaving.append(copy(ends_out, ends_ref, out_sems.at[count + 2]))
    for one in leaving:
        one.wait()


def ends_kernel(comps, ends_ref, near_ref, next_ref, keep_ref, other_ref, out_ref):
    rows = (ends_ref.shape[1] - 2 * TILE) // comps
    width = ends_ref.shape[2]
    row = rows_of((rows, width))
    spot, place = rows_of((TILE, width)), lanes_of((TILE, width))
    core = lax.axis_index("sec") % 2
    odd = lax.axis_index("ax") % 2 == 1
    near, other = near_ref[...], next_ref[...]
    for h, far, at in ((0, jnp.where(odd, near, other), 0), (1, jnp.where(odd, other, near), rows - 1)):
        own_ref = ends_ref.at[h, pl.ds(comps * rows, 2 * TILE)]
        solid_own = own_ref[comps : comps + 1]
        for q in range(comps):
            part = ends_ref[h, pl.ds(q * rows, rows), :]
            part = part + jnp.where(row == at, solid_own * far[TILE + q : TILE + q + 1], 0.0)
            out_ref[h, pl.ds(q * rows, rows), :] = part
        solid_far, disp_far = far[comps : comps + 1], far[TILE:]
        edges = jnp.where(place == spot, disp_far[:, :1], 0.0)
        edges = edges + jnp.where(place == spot + TILE, disp_far[:, width - 1 :], 0.0)
        edges = jnp.sum(edges, axis=0, keepdims=True)
        beyond = far[:TILE] + solid_far * own_ref[TILE:]
        beyond = jnp.where(spot < comps, beyond, jnp.where(spot == TILE - 1, edges, solid_far))
        out_ref[h, pl.ds(comps * rows, TILE), :] = beyond
    keep_ref[...] = out_ref[core]
    other_ref[...] = out_ref[1 - core]


def in_order(odd, own, core, across, both):
    return own, jnp.where(odd, both, core), across, jnp.where(odd, core, both)


def butterfly(x0, x1, x2, x3):
    even, other = x0 + x2, x1 + x3
    return even + other, even - other, x0 - x2, x1 - x3


def edge_table(odd, blocks):
    tiles = in_order(odd, *blocks)
    left = [t[:, :LANES] for t in tiles]
    right = [t[:, LANES:] for t in tiles]
    solid = TILE - 1
    at_left = [left[s][solid:] * right[s - 1] for s in range(SECTORS)]
    at_right = [right[s][solid:] * left[(s + 1) % SECTORS] for s in range(SECTORS)]
    stack = []
    for one, other in zip(butterfly(*at_left), butterfly(*at_right)):
        stack += [one, other]
    stack += [at_left[0], at_right[0]]
    stack += [jnp.where(odd, at_left[3], at_left[1]), jnp.where(odd, at_right[3], at_right[1])]
    stack += [right[3], left[1], jnp.where(odd, right[2], right[0]), jnp.where(odd, left[0], left[2])]
    return jnp.concatenate(stack, axis=0).T


def transform_kernel(
    comps, main, at_end, edge_at, hole_at, own_ref, core_ref, across_ref, both_ref,
    forward_ref, even_ref, odd_ref, beyond_ref, weight_ref, beyond_weight_ref, hole_ref, edge_ref,
    prec_ref, residual_ref, back_ref, left_ref, spectrum_ref, scaled_ref, halo_ref,
):
    width = own_ref.shape[1]
    half = width // 2
    core = lax.axis_index("sec") % 2
    odd = core == 1
    sign = jnp.where(odd, -1.0, 1.0)
    rows = main
    total = comps * rows
    group = 1 if rows % 16 == 0 else 2
    sources = (own_ref, core_ref, across_ref, both_ref)
    start, stride = hole_at
    solid = (1 - hole_ref[pl.ds(pl.multiple_of(start + stride * core, TILE), main)]).astype(F32)
    if not at_end:
        edge_ref[...] = edge_table(odd, [r[total : total + TILE] for r in sources])
    edge = edge_ref[pl.ds(edge_at, main), :]
    lane = lanes_of((main, LANES))
    first = lane == 0
    last = lane == LANES - 1

    def edge_column(tile, q):
        column = tile * TILE + q
        return edge[:, column : column + 1]

    def with_edges(x, array, q):
        head = x[:, :LANES] + jnp.where(first, edge_column(2 * array, q), 0.0)
        tail = x[:, -LANES:] + jnp.where(last, edge_column(2 * array + 1, q), 0.0)
        middle = [x[:, LANES:-LANES]] if width > 2 * LANES else []
        return jnp.concatenate([head] + middle + [tail], axis=1)

    def arrays_of(q):
        at = q * rows
        own, core, across, both = [r[pl.ds(at, main), :] for r in sources]
        arrays = butterfly(own, core, across, both)
        arrays = arrays[:3] + (sign * arrays[3],)
        arrays = [with_edges(x, i, q) for i, x in enumerate(arrays)]
        residual_ref[q] = with_edges(own, 4, q)
        return turned(*arrays)

    def turned(y0, y2, real, imag):
        turned_real = (real[:, half:] - imag[:, half:]) * F32(np.sqrt(0.5))
        turned_imag = (real[:, half:] + imag[:, half:]) * F32(np.sqrt(0.5))
        plus = jnp.concatenate([real[:, :half] + turned_real, imag[:, :half] + turned_imag], axis=1)
        minus = jnp.concatenate([real[:, :half] - turned_real, imag[:, :half] - turned_imag], axis=1)
        return y0, y2, plus, minus

    def arrays_beyond():
        tiles = in_order(odd, *[r[pl.ds(total, TILE), :] for r in sources])
        spot, place = rows_of((TILE, width)), lanes_of((TILE, width))

        def column(tile, at):
            return jnp.sum(jnp.where(place == spot + at, tile[TILE - 1 :], 0.0), axis=1, keepdims=True)

        fixed = []
        for s in range(SECTORS):
            beside = jnp.where(place == 0, column(tiles[s - 1], TILE), 0.0)
            beside = beside + jnp.where(place == width - 1, column(tiles[(s + 1) % SECTORS], 0), 0.0)
            value = tiles[s] + tiles[s][comps : comps + 1] * beside
            fixed.append(jnp.where(spot < comps, value, 0.0))
        return turned(*butterfly(*fixed))

    def put(at, arrays):
        for i, x in enumerate(arrays):
            high, low = split(x)
            left_ref[at, 2 * i * width : (2 * i + 1) * width] = high
            left_ref[at, (2 * i + 1) * width : (2 * i + 2) * width] = low

    for begin in range(0, comps, group):
        found = [arrays_of(q) for q in range(begin, begin + group)]
        put(pl.ds(begin * rows, group * rows), [jnp.concatenate([x[i] for x in found], axis=0) for i in range(4)])
    if at_end:
        put(pl.ds(total, 2 * TILE), [jnp.concatenate([x, jnp.zeros_like(x)], axis=0) for x in arrays_beyond()])
    height = left_ref.shape[0]

    for i in range(4):
        high = left_ref[:, 2 * i * width : (2 * i + 1) * width]
        low = left_ref[:, (2 * i + 1) * width : (2 * i + 2) * width]
        part = product(high, low, forward_ref.at[i])
        spectrum_ref[:, :, i * width : (i + 1) * width] = part.reshape(height // TILE, TILE, width)

    around = SECTORS * width

    def scale(row, count):
        tiles = count // TILE

        def spectrum(p, lanes):
            return spectrum_ref[pl.ds((p * rows + row) // TILE, tiles), :, lanes]

        for begin in range(0, comps, group):
            halo = [[None, None] for _ in range(group)]
            for k in range(4):
                for h in range(2):
                    lanes = slice(k * width + h * half, k * width + (h + 1) * half)
                    kind = h if k == 0 else k + 1
                    values = []
                    for i in range(group):
                        value = None
                        for p in range(comps):
                            weight = weight_ref[(begin + i) * comps + p, :, kind * half : (kind + 1) * half]
                            term = spectrum(p, lanes) * weight
                            value = term if value is None else value + term
                        for side in range(2):
                            term = value * beyond_ref[2 * core + side, :, lanes]
                            halo[i][side] = term if halo[i][side] is None else halo[i][side] + term
                        values.append(value.reshape(count, half))
                    high, low = split(values[0] if group == 1 else jnp.concatenate(values, axis=0))
                    at = pl.ds(begin * rows + row, group * count)
                    scaled_ref[at, lanes] = high
                    scaled_ref[at, around + lanes.start : around + lanes.stop] = low
            for i in range(group):
                before, after = [jnp.sum(x, axis=2, keepdims=True) for x in halo[i]]
                tile = jnp.where(lanes_of((tiles, TILE, LANES)) == 0, before, after)
                halo_ref[pl.ds((begin + i) * rows + row, count), :] = tile.reshape(count, LANES)

    def scale_beyond():
        at = pl.ds(total, 2 * TILE)
        for k in range(4):
            for h in range(2):
                lanes = slice(k * width + h * half, k * width + (h + 1) * half)
                kind = h if k == 0 else k + 1
                parts = spectrum_ref[total // TILE, :, lanes]
                value = None
                for p in range(comps):
                    term = parts[p : p + 1] * beyond_weight_ref[p, :, kind * half : (kind + 1) * half]
                    value = term if value is None else value + term
                high, low = split(jnp.concatenate([value, jnp.zeros_like(value)], axis=0))
                scaled_ref[at, lanes] = high
                scaled_ref[at, around + lanes.start : around + lanes.stop] = low

    if at_end:
        scale_beyond()
    step = rows if group > 1 else 32
    for row in range(0, rows, step):
        scale(row, min(step, rows - row))

    def inverse(columns, table_ref):
        low = scaled_ref[:, around + columns.start : around + columns.stop]
        return product(scaled_ref[:, columns], low, table_ref)

    zero = inverse(slice(0, width), even_ref.at[0])
    two = inverse(slice(width, 2 * width), even_ref.at[1])
    odds = inverse(slice(2 * width, around), odd_ref)
    own_all = zero + two + odds[:, :width]
    other_all = zero - two + sign * odds[:, width:]
    for q in range(comps):
        at = q * rows
        own, other = own_all[at : at + rows], other_all[at : at + rows]
        side = halo_ref[pl.ds(at, rows), :]
        far_before, far_after = side[:, :1], side[:, 1:2]
        own_before = jnp.where(odd, other[:, width - 1 :], far_before)
        own_after = jnp.where(odd, far_after, other[:, :1])
        other_before = jnp.where(odd, far_before, own[:, width - 1 :])
        other_after = jnp.where(odd, own[:, :1], far_after)
        solids = [edge_column(tile, TILE - 1) for tile in (12, 13, 14, 15)]
        at = pl.ds(at, rows)
        prec_ref[at, :width] = own * solid
        prec_ref[at, width:] = jnp.where(first, own_before * solids[0], own_after * solids[1])
        tile = jnp.where(first, other_before * solids[2], other_after * solids[3])
        tile = jnp.where(lane == 2, edge_column(10, q), jnp.where(lane == 3, edge_column(11, q), tile))
        back_ref[at, :width] = other
        back_ref[at, width:] = tile
    if at_end:
        at = pl.ds(total, TILE)
        for ref, result, source in ((prec_ref, own_all, own_ref), (back_ref, other_all, core_ref)):
            ref[at, :width] = result[total : total + TILE] * source[pl.ds(total + comps, 1), :]
            ref[at, width:] = jnp.zeros((TILE, LANES), F32)


def image_rows(q, fields, tile, stiff, solid, factor, before, after, inner):
    field = fields[q][inner]
    beside = beside_sum(field, tile[:, :1], tile[:, 1:2])
    beside = beside + stacked_sum(fields[q], before, after)[inner]
    stiffness = stiff * factor[:, q : q + 1]
    return field, solid * ((stiffness + 4.5) * field - beside - 0.5 * fields[q ^ 1][inner])


def add_sums(sums, residual, field, image):
    rows, width = field.shape
    pairs = ((residual, field), (field, image), (residual, residual), (residual, image), (image, image))
    return [
        total + jnp.sum((x * y).reshape(rows // TILE, TILE, width), axis=0)
        for total, (x, y) in zip(sums, pairs)
    ]


def returned(back, sent, solid, q, rows):
    width = sent.shape[1]
    side = back[pl.ds(q * rows, rows), width:]
    residual = sent[pl.ds(q * rows, rows), :]
    lane = lanes_of(residual.shape)
    residual = residual + jnp.where(lane == 0, side[:, 2:3], 0.0) + jnp.where(lane == width - 1, side[:, 3:4], 0.0)
    return back[pl.ds(q * rows, rows), :width] * solid, side, residual


def end_image(h, end, comps, found, inner_ref, inner_residual_ref, stiff_ref, hole_ref, factor_ref, sums):
    slab, width = hole_ref.shape
    near = 2 * TILE
    lower = h == 1
    there = pl.ds(pl.multiple_of((inner_ref.shape[1] - near) * h, TILE), near)
    here = pl.ds(pl.multiple_of((slab - end - near) * h, TILE), end + near)

    def joined(ends, inner):
        return jnp.where(lower, jnp.concatenate([inner, ends], axis=0), jnp.concatenate([ends, inner], axis=0))

    solid = (1 - hole_ref[here, :]).astype(F32)
    factor = factor_ref[here, :]
    fields = [joined(found[q][0], inner_ref[q, there, :width]) for q in range(comps)]
    row = rows_of((end + near, width))
    valid = (row >= jnp.where(lower, TILE, 0)) & (row < jnp.where(lower, end + near, end + TILE))
    images = []
    for q in range(comps):
        beyond = found[q][2]
        field, image = image_rows(
            q, fields, joined(found[q][1], inner_ref[q, there, width:]), stiff_ref[q, here], solid, factor,
            jnp.where(lower, 0.0, beyond), jnp.where(lower, beyond, 0.0), slice(0, end + near),
        )
        images.append(jnp.where(lower, image[TILE:], image[: end + TILE]))
        residual = joined(found[q][3], inner_residual_ref[q, there])
        sums = add_sums(sums, *[jnp.where(valid, x, 0.0) for x in (residual, field, image)])
    return images, sums


def early_kernel(
    end, comps, stiff_ref, hole_ref, factor_ref, own_ref, back_ref, residual_ref, sent_ref,
    own_ends_ref, residual_ends_ref, prec_out, residual_out, image_ref, sums_ref, image_ends_ref,
):
    slab, width = hole_ref.shape
    inner = slab // 2 - end
    core = lax.axis_index("sec") % 2
    here = pl.ds(pl.multiple_of(inner * core, TILE), inner)
    there = pl.ds(pl.multiple_of(inner * (1 - core), TILE), inner)
    solid_there = (1 - hole_ref[pl.ds(pl.multiple_of(end + inner * (1 - core), TILE), inner)]).astype(F32)
    for q in range(comps):
        prec, side, residual = returned(back_ref, sent_ref, solid_there, q, inner)
        prec_out[q, here] = own_ref[pl.ds(q * inner, inner), :]
        prec_out[q, there, :width] = prec
        prec_out[q, there, width:] = side
        residual_out[q, here] = residual_ref[q]
        residual_out[q, there] = residual
    low, high = end + TILE, slab - end - TILE
    core_rows = slice(TILE, 2 * inner - TILE)
    solid = (1 - hole_ref[low:high]).astype(F32)
    factor = factor_ref[low:high]
    sums = [jnp.zeros((TILE, width), F32) for _ in range(5)]
    for q in range(comps):
        fields = {k: prec_out[k, :, :width] for k in (q, q ^ 1)}
        field, image = image_rows(
            q, fields, prec_out[q, core_rows, width:], stiff_ref[q, low:high], solid, factor, 0.0, 0.0, core_rows
        )
        image_ref[q] = image
        sums = add_sums(sums, residual_out[q, core_rows], field, image)
    found = []
    for q in range(comps):
        rows = pl.ds(q * end, end)
        far = own_ends_ref[pl.ds(comps * end + q, 1), :width]
        found.append((own_ends_ref[rows, :width], own_ends_ref[rows, width:], far, residual_ends_ref[q]))
    images, sums = end_image(
        core, end, comps, found, prec_out, residual_out, stiff_ref, hole_ref, factor_ref, sums
    )
    for q in range(comps):
        image_ends_ref[q] = images[q]
    for i, total in enumerate(sums):
        sums_ref[pl.ds(i * TILE, TILE), :] = total


def late_kernel(
    end, comps, stiff_ref, hole_ref, factor_ref, inner_ref, inner_residual_ref,
    own_ref, back_ref, residual_ref, sent_ref, partial_ref, image_own_ref,
    prec_out, residual_out, image_ref, sums_ref,
):
    slab, width = hole_ref.shape
    reach = end + TILE
    core = lax.axis_index("sec") % 2
    other = 1 - core
    solid = (1 - hole_ref[pl.ds(pl.multiple_of((slab - end) * other, TILE), end), :]).astype(F32)
    sums = [partial_ref[pl.ds(i * TILE, TILE), :] for i in range(5)]
    here, there = [pl.ds(pl.multiple_of(end * h, TILE), end) for h in (core, other)]
    found = []
    for q in range(comps):
        prec, side, residual = returned(back_ref, sent_ref, solid, q, end)
        found.append((prec, side, back_ref[pl.ds(comps * end + q, 1), :width], residual))
        prec_out[q, there] = prec
        residual_out[q, there] = residual
        prec_out[q, here] = own_ref[pl.ds(q * end, end), :width]
        residual_out[q, here] = residual_ref[q]
        image_ref[q, pl.ds(pl.multiple_of(reach * core, TILE), reach)] = image_own_ref[q]
    images, sums = end_image(
        other, end, comps, found, inner_ref, inner_residual_ref, stiff_ref, hole_ref, factor_ref, sums
    )
    for q in range(comps):
        image_ref[q, pl.ds(pl.multiple_of(reach * other, TILE), reach)] = images[q]
    row = jnp.zeros((1, LANES), F32)
    spot = lanes_of((1, LANES))
    for i, value in enumerate(sums):
        value = jnp.sum(jnp.sum(value, axis=0, keepdims=True), axis=1, keepdims=True)
        row = jnp.where(spot == i, value, row)
    sums_ref[...] = jnp.broadcast_to(row, sums_ref.shape)


def update_kernel(
    end, comps, cell_total, disp_ref, gathered_ref, inner_ref, inner_residual_ref, inner_image_ref,
    ends_ref, ends_residual_ref, ends_image_ref, disp_out, residual_out, stats_out,
):
    slab, width = disp_ref.shape[1:]
    values = jnp.sum(gathered_ref[...], axis=0, keepdims=True) * F32(1.0 / cell_total)
    rz, zq, rr, ri, ii = [values[:, i : i + 1] for i in range(5)]
    alpha = rz / zq
    square = rr + alpha * (alpha * ii - 2.0 * ri)
    stats_out[...] = jnp.concatenate([rz, zq, square], axis=1)
    reach = end + TILE
    inner = slice(end, slab - end)
    for q in range(comps):
        disp_out[q, :end] = disp_ref[q, :end] + alpha * ends_ref[q, :end]
        disp_out[q, inner] = disp_ref[q, inner] + alpha * inner_ref[q, :, :width]
        disp_out[q, slab - end :] = disp_ref[q, slab - end :] + alpha * ends_ref[q, end:]
        image = jnp.concatenate([ends_image_ref[q, :reach], inner_image_ref[q], ends_image_ref[q, reach:]], axis=0)
        residual_out[q, :end] = ends_residual_ref[q, :end] - alpha * image[:end]
        residual_out[q, inner] = inner_residual_ref[q] - alpha * image[inner]
        residual_out[q, slab - end :] = ends_residual_ref[q, end:] - alpha * image[slab - end :]


VMEM = pl.BlockSpec(memory_space=pltpu.VMEM)
SMEM = pl.BlockSpec(memory_space=pltpu.SMEM)
HBM = pl.BlockSpec(memory_space=pltpu.HBM)
FULL = 60


def call(kernel, name, out_shapes, in_specs, flops, moved, scratch=(), grant=32, out_specs=None):
    return pl.pallas_call(
        kernel,
        out_shape=[jax.ShapeDtypeStruct(s, F32) for s in out_shapes],
        in_specs=in_specs,
        out_specs=out_specs or [VMEM] * len(out_shapes),
        scratch_shapes=list(scratch),
        compiler_params=pltpu.CompilerParams(vmem_limit_bytes=grant * 1024 * 1024),
        cost_estimate=pl.CostEstimate(flops=flops, bytes_accessed=moved, transcendentals=0),
        name=name,
    )


def transform_call(blocks, tables, hole, edge, main, edge_at, hole_at, comps, width, slab, weight):
    around = SECTORS * width
    at_end = edge is not None
    total = comps * main
    out_rows = total + (TILE if at_end else 0)
    rows = total + (2 * TILE if at_end else 0)
    operands = list(blocks) + list(tables) + [hole] + ([edge] if at_end else [])
    shapes = [(out_rows, width + LANES), (comps, main, width), (out_rows, width + LANES)]
    return call(
        functools.partial(transform_kernel, comps, main, at_end, edge_at, hole_at), "transform",
        ([] if at_end else [(slab, LANES)]) + shapes, [VMEM] * len(operands),
        weight * 2 * total * 3 * around * 3 * width, weight * 4 * total * width * 8,
        [pltpu.VMEM((rows, 8 * width), BF16), pltpu.VMEM((rows // TILE, TILE, around), F32),
         pltpu.VMEM((rows, 2 * around), BF16), pltpu.VMEM((total, LANES), F32)],
    )(*operands)


def after_all(x, *others):
    return lax.optimization_barrier((x, *others))[0]


def shards(load, disp, stiff, hole, section_class, class_table, precond):
    slab, comps, width = disp.shape
    ax, sec = lax.axis_size("ax"), lax.axis_size("sec")
    around = width * sec
    cell_total = slab * ax * comps * around
    end = slab // 16 * 2
    inner = slab // 2 - end
    load, disp, stiff = [x.transpose(1, 0, 2) for x in (load, disp, stiff)]
    forward, even, odd, beyond = harmonic_tables(width)
    block = 4 * comps * slab * width
    classes = section_class.reshape(1, slab)

    sent = (comps * inner + TILE, width)
    ends_shape = (2, comps * end + 2 * TILE, width)
    shapes = [sent, ends_shape, (slab, LANES), (2 * TILE, width), (2 * TILE, width)]
    small = [pltpu.SMEM(class_table.shape, F32), pltpu.VMEM((1, slab), jnp.int32)]
    arguments = (class_table, classes, load, disp, stiff, hole)
    reach = slab // 2 + TILE
    (keep,) = call(
        functools.partial(first_kernel, end, comps, ax), "first",
        [sent], [HBM] * 6, 10 * comps * inner * width, block,
        small + [pltpu.VMEM((comps, rows, width), F32) for rows in (inner, reach, inner)]
        + [pltpu.VMEM((reach, width), jnp.int32), pltpu.VMEM(sent, F32), pltpu.VMEM((slab, LANES), F32)]
        + [pltpu.SemaphoreType.DMA((3 + 3 * comps // 2,)), pltpu.SemaphoreType.DMA((1 + comps,))],
        FULL, [HBM],
    )(*arguments)
    other, edge, factor, near, other_side = call(
        functools.partial(second_kernel, end, comps, ax), "second",
        shapes, [HBM] * 6, 10 * comps * slab * width, 2 * block,
        small + [pltpu.VMEM((comps, slab, width), F32)] * 3 + [pltpu.VMEM((slab, width), jnp.int32)]
        + [pltpu.VMEM((2,) + sent, F32)] + [pltpu.VMEM(shape, F32) for shape in shapes[1:3] + [(2, 2 * TILE, width)]]
        + [pltpu.SemaphoreType.DMA((3 + 3 * comps // 2,)), pltpu.SemaphoreType.DMA((6 + comps,))],
        FULL, [HBM] * len(shapes),
    )(*arguments)

    def to(x, mask):
        return lax.ppermute(x, "sec", [(i, i ^ mask) for i in range(sec)])

    def gather(keep, other):
        return keep, to(other, 1), to(keep, 2), to(other, 3)

    blocks = gather(keep, other)
    near = lax.ppermute(near, "ax", [(i, i ^ 1) for i in range(ax)])
    other_side = lax.ppermute(other_side, "ax", [(i, ((i + 1) ^ 1) - 1) for i in range(1, ax - 1)])
    weight, beyond_weight = call(
        fold_kernel, "fold", [(comps * comps, TILE, 5 * width // 2), (comps, TILE, 5 * width // 2)], [VMEM] * 5,
        1, 1,
    )(precond, forward, even, odd, beyond)
    rows = (comps * end + TILE, width)
    keep_ends, other_ends = call(
        functools.partial(ends_kernel, comps), "ends",
        [rows, rows], [VMEM] * 3, 2 * comps * end * width, 16 * comps * end * width, [pltpu.VMEM((2,) + rows, F32)],
    )(after_all(edge, weight), near, other_side)
    end_blocks = gather(keep_ends, other_ends)
    tables = (forward, even, odd, beyond, weight, beyond_weight)

    across = after_all(blocks[2], keep_ends, weight)
    edge, own, residual, back = transform_call(
        (keep, blocks[1], across, blocks[3]), tables, hole, None, inner, 0, (end, inner), comps, width, slab, 0
    )
    back = to(back, 1)
    across = after_all(end_blocks[2], own)
    own_ends, residual_ends, back_ends = transform_call(
        (keep_ends, end_blocks[1], across, end_blocks[3]), tables, hole, edge, end, inner, (0, slab - end),
        comps, width, slab, 100,
    )
    back_ends = to(back_ends, 1)
    prec, residual, image, partial, image_own = call(
        functools.partial(early_kernel, end, comps), "early",
        [(comps, 2 * inner, width + LANES), (comps, 2 * inner, width), (comps, 2 * (inner - TILE), width),
         (5 * TILE, width), (comps, end + TILE, width)],
        [VMEM] * 9, 30 * comps * slab * width, 4 * block,
    )(stiff, hole, factor, own, back, residual, other, own_ends, residual_ends)
    prec_ends, residual_ends, image_ends, sums = call(
        functools.partial(late_kernel, end, comps), "late",
        [(comps, 2 * end, width), (comps, 2 * end, width), (comps, 2 * (end + TILE), width), (ax * sec, LANES)],
        [VMEM] * 11, 8 * comps * slab * width, block,
    )(stiff, hole, factor, prec, residual, own_ends, back_ends, residual_ends, other_ends, partial, image_own)
    gathered = lax.all_to_all(sums, ("ax", "sec"), 0, 0, tiled=True)
    disp_new, residual_new, stats = call(
        functools.partial(update_kernel, end, comps, cell_total), "update",
        [(comps, slab, width), (comps, slab, width), (1, 3)], [VMEM] * 8,
        4 * comps * slab * width, 6 * block,
    )(disp, gathered, prec, residual, image, prec_ends, residual_ends, image_ends)
    return disp_new.transpose(1, 0, 2), residual_new.transpose(1, 0, 2), stats.reshape(3)


def solution(mesh):
    in_specs = (
        P("ax", None, "sec"),
        P("ax", None, "sec"),
        P("ax", None, "sec"),
        P("ax", "sec"),
        P("ax"),
        P(),
        P(),
    )
    out_specs = (P("ax", None, "sec"), P("ax", None, "sec"), P())
    return jax.shard_map(shards, mesh=mesh, in_specs=in_specs, out_specs=out_specs, check_vma=False)
```

```python
import functools

import jax
import jax.numpy as jnp
import ml_dtypes
import numpy as np
from jax import lax
from jax.experimental import pallas as pl
from jax.experimental.pallas import tpu as pltpu
from jax.sharding import PartitionSpec as P

F32 = jnp.float32
BF16 = jnp.bfloat16
SECTORS = 4
TILE = 8
LANES = 128


def two_parts(table):
    high = table.astype(ml_dtypes.bfloat16)
    low = (table - high.astype(np.float64)).astype(ml_dtypes.bfloat16)
    return np.stack([high, low])


@functools.lru_cache(maxsize=None)
def harmonic_tables(width):
    around = SECTORS * width
    half = width // 2
    zero = [("c", 4 * q) for q in range(half + 1)] + [("s", 4 * q) for q in range(1, half)]
    two = [(f, 4 * q + 2) for f in "cs" for q in range(half)]
    one = [(f, 8 * q + 1) for f in "cs" for q in range(half)]
    five = [(f, 8 * q + 5) for f in "cs" for q in range(half)]
    columns = zero + two + one + five
    harmonic = np.array([k for _, k in columns], dtype=np.int64)
    is_sin = np.array([f == "s" for f, _ in columns])

    def wave(place, shift):
        angle = 2.0 * np.pi / around * ((place[:, None] * harmonic[None, :]) % around)
        return np.cos(angle - shift)

    place = np.arange(width)
    shift = np.where(is_sin, np.pi / 2, 0.0)[None, :]
    direct = wave(place, shift)
    turned = np.concatenate([direct[:half], wave(place[:half], shift - np.pi / 2)], axis=0)
    forward = [direct[:, :width], direct[:, width : 2 * width]]
    forward += [turned[:, 2 * width : 3 * width], turned[:, 3 * width :]]
    ends = np.array([around - 1, 2 * width, around - width - 1, width])
    beyond = np.repeat(wave(ends, shift).astype(np.float32)[:, None, :], TILE, axis=1)
    odd = np.concatenate([direct.T, wave(place + width, shift).T], axis=1)[2 * width :]
    return (
        np.stack([two_parts(t) for t in forward]),
        np.stack([two_parts(t) for t in (direct.T[:width], direct.T[width : 2 * width])]),
        two_parts(odd),
        beyond,
    )


def split(x):
    high = x.astype(BF16)
    return high, (x - high.astype(F32)).astype(BF16)


def product(high, low, table_ref):
    left = jnp.concatenate([high, low, high], axis=1)
    table = jnp.concatenate([table_ref[0], table_ref[0], table_ref[1]], axis=0)
    return jnp.dot(left, table, preferred_element_type=F32)


def lanes_of(shape):
    return lax.broadcasted_iota(jnp.int32, shape, len(shape) - 1)


def rows_of(shape):
    return lax.broadcasted_iota(jnp.int32, shape, len(shape) - 2)


def beside_sum(x, before, after):
    lane = lanes_of(x.shape)
    size = x.shape[-1]
    left = jnp.where(lane == 0, before, pltpu.roll(x, 1, x.ndim - 1))
    right = jnp.where(lane == size - 1, after, pltpu.roll(x, size - 1, x.ndim - 1))
    return left + right


def stacked_sum(x, before=0.0, after=0.0):
    row = rows_of(x.shape)
    size = x.shape[0]
    up = jnp.where(row == 0, before, pltpu.roll(x, 1, 0))
    down = jnp.where(row == size - 1, after, pltpu.roll(x, size - 1, 0))
    return up + down


def fold_kernel(precond_ref, *refs):
    out_ref, beyond_ref = refs[-2:]
    comps = precond_ref.shape[0]
    value = jnp.concatenate([precond_ref[q] for q in range(comps)], axis=0)
    pairs, around = value.shape
    high = value.astype(BF16)
    rest = value - high.astype(F32)
    middle = rest.astype(BF16)
    low = (rest - middle.astype(F32)).astype(BF16)
    half = around // 8
    row, step = rows_of((around, half)), lanes_of((around, half))
    kinds = []
    for k in (4 * step, 4 * step + 2, 8 * step + 1, 8 * step + 5):
        kinds.append(jnp.where((row == k) | (row == around - k), F32(1.0 / around), 0.0).astype(BF16))
    fold = jnp.concatenate(kinds, axis=1)
    terms = [jnp.dot(t, fold, preferred_element_type=F32) for t in (high, middle, low)]
    folded = terms[0] + (terms[1] + terms[2])
    zero = folded[:, :half]
    top = value[:, around // 2 : around // 2 + 1] * F32(1.0 / around)
    other = jnp.where(lanes_of(zero.shape) == 0, top, zero)
    folded = jnp.concatenate([zero, other, folded[:, half:]], axis=1)
    for i in range(pairs):
        out_ref[i] = jnp.broadcast_to(folded[i : i + 1], out_ref.shape[1:])
    rest = [jnp.zeros((TILE - comps, folded.shape[1]), F32)]
    for p in range(comps):
        beyond_ref[p] = jnp.concatenate([folded[i : i + 1] for i in range(p, pairs, comps)] + rest, axis=0)


def factor_columns(table_ref, class_ref, ax_size, comps):
    classes = class_ref[...]
    slab = classes.shape[1]
    position = lax.axis_index("ax") * slab + lanes_of(classes.shape)
    taper = 1.0 + 2.0 * position.astype(F32) / F32(ax_size * slab - 1)
    rows = []
    for q in range(comps):
        value = jnp.zeros(classes.shape, F32)
        for kind in range(table_ref.shape[0]):
            value = jnp.where(classes == kind, table_ref[kind, q], value)
        rows.append(value * taper)
    rows.append(jnp.zeros((LANES - comps, slab), F32))
    return jnp.concatenate(rows, axis=0).T


def local_part(q, block, inner, solid, factor, load, stiff, other):
    field = block[inner]
    beside = stacked_sum(block)[inner] + beside_sum(field, 0.0, 0.0)
    stiffness = stiff * factor[:, q : q + 1]
    image = (stiffness + 4.5) * field - beside - 0.5 * other[inner]
    return solid * (load - image)


def edge_rows(fields, solid):
    rows, width = solid.shape
    sources = fields + [solid] * (TILE - len(fields))
    lane = lanes_of((rows, LANES))
    table = jnp.zeros((rows, LANES), F32)
    for i, x in enumerate(sources):
        table = jnp.where(lane == i, pltpu.roll(x[:, :LANES], i, 1) if i else x[:, :LANES], table)
        table = jnp.where(lane == TILE + i, pltpu.roll(x[:, width - LANES :], TILE + i + 1, 1), table)
    if rows < LANES:
        table = jnp.concatenate([table, jnp.zeros((LANES - rows, LANES), F32)], axis=0)
    table = table.T
    return table[:TILE], table[TILE : 2 * TILE]


def copy(src, dst, sem):
    moving = pltpu.make_async_copy(src, dst, sem)
    moving.start()
    return moving


def first_kernel(
    end, comps, ax_size, table_ref, class_ref, load_ref, disp_ref, stiff_ref, hole_ref, keep_ref,
    table_in, class_in, load_in, disp_in, stiff_in, hole_in, keep_out, factor_in, in_sems, out_sems,
):
    slab, width = hole_ref.shape
    half = slab // 2
    inner, reach = half - end, half + TILE
    core = lax.axis_index("sec") % 2
    base = pl.multiple_of((half - TILE) * core, TILE)
    start = pl.multiple_of(end + inner * core, TILE)
    here = pl.ds(pl.multiple_of(end - (end - TILE) * core, TILE), inner)
    around = pl.ds(pl.multiple_of(end - TILE - (end - TILE) * core, TILE), inner + 2 * TILE)
    tail = pl.ds(pl.multiple_of((reach - end) * core, TILE), end)
    small = [
        copy(class_ref, class_in, in_sems.at[0]),
        copy(table_ref, table_in, in_sems.at[1]),
        copy(hole_ref.at[pl.ds(base, reach)], hole_in, in_sems.at[2]),
    ]
    pairs = comps // 2
    moving = []
    for g in range(pairs):
        both = pl.ds(2 * g, 2)
        arrays = (
            (disp_ref.at[both, pl.ds(base, reach)], disp_in), (load_ref.at[both, pl.ds(start, inner)], load_in),
            (stiff_ref.at[both, pl.ds(start, inner)], stiff_in),
        )
        moving.append([copy(src, dst.at[both], in_sems.at[3 + 3 * g + k]) for k, (src, dst) in enumerate(arrays)])
    for one in small:
        one.wait()
    factor_in[...] = factor_columns(table_in, class_in, ax_size, comps)
    factor = factor_in[pl.ds(start, inner), :]
    solid = (1 - hole_in[here, :]).astype(F32)
    solid_tail = (1 - hole_in[tail, :]).astype(F32)
    inside = slice(TILE, TILE + inner)
    leaving = []
    for g in range(pairs):
        moving[g][0].wait()
        if g == pairs - 1:
            fields = [jnp.concatenate([disp_in[q, here], disp_in[q, tail]], axis=0) for q in range(comps)]
            last = pl.ds(comps * inner, TILE)
            keep_out[last, :] = jnp.concatenate(
                edge_rows(fields, jnp.concatenate([solid, solid_tail], axis=0)), axis=1
            )
            leaving.append(copy(keep_out.at[last], keep_ref.at[last], out_sems.at[comps]))
        moving[g][1].wait()
        moving[g][2].wait()
        for q in (2 * g, 2 * g + 1):
            rows = pl.ds(q * inner, inner)
            keep_out[rows, :] = local_part(
                q, disp_in[q, around], inside, solid, factor, load_in[q], stiff_in[q], disp_in[q ^ 1, around]
            )
            leaving.append(copy(keep_out.at[rows], keep_ref.at[rows], out_sems.at[q]))
    for one in leaving:
        one.wait()


def second_kernel(
    end, comps, ax_size, table_ref, class_ref, load_ref, disp_ref, stiff_ref, hole_ref,
    other_ref, ends_ref, factor_ref, near_ref, next_ref,
    table_in, class_in, load_in, disp_in, stiff_in, hole_in, inner_out, ends_out, factor_out, message_out,
    in_sems, out_sems,
):
    slab, width = hole_ref.shape
    half = slab // 2
    inner = half - end
    core = lax.axis_index("sec") % 2

    small = [
        copy(class_ref, class_in, in_sems.at[0]), copy(table_ref, table_in, in_sems.at[1]), copy(hole_ref, hole_in, in_sems.at[2])
    ]
    pairs = comps // 2
    moving = []
    for g in range(pairs):
        both = pl.ds(2 * g, 2)
        arrays = ((disp_ref, disp_in), (load_ref, load_in), (stiff_ref, stiff_in))
        moving.append([copy(src.at[both], dst.at[both], in_sems.at[3 + 3 * g + k]) for k, (src, dst) in enumerate(arrays)])
    for one in small:
        one.wait()
    factor_out[...] = factor_columns(table_in, class_in, ax_size, comps)
    leaving = [copy(factor_out, factor_ref, out_sems.at[0])]
    solid = (1 - hole_in[...]).astype(F32)
    spare = TILE - comps
    for h, row in ((0, 0), (1, slab - 1)):
        message_out[h, comps:TILE, :] = jnp.broadcast_to(solid[row : row + 1], (spare, width))
        message_out[h, TILE + comps :, :] = jnp.zeros((spare, width), F32)
    factor = factor_out[...]

    def ordered(x):
        return jnp.concatenate([x[end:half], x[:end], x[half:]], axis=0)

    for g in range(pairs):
        moving[g][0].wait()
        if g == pairs - 1:
            edges = edge_rows([ordered(disp_in[q]) for q in range(comps)], ordered(solid))
            last = pl.ds(comps * inner, TILE)
            for h in range(2):
                inner_out[h, last, :] = jnp.concatenate(
                    [pltpu.roll(x, (LANES - half * h) % LANES, 1) for x in edges], axis=1
                )
            leaving.append(copy(inner_out.at[1 - core, last], other_ref.at[last], out_sems.at[2]))
        moving[g][1].wait()
        moving[g][2].wait()
        for q in (2 * g, 2 * g + 1):
            field = disp_in[q]
            part = local_part(q, field, slice(0, slab), solid, factor, load_in[q], stiff_in[q], disp_in[q ^ 1])
            rows = pl.ds(q * inner, inner)
            inner_out[0, rows, :] = part[end:half]
            inner_out[1, rows, :] = part[half : slab - end]
            rows = pl.ds(q * end, end)
            ends_out[0, rows, :] = part[:end]
            ends_out[1, rows, :] = part[slab - end :]
            for h, row in ((0, slice(0, 1)), (1, slice(slab - 1, slab))):
                message_out[h, q : q + 1, :] = part[row]
                message_out[h, TILE + q : TILE + q + 1, :] = field[row]
        rows = pl.ds(2 * g * inner, 2 * inner)
        leaving.append(copy(inner_out.at[1 - core, rows], other_ref.at[rows], out_sems.at[4 + 2 * g]))
    count = 3 + 2 * pairs
    side = lax.axis_index("ax") % 2
    leaving.append(copy(message_out.at[1 - side], near_ref, out_sems.at[count]))
    leaving.append(copy(message_out.at[side], next_ref, out_sems.at[count + 1]))
    for h in range(2):
        ends_out[h, pl.ds(comps * end, 2 * TILE), :] = message_out[h]
    leaving.append(copy(ends_out, ends_ref, out_sems.at[count + 2]))
    for one in leaving:
        one.wait()


def ends_kernel(comps, ends_ref, near_ref, next_ref, keep_ref, other_ref, out_ref):
    rows = (ends_ref.shape[1] - 2 * TILE) // comps
    width = ends_ref.shape[2]
    row = rows_of((rows, width))
    spot, place = rows_of((TILE, width)), lanes_of((TILE, width))
    core = lax.axis_index("sec") % 2
    odd = lax.axis_index("ax") % 2 == 1
    near, other = near_ref[...], next_ref[...]
    for h, far, at in ((0, jnp.where(odd, near, other), 0), (1, jnp.where(odd, other, near), rows - 1)):
        own_ref = ends_ref.at[h, pl.ds(comps * rows, 2 * TILE)]
        solid_own = own_ref[comps : comps + 1]
        for q in range(comps):
            part = ends_ref[h, pl.ds(q * rows, rows), :]
            part = part + jnp.where(row == at, solid_own * far[TILE + q : TILE + q + 1], 0.0)
            out_ref[h, pl.ds(q * rows, rows), :] = part
        solid_far, disp_far = far[comps : comps + 1], far[TILE:]
        edges = jnp.where(place == spot, disp_far[:, :1], 0.0)
        edges = edges + jnp.where(place == spot + TILE, disp_far[:, width - 1 :], 0.0)
        edges = jnp.sum(edges, axis=0, keepdims=True)
        beyond = far[:TILE] + solid_far * own_ref[TILE:]
        beyond = jnp.where(spot < comps, beyond, jnp.where(spot == TILE - 1, edges, solid_far))
        out_ref[h, pl.ds(comps * rows, TILE), :] = beyond
    keep_ref[...] = out_ref[core]
    other_ref[...] = out_ref[1 - core]


def in_order(odd, own, core, across, both):
    return own, jnp.where(odd, both, core), across, jnp.where(odd, core, both)


def butterfly(x0, x1, x2, x3):
    even, other = x0 + x2, x1 + x3
    return even + other, even - other, x0 - x2, x1 - x3


def edge_table(odd, blocks):
    tiles = in_order(odd, *blocks)
    left = [t[:, :LANES] for t in tiles]
    right = [t[:, LANES:] for t in tiles]
    solid = TILE - 1
    at_left = [left[s][solid:] * right[s - 1] for s in range(SECTORS)]
    at_right = [right[s][solid:] * left[(s + 1) % SECTORS] for s in range(SECTORS)]
    stack = []
    for one, other in zip(butterfly(*at_left), butterfly(*at_right)):
        stack += [one, other]
    stack += [at_left[0], at_right[0]]
    stack += [jnp.where(odd, at_left[3], at_left[1]), jnp.where(odd, at_right[3], at_right[1])]
    stack += [right[3], left[1], jnp.where(odd, right[2], right[0]), jnp.where(odd, left[0], left[2])]
    return jnp.concatenate(stack, axis=0).T


def transform_kernel(
    comps, main, at_end, edge_at, hole_at, own_ref, core_ref, across_ref, both_ref,
    forward_ref, even_ref, odd_ref, beyond_ref, weight_ref, beyond_weight_ref, hole_ref, edge_ref,
    prec_ref, residual_ref, back_ref, left_ref, spectrum_ref, scaled_ref, halo_ref,
):
    width = own_ref.shape[1]
    half = width // 2
    core = lax.axis_index("sec") % 2
    odd = core == 1
    sign = jnp.where(odd, -1.0, 1.0)
    rows = main
    total = comps * rows
    group = 1 if rows % 16 == 0 else 2
    sources = (own_ref, core_ref, across_ref, both_ref)
    start, stride = hole_at
    solid = (1 - hole_ref[pl.ds(pl.multiple_of(start + stride * core, TILE), main)]).astype(F32)
    if not at_end:
        edge_ref[...] = edge_table(odd, [r[total : total + TILE] for r in sources])
    edge = edge_ref[pl.ds(edge_at, main), :]
    lane = lanes_of((main, LANES))
    first = lane == 0
    last = lane == LANES - 1

    def edge_column(tile, q):
        column = tile * TILE + q
        return edge[:, column : column + 1]

    def with_edges(x, array, q):
        head = x[:, :LANES] + jnp.where(first, edge_column(2 * array, q), 0.0)
        tail = x[:, -LANES:] + jnp.where(last, edge_column(2 * array + 1, q), 0.0)
        middle = [x[:, LANES:-LANES]] if width > 2 * LANES else []
        return jnp.concatenate([head] + middle + [tail], axis=1)

    def arrays_of(q):
        at = q * rows
        own, core, across, both = [r[pl.ds(at, main), :] for r in sources]
        arrays = butterfly(own, core, across, both)
        arrays = arrays[:3] + (sign * arrays[3],)
        arrays = [with_edges(x, i, q) for i, x in enumerate(arrays)]
        residual_ref[q] = with_edges(own, 4, q)
        return turned(*arrays)

    def turned(y0, y2, real, imag):
        turned_real = (real[:, half:] - imag[:, half:]) * F32(np.sqrt(0.5))
        turned_imag = (real[:, half:] + imag[:, half:]) * F32(np.sqrt(0.5))
        plus = jnp.concatenate([real[:, :half] + turned_real, imag[:, :half] + turned_imag], axis=1)
        minus = jnp.concatenate([real[:, :half] - turned_real, imag[:, :half] - turned_imag], axis=1)
        return y0, y2, plus, minus

    def arrays_beyond():
        tiles = in_order(odd, *[r[pl.ds(total, TILE), :] for r in sources])
        spot, place = rows_of((TILE, width)), lanes_of((TILE, width))

        def column(tile, at):
            return jnp.sum(jnp.where(place == spot + at, tile[TILE - 1 :], 0.0), axis=1, keepdims=True)

        fixed = []
        for s in range(SECTORS):
            beside = jnp.where(place == 0, column(tiles[s - 1], TILE), 0.0)
            beside = beside + jnp.where(place == width - 1, column(tiles[(s + 1) % SECTORS], 0), 0.0)
            value = tiles[s] + tiles[s][comps : comps + 1] * beside
            fixed.append(jnp.where(spot < comps, value, 0.0))
        return turned(*butterfly(*fixed))

    def put(at, arrays):
        for i, x in enumerate(arrays):
            high, low = split(x)
            left_ref[at, 2 * i * width : (2 * i + 1) * width] = high
            left_ref[at, (2 * i + 1) * width : (2 * i + 2) * width] = low

    for begin in range(0, comps, group):
        found = [arrays_of(q) for q in range(begin, begin + group)]
        put(pl.ds(begin * rows, group * rows), [jnp.concatenate([x[i] for x in found], axis=0) for i in range(4)])
    if at_end:
        put(pl.ds(total, 2 * TILE), [jnp.concatenate([x, jnp.zeros_like(x)], axis=0) for x in arrays_beyond()])
    height = left_ref.shape[0]

    for i in range(4):
        high = left_ref[:, 2 * i * width : (2 * i + 1) * width]
        low = left_ref[:, (2 * i + 1) * width : (2 * i + 2) * width]
        part = product(high, low, forward_ref.at[i])
        spectrum_ref[:, :, i * width : (i + 1) * width] = part.reshape(height // TILE, TILE, width)

    around = SECTORS * width

    def scale(row, count):
        tiles = count // TILE

        def spectrum(p, lanes):
            return spectrum_ref[pl.ds((p * rows + row) // TILE, tiles), :, lanes]

        for begin in range(0, comps, group):
            halo = [[None, None] for _ in range(group)]
            for k in range(4):
                for h in range(2):
                    lanes = slice(k * width + h * half, k * width + (h + 1) * half)
                    kind = h if k == 0 else k + 1
                    values = []
                    for i in range(group):
                        value = None
                        for p in range(comps):
                            weight = weight_ref[(begin + i) * comps + p, :, kind * half : (kind + 1) * half]
                            term = spectrum(p, lanes) * weight
                            value = term if value is None else value + term
                        for side in range(2):
                            term = value * beyond_ref[2 * core + side, :, lanes]
                            halo[i][side] = term if halo[i][side] is None else halo[i][side] + term
                        values.append(value.reshape(count, half))
                    high, low = split(values[0] if group == 1 else jnp.concatenate(values, axis=0))
                    at = pl.ds(begin * rows + row, group * count)
                    scaled_ref[at, lanes] = high
                    scaled_ref[at, around + lanes.start : around + lanes.stop] = low
            for i in range(group):
                before, after = [jnp.sum(x, axis=2, keepdims=True) for x in halo[i]]
                tile = jnp.where(lanes_of((tiles, TILE, LANES)) == 0, before, after)
                halo_ref[pl.ds((begin + i) * rows + row, count), :] = tile.reshape(count, LANES)

    def scale_beyond():
        at = pl.ds(total, 2 * TILE)
        for k in range(4):
            for h in range(2):
                lanes = slice(k * width + h * half, k * width + (h + 1) * half)
                kind = h if k == 0 else k + 1
                parts = spectrum_ref[total // TILE, :, lanes]
                value = None
                for p in range(comps):
                    term = parts[p : p + 1] * beyond_weight_ref[p, :, kind * half : (kind + 1) * half]
                    value = term if value is None else value + term
                high, low = split(jnp.concatenate([value, jnp.zeros_like(value)], axis=0))
                scaled_ref[at, lanes] = high
                scaled_ref[at, around + lanes.start : around + lanes.stop] = low

    if at_end:
        scale_beyond()
    step = rows if group > 1 else 32
    for row in range(0, rows, step):
        scale(row, min(step, rows - row))

    def inverse(columns, table_ref):
        low = scaled_ref[:, around + columns.start : around + columns.stop]
        return product(scaled_ref[:, columns], low, table_ref)

    zero = inverse(slice(0, width), even_ref.at[0])
    two = inverse(slice(width, 2 * width), even_ref.at[1])
    odds = inverse(slice(2 * width, around), odd_ref)
    own_all = zero + two + odds[:, :width]
    other_all = zero - two + sign * odds[:, width:]
    for q in range(comps):
        at = q * rows
        own, other = own_all[at : at + rows], other_all[at : at + rows]
        side = halo_ref[pl.ds(at, rows), :]
        far_before, far_after = side[:, :1], side[:, 1:2]
        own_before = jnp.where(odd, other[:, width - 1 :], far_before)
        own_after = jnp.where(odd, far_after, other[:, :1])
        other_before = jnp.where(odd, far_before, own[:, width - 1 :])
        other_after = jnp.where(odd, own[:, :1], far_after)
        solids = [edge_column(tile, TILE - 1) for tile in (12, 13, 14, 15)]
        at = pl.ds(at, rows)
        prec_ref[at, :width] = own * solid
        prec_ref[at, width:] = jnp.where(first, own_before * solids[0], own_after * solids[1])
        tile = jnp.where(first, other_before * solids[2], other_after * solids[3])
        tile = jnp.where(lane == 2, edge_column(10, q), jnp.where(lane == 3, edge_column(11, q), tile))
        back_ref[at, :width] = other
        back_ref[at, width:] = tile
    if at_end:
        at = pl.ds(total, TILE)
        for ref, result, source in ((prec_ref, own_all, own_ref), (back_ref, other_all, core_ref)):
            ref[at, :width] = result[total : total + TILE] * source[pl.ds(total + comps, 1), :]
            ref[at, width:] = jnp.zeros((TILE, LANES), F32)


def image_rows(q, fields, tile, stiff, solid, factor, before, after, inner):
    field = fields[q][inner]
    beside = beside_sum(field, tile[:, :1], tile[:, 1:2])
    beside = beside + stacked_sum(fields[q], before, after)[inner]
    stiffness = stiff * factor[:, q : q + 1]
    return field, solid * ((stiffness + 4.5) * field - beside - 0.5 * fields[q ^ 1][inner])


def add_sums(sums, residual, field, image):
    rows, width = field.shape
    pairs = ((residual, field), (field, image), (residual, residual), (residual, image), (image, image))
    return [
        total + jnp.sum((x * y).reshape(rows // TILE, TILE, width), axis=0)
        for total, (x, y) in zip(sums, pairs)
    ]


def returned(back, sent, solid, q, rows):
    width = sent.shape[1]
    side = back[pl.ds(q * rows, rows), width:]
    residual = sent[pl.ds(q * rows, rows), :]
    lane = lanes_of(residual.shape)
    residual = residual + jnp.where(lane == 0, side[:, 2:3], 0.0) + jnp.where(lane == width - 1, side[:, 3:4], 0.0)
    return back[pl.ds(q * rows, rows), :width] * solid, side, residual


def early_kernel(
    end, comps, stiff_ref, hole_ref, factor_ref, own_ref, back_ref, residual_ref, sent_ref,
    prec_out, residual_out, image_ref, sums_ref,
):
    slab, width = hole_ref.shape
    inner = slab // 2 - end
    core = lax.axis_index("sec") % 2
    here = pl.ds(pl.multiple_of(inner * core, TILE), inner)
    there = pl.ds(pl.multiple_of(inner * (1 - core), TILE), inner)
    solid_there = (1 - hole_ref[pl.ds(pl.multiple_of(end + inner * (1 - core), TILE), inner)]).astype(F32)
    for q in range(comps):
        prec, side, residual = returned(back_ref, sent_ref, solid_there, q, inner)
        prec_out[q, here] = own_ref[pl.ds(q * inner, inner), :]
        prec_out[q, there, :width] = prec
        prec_out[q, there, width:] = side
        residual_out[q, here] = residual_ref[q]
        residual_out[q, there] = residual
    low, high = end + TILE, slab - end - TILE
    core_rows = slice(TILE, 2 * inner - TILE)
    solid = (1 - hole_ref[low:high]).astype(F32)
    factor = factor_ref[low:high]
    sums = [jnp.zeros((TILE, width), F32) for _ in range(5)]
    for q in range(comps):
        fields = {k: prec_out[k, :, :width] for k in (q, q ^ 1)}
        field, image = image_rows(
            q, fields, prec_out[q, core_rows, width:], stiff_ref[q, low:high], solid, factor, 0.0, 0.0, core_rows
        )
        image_ref[q] = image
        sums = add_sums(sums, residual_out[q, core_rows], field, image)
    for i, total in enumerate(sums):
        sums_ref[pl.ds(i * TILE, TILE), :] = total


def late_kernel(
    end, comps, stiff_ref, hole_ref, factor_ref, inner_ref, inner_residual_ref,
    own_ref, back_ref, residual_ref, sent_ref, partial_ref,
    prec_out, residual_out, image_ref, sums_ref,
):
    slab, width = hole_ref.shape
    reach = end + TILE
    core = lax.axis_index("sec") % 2
    odd = core == 1
    solid = (1 - hole_ref[...]).astype(F32)
    factor = factor_ref[...]
    sums = [partial_ref[pl.ds(i * TILE, TILE), :] for i in range(5)]
    fields, tiles, beyond, residuals = [[], []], [[], []], [[], []], [[], []]
    for q in range(comps):
        solid_there = jnp.where(odd, solid[:end], solid[slab - end :])
        there, side, residual = returned(back_ref, sent_ref, solid_there, q, end)
        rows, far = pl.ds(q * end, end), pl.ds(comps * end + q, 1)
        here, own_side = own_ref[rows, :width], own_ref[rows, width:]
        far_here, far_there = own_ref[far, :width], back_ref[far, :width]
        for h, swap in ((0, odd), (1, core == 0)):
            prec = jnp.where(swap, there, here)
            tile = jnp.where(swap, side, own_side)
            rest = jnp.where(swap, residual, residual_ref[q])
            beyond[h].append(jnp.where(swap, far_there, far_here))
            rows = pl.ds(end * h, end)
            prec_out[q, rows] = prec
            residual_out[q, rows] = rest
            near = slice(0, 2 * TILE) if h == 0 else slice(-2 * TILE, None)
            close = slice(0, TILE) if h == 0 else slice(-TILE, None)
            parts = [prec, inner_ref[q, near, :width]]
            sides = [tile, inner_ref[q, close, width:]]
            rests = [rest, inner_residual_ref[q, close]]
            order = slice(None) if h == 0 else slice(None, None, -1)
            fields[h].append(jnp.concatenate(parts[order], axis=0))
            tiles[h].append(jnp.concatenate(sides[order], axis=0))
            residuals[h].append(jnp.concatenate(rests[order], axis=0))
    for h in range(2):
        rows = slice(0, reach) if h == 0 else slice(slab - reach, slab)
        inner = slice(0, reach) if h == 0 else slice(TILE, None)
        for q in range(comps):
            before, after = (beyond[0][q], 0.0) if h == 0 else (0.0, beyond[1][q])
            field, image = image_rows(
                q, fields[h], tiles[h][q], stiff_ref[q, rows], solid[rows], factor[rows], before, after, inner
            )
            image_ref[q, pl.ds(reach * h, reach)] = image
            sums = add_sums(sums, residuals[h][q], field, image)
    row = jnp.zeros((1, LANES), F32)
    spot = lanes_of((1, LANES))
    for i, value in enumerate(sums):
        value = jnp.sum(jnp.sum(value, axis=0, keepdims=True), axis=1, keepdims=True)
        row = jnp.where(spot == i, value, row)
    sums_ref[...] = jnp.broadcast_to(row, sums_ref.shape)


def update_kernel(
    end, comps, cell_total, disp_ref, gathered_ref, inner_ref, inner_residual_ref, inner_image_ref,
    ends_ref, ends_residual_ref, ends_image_ref, disp_out, residual_out, stats_out,
):
    slab, width = disp_ref.shape[1:]
    values = jnp.sum(gathered_ref[...], axis=0, keepdims=True) * F32(1.0 / cell_total)
    rz, zq, rr, ri, ii = [values[:, i : i + 1] for i in range(5)]
    alpha = rz / zq
    square = rr + alpha * (alpha * ii - 2.0 * ri)
    stats_out[...] = jnp.concatenate([rz, zq, square], axis=1)
    reach = end + TILE
    inner = slice(end, slab - end)
    for q in range(comps):
        disp_out[q, :end] = disp_ref[q, :end] + alpha * ends_ref[q, :end]
        disp_out[q, inner] = disp_ref[q, inner] + alpha * inner_ref[q, :, :width]
        disp_out[q, slab - end :] = disp_ref[q, slab - end :] + alpha * ends_ref[q, end:]
        image = jnp.concatenate([ends_image_ref[q, :reach], inner_image_ref[q], ends_image_ref[q, reach:]], axis=0)
        residual_out[q, :end] = ends_residual_ref[q, :end] - alpha * image[:end]
        residual_out[q, inner] = inner_residual_ref[q] - alpha * image[inner]
        residual_out[q, slab - end :] = ends_residual_ref[q, end:] - alpha * image[slab - end :]


VMEM = pl.BlockSpec(memory_space=pltpu.VMEM)
SMEM = pl.BlockSpec(memory_space=pltpu.SMEM)
HBM = pl.BlockSpec(memory_space=pltpu.HBM)
FULL = 62


def call(kernel, name, out_shapes, in_specs, flops, moved, scratch=(), grant=32, out_specs=None):
    return pl.pallas_call(
        kernel,
        out_shape=[jax.ShapeDtypeStruct(s, F32) for s in out_shapes],
        in_specs=in_specs,
        out_specs=out_specs or [VMEM] * len(out_shapes),
        scratch_shapes=list(scratch),
        compiler_params=pltpu.CompilerParams(vmem_limit_bytes=grant * 1024 * 1024),
        cost_estimate=pl.CostEstimate(flops=flops, bytes_accessed=moved, transcendentals=0),
        name=name,
    )


def transform_call(blocks, tables, hole, edge, main, edge_at, hole_at, comps, width, slab, weight):
    around = SECTORS * width
    at_end = edge is not None
    total = comps * main
    out_rows = total + (TILE if at_end else 0)
    rows = total + (2 * TILE if at_end else 0)
    operands = list(blocks) + list(tables) + [hole] + ([edge] if at_end else [])
    shapes = [(out_rows, width + LANES), (comps, main, width), (out_rows, width + LANES)]
    return call(
        functools.partial(transform_kernel, comps, main, at_end, edge_at, hole_at), "transform",
        ([] if at_end else [(slab, LANES)]) + shapes, [VMEM] * len(operands),
        weight * 2 * total * 3 * around * 3 * width, weight * 4 * total * width * 8,
        [pltpu.VMEM((rows, 8 * width), BF16), pltpu.VMEM((rows // TILE, TILE, around), F32),
         pltpu.VMEM((rows, 2 * around), BF16), pltpu.VMEM((total, LANES), F32)],
    )(*operands)


def after_all(x, *others):
    return lax.optimization_barrier((x, *others))[0]


def shards(load, disp, stiff, hole, section_class, class_table, precond):
    slab, comps, width = disp.shape
    ax, sec = lax.axis_size("ax"), lax.axis_size("sec")
    around = width * sec
    cell_total = slab * ax * comps * around
    end = slab // 16 * 2
    inner = slab // 2 - end
    load, disp, stiff = [x.transpose(1, 0, 2) for x in (load, disp, stiff)]
    forward, even, odd, beyond = harmonic_tables(width)
    block = 4 * comps * slab * width
    classes = section_class.reshape(1, slab)

    sent = (comps * inner + TILE, width)
    ends_shape = (2, comps * end + 2 * TILE, width)
    shapes = [sent, ends_shape, (slab, LANES), (2 * TILE, width), (2 * TILE, width)]
    small = [pltpu.SMEM(class_table.shape, F32), pltpu.VMEM((1, slab), jnp.int32)]
    arguments = (class_table, classes, load, disp, stiff, hole)
    reach = slab // 2 + TILE
    (keep,) = call(
        functools.partial(first_kernel, end, comps, ax), "first",
        [sent], [HBM] * 6, 10 * comps * inner * width, block,
        small + [pltpu.VMEM((comps, rows, width), F32) for rows in (inner, reach, inner)]
        + [pltpu.VMEM((reach, width), jnp.int32), pltpu.VMEM(sent, F32), pltpu.VMEM((slab, LANES), F32)]
        + [pltpu.SemaphoreType.DMA((3 + 3 * comps // 2,)), pltpu.SemaphoreType.DMA((1 + comps,))],
        FULL, [HBM],
    )(*arguments)
    other, edge, factor, near, other_side = call(
        functools.partial(second_kernel, end, comps, ax), "second",
        shapes, [HBM] * 6, 10 * comps * slab * width, 2 * block,
        small + [pltpu.VMEM((comps, slab, width), F32)] * 3 + [pltpu.VMEM((slab, width), jnp.int32)]
        + [pltpu.VMEM((2,) + sent, F32)] + [pltpu.VMEM(shape, F32) for shape in shapes[1:3] + [(2, 2 * TILE, width)]]
        + [pltpu.SemaphoreType.DMA((3 + 3 * comps // 2,)), pltpu.SemaphoreType.DMA((6 + comps,))],
        FULL, [HBM] * len(shapes),
    )(*arguments)

    def to(x, mask):
        return lax.ppermute(x, "sec", [(i, i ^ mask) for i in range(sec)])

    def gather(keep, other):
        return keep, to(other, 1), to(keep, 2), to(other, 3)

    blocks = gather(keep, other)
    near = lax.ppermute(near, "ax", [(i, i ^ 1) for i in range(ax)])
    other_side = lax.ppermute(other_side, "ax", [(i, ((i + 1) ^ 1) - 1) for i in range(1, ax - 1)])
    weight, beyond_weight = call(
        fold_kernel, "fold", [(comps * comps, TILE, 5 * width // 2), (comps, TILE, 5 * width // 2)], [VMEM] * 5,
        1, 1,
    )(precond, forward, even, odd, beyond)
    rows = (comps * end + TILE, width)
    keep_ends, other_ends = call(
        functools.partial(ends_kernel, comps), "ends",
        [rows, rows], [VMEM] * 3, 2 * comps * end * width, 16 * comps * end * width, [pltpu.VMEM((2,) + rows, F32)],
    )(after_all(edge, weight), near, other_side)
    end_blocks = gather(keep_ends, other_ends)
    tables = (forward, even, odd, beyond, weight, beyond_weight)

    across = after_all(blocks[2], keep_ends, weight)
    edge, own, residual, back = transform_call(
        (keep, blocks[1], across, blocks[3]), tables, hole, None, inner, 0, (end, inner), comps, width, slab, 0
    )
    back = to(back, 1)
    across = after_all(end_blocks[2], own)
    own_ends, residual_ends, back_ends = transform_call(
        (keep_ends, end_blocks[1], across, end_blocks[3]), tables, hole, edge, end, inner, (0, slab - end),
        comps, width, slab, 100,
    )
    back_ends = to(back_ends, 1)
    prec, residual, image, partial = call(
        functools.partial(early_kernel, end, comps), "early",
        [(comps, 2 * inner, width + LANES), (comps, 2 * inner, width), (comps, 2 * (inner - TILE), width), (5 * TILE, width)],
        [VMEM] * 7, 30 * comps * slab * width, 4 * block,
    )(stiff, hole, after_all(factor, own_ends), own, back, residual, other)
    prec_ends, residual_ends, image_ends, sums = call(
        functools.partial(late_kernel, end, comps), "late",
        [(comps, 2 * end, width), (comps, 2 * end, width), (comps, 2 * (end + TILE), width), (ax * sec, LANES)],
        [VMEM] * 10, 8 * comps * slab * width, block,
    )(stiff, hole, factor, prec, residual, own_ends, back_ends, residual_ends, other_ends, partial)
    gathered = lax.all_to_all(sums, ("ax", "sec"), 0, 0, tiled=True)
    disp_new, residual_new, stats = call(
        functools.partial(update_kernel, end, comps, cell_total), "update",
        [(comps, slab, width), (comps, slab, width), (1, 3)], [VMEM] * 8,
        4 * comps * slab * width, 6 * block,
    )(disp, gathered, prec, residual, image, prec_ends, residual_ends, image_ends)
    return disp_new.transpose(1, 0, 2), residual_new.transpose(1, 0, 2), stats.reshape(3)


def solution(mesh):
    in_specs = (
        P("ax", None, "sec"),
        P("ax", None, "sec"),
        P("ax", None, "sec"),
        P("ax", "sec"),
        P("ax"),
        P(),
        P(),
    )
    out_specs = (P("ax", None, "sec"), P("ax", None, "sec"), P())
    return jax.shard_map(shards, mesh=mesh, in_specs=in_specs, out_specs=out_specs, check_vma=False)
```
